128 devices in a mesh: pre: 8 (over x, core), tp: 16 (over z, y).
Axes of the slice: x: 4, y: 4, z: 4, core: 2. Of those that a mesh axis runs over, the one named last changes fastest.
Arguments:
- latent_rows: float32 [131072, 576], P(('pre', 'tp'))
- index_keys: float32 [131072, 128], P(('pre', 'tp'))
- queries: bfloat16 [2, 32, 128, 576], P(None, 'pre', 'tp')
- index_queries: bfloat16 [2, 32, 64, 128], P(None, 'pre')
- index_gates: bfloat16 [2, 32, 64], P(None, 'pre'), may hold values from 0.14941406 to 1.5
- value_proj: bfloat16 [128, 512, 128], P('tp'), may hold values from -2 to 2
- out_proj: bfloat16 [16384, 7168], P('tp'), may hold values from -0.046875 to 0.046875
- block_rows: int32 [2, 32, 64, 64], P(None, 'pre'), may hold values from 0 to 8191, as said below
- block_owner: int32 [2, 32, 64], P(None, 'pre'), may hold values from 0 to 15, as said below
- block_count: int32 [2, 32, 64], P(None, 'pre'), may hold values from 0 to 64, as said below
Outputs:
- attended: bfloat16 [2, 32, 7168], P(None, 'pre')
- index_total: float32 [2, 32], P(None, 'pre')
The draws below stay inside these ranges and needn't reach their ends.
Inputs may be any that keep to these rules, and one draw needn't show every extreme that they name: `block_owner`: for each step and query every owner is named by exactly 4 blocks. `block_count`: the counts of one step and query sum to 2048; the blocks of one owner hold at most 256 valid rows, and in every step and query some owner holds exactly that many. `block_rows`: rows index the owner's 8192 cache rows; the first block_count entries of a block are valid; the valid rows of one owner in one step and query are distinct.
All inputs are finite; a program needn't handle non-finite values.
Results may differ from the reference program's by a relative error of at most 0.012.
The reference program's roundings to bfloat16 on the way count: a program that leaves them out, or rounds other values in their place, can miss the bound.
Values may be sent and summed in bfloat16 or wider, within the bound.
No kernel may reach another device: no remote copies, remote signals or barrier semaphores. Data moves between devices by JAX's collectives and lax.ppermute only.
A program may use at most 128 MiB of HBM per device.

```python
import math
import jax
import jax.numpy as jnp
from jax import lax

H = 128
HI = 64
IDX = 128
LAT = 512
VDIM = 128
D = 7168
TOPK = 2048
ROWS_DEV = 1024
STEPS = 2
BLOCK = 64
KV = 576
SEQ = 131072
SHARD = 8192
QUERIES = 32
OWNERS = 16
OWN_BLOCKS = 4
NBLK = 64
N_TP = 16


def block_table(key):
    key = jax.random.fold_in(key, 11)
    pair_count = STEPS * QUERIES
    quarter = N_TP // 4
    half_quarter = quarter // 2
    mean_rows = TOPK // N_TP
    owner_most = OWN_BLOCKS * BLOCK
    order_keys = jax.random.split(jax.random.fold_in(key, 1), pair_count)
    rank_owner = jax.vmap(lambda subkey: jax.random.permutation(subkey, N_TP))(order_keys).astype(jnp.int32)
    upper_shift = jax.random.randint(jax.random.fold_in(key, 2), (pair_count, N_TP), 0, mean_rows)
    lower_shift = jax.random.randint(jax.random.fold_in(key, 3), (pair_count, N_TP), 0, mean_rows // 2 + 1)
    rank_index = jnp.arange(N_TP, dtype=jnp.int32)
    second_pos = rank_index - quarter
    upper_partner = jnp.where(second_pos < half_quarter, rank_index, rank_index - half_quarter)
    upper_sign = jnp.where(second_pos < half_quarter, 1, -1)
    lower_partner = jnp.where(rank_index < 3 * quarter, rank_index, rank_index - quarter)
    lower_sign = jnp.where(rank_index < 3 * quarter, 1, -1)
    upper_value = jnp.take(upper_shift, upper_partner, axis=1)
    lower_value = jnp.take(lower_shift, lower_partner, axis=1)
    rank_rows = jnp.where(rank_index < quarter, 2 * mean_rows, jnp.where(rank_index < 2 * quarter, mean_rows + upper_sign * upper_value, mean_rows // 2 + lower_sign * lower_value))
    owner_match = rank_owner[:, :, None] == rank_index[None, None, :]
    owner_rows = jnp.sum(jnp.where(owner_match, rank_rows[:, :, None], 0), axis=1)
    row_keys = jax.random.split(jax.random.fold_in(key, 4), pair_count * N_TP)
    local_rows = jax.vmap(lambda subkey: jax.random.permutation(subkey, SHARD)[:owner_most])(row_keys)
    local_rows = local_rows.reshape(pair_count, N_TP, OWN_BLOCKS, BLOCK).astype(jnp.int32)
    block_index = jnp.arange(OWN_BLOCKS, dtype=jnp.int32)
    counts = jnp.clip(owner_rows[:, :, None] - block_index[None, None, :] * BLOCK, 0, BLOCK)
    owners = jnp.broadcast_to(rank_index[None, :, None], (pair_count, N_TP, OWN_BLOCKS))
    leading_owner = rank_owner[:, 0]
    leading_local = jnp.take_along_axis(local_rows[:, :, 0, :2], leading_owner[:, None, None], axis=1)[:, 0, :]
    leading = (leading_local // ROWS_DEV * N_TP + leading_owner[:, None]) * ROWS_DEV + leading_local % ROWS_DEV
    shuffle_keys = jax.random.split(jax.random.fold_in(key, 5), pair_count)
    shuffle = jax.vmap(lambda subkey: jax.random.permutation(subkey, NBLK))(shuffle_keys)
    rows_out = jnp.take_along_axis(local_rows.reshape(pair_count, NBLK, BLOCK), shuffle[:, :, None], axis=1)
    owners_out = jnp.take_along_axis(owners.reshape(pair_count, NBLK), shuffle, axis=1)
    counts_out = jnp.take_along_axis(counts.reshape(pair_count, NBLK), shuffle, axis=1)
    return (rows_out.reshape(STEPS, QUERIES, NBLK, BLOCK).astype(jnp.int32), owners_out.reshape(STEPS, QUERIES, NBLK).astype(jnp.int32), counts_out.reshape(STEPS, QUERIES, NBLK).astype(jnp.int32), leading.astype(jnp.int32))


def mixed_values(key, salt, width):
    key = jax.random.fold_in(key, salt)
    normal_part = jax.random.normal(jax.random.fold_in(key, 1), (SEQ, width), jnp.float32)
    return normal_part


def owner_keys(key):
    values = mixed_values(key, 41, IDX)
    position = jnp.arange(SEQ, dtype=jnp.int32)
    owner = (position // ROWS_DEV % N_TP).astype(jnp.float32)
    rise = 1.0 + 2.0 / (0.234 * HI) * owner / (N_TP - 1)
    return values * rise[:, None]


def draw_latent_rows(key, part):
    return mixed_values(key, 31, KV)


def draw_index_keys(key, part):
    return owner_keys(key)


def draw_queries(key, part):
    key = jax.random.fold_in(key, 51)
    pair_count = STEPS * QUERIES
    drawn = jax.random.normal(key, (pair_count, H, KV), jnp.float32)
    return drawn.reshape(STEPS, QUERIES, H, KV).astype(jnp.bfloat16)


def draw_index_queries(key, part):
    key = jax.random.fold_in(key, 61)
    pair_count = STEPS * QUERIES
    drawn = jax.random.normal(key, (pair_count, HI, IDX), jnp.float32)
    return drawn.reshape(STEPS, QUERIES, HI, IDX).astype(jnp.bfloat16)


def draw_block_rows(key, part):
    block_info = block_table(key)
    return block_info[0]


def draw_block_owner(key, part):
    block_info = block_table(key)
    return block_info[1]


def draw_block_count(key, part):
    block_info = block_table(key)
    return block_info[2]


def levels(own_key, shape, shards, smallest, high):
    level = 1.0
    for dim, blocks in shards:
        steps = jax.random.uniform(jax.random.fold_in(jax.random.fold_in(own_key, 6), dim), (blocks,), jnp.float32, smallest / len(shards), high / len(shards))
        level = level * jnp.repeat(jnp.exp(steps), shape[dim] // blocks).reshape((-1,) + (1,) * (len(shape) - 1 - dim))
    return level


def gaussian(stream_key, dims, deviation, limit, cuts=(), kind=jnp.bfloat16):
    loudness = levels(stream_key, dims, cuts, -0.22, 0.18) if cuts else 1.0
    values = jax.random.normal(stream_key, dims, jnp.float32) * deviation * loudness
    return jnp.minimum(jnp.maximum(values, -limit), limit).astype(kind)


def setup_inputs(seed: int = 0) -> dict:
    streams_of = jax.random.split(jax.random.key(seed), 11)
    latent_rows = draw_latent_rows(jax.random.fold_in(streams_of[10], 71), 0)
    index_keys = draw_index_keys(jax.random.fold_in(streams_of[10], 71), 0)
    queries = draw_queries(jax.random.fold_in(streams_of[10], 71), 0)
    index_queries = draw_index_queries(jax.random.fold_in(streams_of[10], 71), 0)
    index_gates = jnp.clip(jnp.exp(math.log(1.5) - 2.306499 * jax.random.uniform(streams_of[4], (STEPS, QUERIES, HI), jnp.float32) ** levels(streams_of[4], (STEPS, QUERIES, HI), ((1, 8),), -0.2, 0.2)), 0.14941406, 1.5).astype(jnp.bfloat16)
    value_proj = gaussian(streams_of[5], (H, LAT, VDIM), (max(LAT // 64, 1)) ** -0.5, 2.0, ((0, 16),))
    out_proj = gaussian(streams_of[6], (H * VDIM, D), (H * VDIM) ** -0.5, 0.046875, ((0, 16),))
    block_rows = draw_block_rows(jax.random.fold_in(streams_of[10], 71), 0)
    block_owner = draw_block_owner(jax.random.fold_in(streams_of[10], 71), 0)
    block_count = draw_block_count(jax.random.fold_in(streams_of[10], 71), 0)
    return dict(latent_rows=latent_rows, index_keys=index_keys, queries=queries, index_queries=index_queries, index_gates=index_gates, value_proj=value_proj, out_proj=out_proj, block_rows=block_rows, block_owner=block_owner, block_count=block_count)


NEGATIVE = -1.0e30
SOFT_SCALE = 192.0 ** -0.5


def reference(latent_rows, index_keys, queries, index_queries, index_gates, value_proj, out_proj, block_rows, block_owner, block_count):
    cache_rows = latent_rows.astype(jnp.bfloat16)
    key_cache = lax.optimization_barrier(index_keys.astype(jnp.bfloat16)).astype(jnp.float32)
    pair_count = STEPS * QUERIES
    flat_queries = index_queries.astype(jnp.float32).reshape(pair_count, HI, IDX)
    flat_gates = index_gates.astype(jnp.float32).reshape(pair_count, HI)

    def index_one(inputs):
        query_rows, gate_rows = inputs
        logits = jnp.dot(key_cache, query_rows.T, precision=lax.Precision.HIGHEST)
        scores = jnp.sum(jnp.maximum(logits, 0.0) * gate_rows[None, :], axis=1) * IDX ** -0.5
        largest = jnp.max(scores)
        return largest + jnp.log(jnp.sum(jnp.exp(scores - largest)))

    index_total = lax.map(index_one, (flat_queries, flat_gates)).reshape(STEPS, QUERIES)
    value_full = value_proj.astype(jnp.float32)

    def attend_one(inputs):
        query_heads, local_rows, owners, counts = inputs
        positions = ((local_rows // ROWS_DEV) * OWNERS + owners[:, None]) * ROWS_DEV + local_rows % ROWS_DEV
        gathered = cache_rows[positions.reshape(-1).astype(jnp.int32)]
        present = (jnp.arange(BLOCK, dtype=jnp.int32)[None, :] < counts[:, None]).reshape(-1)
        scores = jnp.dot(query_heads, gathered.T, preferred_element_type=jnp.float32) * SOFT_SCALE
        scores = jnp.where(present[None, :], scores, NEGATIVE)
        largest = jnp.max(scores, axis=1)
        weights = jnp.where(present[None, :], jnp.exp(scores - largest[:, None]), 0.0)
        totals = jnp.sum(weights, axis=1)
        weighted = jnp.dot(weights, gathered[:, :LAT].astype(jnp.float32), precision=lax.Precision.HIGHEST)
        attn_rows = (weighted / totals[:, None]).astype(jnp.bfloat16)
        head_values = jnp.einsum("hl,hlv->hv", attn_rows.astype(jnp.float32), value_full, precision=lax.Precision.HIGHEST).astype(jnp.bfloat16)
        projected = jnp.dot(head_values.reshape(1, H * VDIM), out_proj, preferred_element_type=jnp.float32)
        return projected[0].astype(jnp.bfloat16)

    attended = lax.map(attend_one, (queries.reshape(pair_count, H, KV), block_rows.reshape(pair_count, NBLK, BLOCK), block_owner.reshape(pair_count, NBLK), block_count.reshape(pair_count, NBLK)))
    return attended.reshape(STEPS, QUERIES, D), index_total
```

```python
import jax
import jax.numpy as jnp
from jax import lax
from jax.experimental import pallas as pl
from jax.experimental.pallas import tpu as pltpu
from jax.sharding import PartitionSpec as P

IDX = 128
LAT = 512
KV = 576
BLOCK = 64
PRE = 8
TP = 16
PAIRS = 8
HEADS = 8
ROWS = 1024
HALF = 512
PACK = 256
STAT = 128
QROWS = TP * PAIRS * HEADS
LOWEST = -3.0e38
SOFT_SCALE = 192.0 ** (-0.5)
LOG2E = 1.4426950408889634
SCORE_SCALE = SOFT_SCALE * LOG2E

NT = (((1,), (1,)), ((), ()))


def vmem():
    return pl.BlockSpec(memory_space=pltpu.VMEM)


def smem():
    return pl.BlockSpec(memory_space=pltpu.SMEM)


def table_kernel(rows_ref, mask_ref, pos_ref, count_ref):
    entries = rows_ref.shape[1]
    high_iota = lax.broadcasted_iota(jnp.int32, (PRE * 8, entries), 0)
    low_iota = lax.broadcasted_iota(jnp.int32, (128, entries), 0)
    for pair in range(PAIRS):
        rows = rows_ref[pair : pair + 1, :]
        high = jnp.where(high_iota == (rows >> 7), 1.0, 0.0).astype(jnp.bfloat16)
        low = jnp.where(low_iota == (rows & 127), 1.0, 0.0).astype(jnp.bfloat16)
        chosen = lax.dot_general(high, low, NT, preferred_element_type=jnp.float32)
        for block in range(PRE):
            for part in range(8):
                mask_ref[block, pair : pair + 1, part * 128 : (part + 1) * 128] = chosen[
                    block * 8 + part : block * 8 + part + 1, :
                ]
    union = jnp.concatenate([jnp.max(mask_ref[block], axis=0, keepdims=True) for block in range(PRE)], axis=0)
    before = (
        lax.broadcasted_iota(jnp.int32, (128, 128), 0) < lax.broadcasted_iota(jnp.int32, (128, 128), 1)
    ).astype(jnp.float32).astype(jnp.bfloat16)
    carry = jnp.zeros((PRE, 1), jnp.float32)
    for part in range(8):
        piece = union[:, part * 128 : (part + 1) * 128]
        ahead = jnp.dot(piece.astype(jnp.bfloat16), before, preferred_element_type=jnp.float32) + carry
        pos_ref[:, part * 128 : (part + 1) * 128] = jnp.where(piece > 0.0, ahead, -1.0)
        carry = carry + jnp.sum(piece, axis=1, keepdims=True)
    count_ref[...] = jnp.broadcast_to(carry, (PRE, 128)).astype(jnp.int32)


def make_tables(effective_rows):
    return pl.pallas_call(
        table_kernel,
        out_shape=(
            jax.ShapeDtypeStruct((PRE, PAIRS, ROWS), jnp.float32),
            jax.ShapeDtypeStruct((PRE, ROWS), jnp.float32),
            jax.ShapeDtypeStruct((PRE, 128), jnp.int32),
        ),
        in_specs=[vmem()],
        out_specs=(vmem(), vmem(), vmem()),
        compiler_params=pltpu.CompilerParams(vmem_limit_bytes=32 << 20),
        cost_estimate=pl.CostEstimate(flops=2 * 8 * 64 * 4096 * 128, bytes_accessed=1 << 19, transcendentals=0),
        name="row_tables",
    )(effective_rows)


def attend_kernel(blocks, first, last, count_ref, query_ref, mask_ref, pos_ref, *refs):
    halves = refs[: 2 * blocks]
    refs = refs[2 * blocks :]
    if not first:
        high_in, total_in, acc_in = refs[:3]
        refs = refs[3:]
    if last:
        (out_ref, high_ref, total_ref, acc_ref) = refs
    else:
        high_ref, total_ref, acc_ref = refs
    if first:
        high_ref[...] = jnp.full((QROWS, STAT), LOWEST, jnp.float32)
        total_ref[...] = jnp.zeros((QROWS, STAT), jnp.float32)
        acc_ref[...] = jnp.zeros((QROWS, LAT), jnp.float32)
    else:
        high_ref[...] = high_in[...]
        total_ref[...] = total_in[...]
        acc_ref[...] = acc_in[...]
    for block in range(blocks):
        left, right = halves[2 * block], halves[2 * block + 1]

        def one_pack(pack, carry, block=block, left=left, right=right):
            slot = (lax.broadcasted_iota(jnp.int32, (PACK, ROWS), 0) + pack * PACK).astype(jnp.float32)
            pick = jnp.where(slot == pos_ref[block], 1.0, 0.0).astype(jnp.bfloat16)
            packed = lax.dot_general(left[...], pick[:, :HALF], NT, preferred_element_type=jnp.float32)
            packed = packed + lax.dot_general(right[...], pick[:, HALF:], NT, preferred_element_type=jnp.float32)
            packed = packed.astype(jnp.bfloat16)
            present = lax.dot_general(
                mask_ref[block].astype(jnp.bfloat16), pick, NT, preferred_element_type=jnp.float32
            )
            absent = jnp.where(present > 0.5, 0.0, -jnp.inf)
            scores = jnp.dot(query_ref[...], packed, preferred_element_type=jnp.float32)
            scores = scores.reshape(TP, PAIRS, HEADS, PACK) * SCORE_SCALE + absent[None, :, None, :]
            scores = scores.reshape(QROWS, PACK)
            former = high_ref[:, :1]
            newer = jnp.maximum(former, jnp.max(scores, axis=1, keepdims=True))
            weights = jnp.exp2(scores - newer)
            decay = jnp.exp2(former - newer)
            total = total_ref[:, :1] * decay + jnp.sum(weights, axis=1, keepdims=True)
            added = lax.dot_general(
                weights.astype(jnp.bfloat16), packed[:LAT, :], NT, preferred_element_type=jnp.float32
            )
            acc_ref[...] = acc_ref[...] * decay + added
            high_ref[...] = jnp.broadcast_to(newer, (QROWS, STAT))
            total_ref[...] = jnp.broadcast_to(total, (QROWS, STAT))
            return carry

        lax.fori_loop(0, (count_ref[block] + (PACK - 1)) // PACK, one_pack, 0)
    if last:
        out_ref[:, :LAT] = acc_ref[...].astype(jnp.bfloat16)
        lane = lax.broadcasted_iota(jnp.int32, (QROWS, STAT), 1)
        stats = jnp.zeros((QROWS, STAT), jnp.float32)
        for start, value in ((0, high_ref[...]), (3, total_ref[...])):
            for step in range(3):
                piece = value.astype(jnp.bfloat16).astype(jnp.float32)
                stats = jnp.where(lane == start + step, piece, stats)
                value = value - piece
        out_ref[:, LAT:] = stats.astype(jnp.bfloat16)


def attend(counts, query_rows, masks, positions, halves, state=None, last=False):
    blocks = len(halves) // 2
    first = state is None
    state_shapes = (
        jax.ShapeDtypeStruct((QROWS, STAT), jnp.float32),
        jax.ShapeDtypeStruct((QROWS, STAT), jnp.float32),
        jax.ShapeDtypeStruct((QROWS, LAT), jnp.float32),
    )
    if last:
        out_shape = jax.ShapeDtypeStruct((QROWS, LAT + STAT), jnp.bfloat16)
        out_specs = vmem()
        scratch = [pltpu.VMEM(s.shape, s.dtype) for s in state_shapes]
    else:
        out_shape = state_shapes
        out_specs = (vmem(), vmem(), vmem())
        scratch = []
    args = [counts, query_rows, masks, positions] + list(halves) + ([] if first else list(state))

    def body(*refs):
        attend_kernel(blocks, first, last, *refs)

    return pl.pallas_call(
        body,
        out_shape=out_shape,
        in_specs=[smem()] + [vmem()] * (len(args) - 1),
        out_specs=out_specs,
        scratch_shapes=scratch,
        compiler_params=pltpu.CompilerParams(vmem_limit_bytes=40 << 20),
        cost_estimate=pl.CostEstimate(
            flops=blocks * 2 * PACK * ROWS * (KV + KV + LAT), bytes_accessed=8 << 20, transcendentals=blocks * QROWS * PACK
        ),
        name="attend_%d" % blocks,
    )(*args)


def project_kernel(recv_ref, value_ref, out_proj_ref, out_ref):
    row = lax.broadcasted_iota(jnp.int32, (STAT, 2 * STAT), 0)
    col = lax.broadcasted_iota(jnp.int32, (STAT, 2 * STAT), 1)
    spread = jnp.where((row // 3) == (col // STAT), 1.0, 0.0).astype(jnp.bfloat16)
    stats = [
        jnp.dot(recv_ref[owner, :, LAT:], spread, preferred_element_type=jnp.float32) for owner in range(TP)
    ]
    highest = stats[0][:, :STAT]
    for owner in range(1, TP):
        highest = jnp.maximum(highest, stats[owner][:, :STAT])
    total = jnp.zeros((PAIRS * HEADS, STAT), jnp.float32)
    acc = jnp.zeros((PAIRS * HEADS, LAT), jnp.float32)
    for owner in range(TP):
        weight = jnp.exp2(stats[owner][:, :STAT] - highest)
        total = total + weight * stats[owner][:, STAT:]
        wide = jnp.concatenate([weight] * (LAT // STAT), axis=1)
        acc = acc + wide * recv_ref[owner, :, :LAT].astype(jnp.float32)
    attn = (acc / jnp.concatenate([total] * (LAT // STAT), axis=1)).astype(jnp.bfloat16)
    head_of = lax.broadcasted_iota(jnp.int32, (PAIRS, HEADS, 128), 1)
    pieces = []
    for head in range(HEADS):
        product = jnp.dot(attn, value_ref[head], preferred_element_type=jnp.float32)
        product = jnp.where(head_of == head, product.reshape(PAIRS, HEADS, 128), 0.0)
        pieces.append(jnp.sum(product, axis=1))
    values = jnp.concatenate(pieces, axis=1).astype(jnp.bfloat16)
    out_ref[...] = jnp.dot(values, out_proj_ref[...], preferred_element_type=jnp.float32).astype(jnp.bfloat16)


def project(received, value_proj, out_proj):
    return pl.pallas_call(
        project_kernel,
        out_shape=jax.ShapeDtypeStruct((PAIRS, out_proj.shape[1]), jnp.bfloat16),
        in_specs=[vmem(), vmem(), vmem()],
        out_specs=vmem(),
        compiler_params=pltpu.CompilerParams(vmem_limit_bytes=32 << 20),
        cost_estimate=pl.CostEstimate(flops=2 * 8 * 1024 * 7168, bytes_accessed=18 << 20, transcendentals=0),
        name="project",
    )(received, value_proj, out_proj)


def x_shift(step):
    return [(x * 2 + c, ((x + step) % 4) * 2 + c) for x in range(4) for c in range(2)]


def y_shift(step):
    return [(z * 4 + y, z * 4 + (y + step) % 4) for z in range(4) for y in range(4)]


def z_shift(step):
    return [(z * 4 + y, ((z + step) % 4) * 4 + y) for z in range(4) for y in range(4)]


CORE_SWAP = [(i, i ^ 1) for i in range(PRE)]


def index_partial(query_rows, gate_rows, key_rows):
    logits = jnp.einsum("tgid,kd->tgik", query_rows, key_rows, preferred_element_type=jnp.float32)
    logits = logits.reshape(PAIRS, 2, PRE, 32, ROWS)
    gates = gate_rows.astype(jnp.float32).transpose(1, 2, 0, 3)
    scores = jnp.sum(jnp.maximum(logits, 0.0) * gates[..., None], axis=(1, 3)) * IDX ** (-0.5)
    largest = jnp.max(scores, axis=-1)
    return largest + jnp.log(jnp.sum(jnp.exp(scores - largest[..., None]), axis=-1))


def summed_over(value, shift):
    far = lax.ppermute(value, "tp", shift(2)).astype(jnp.float32)
    right = lax.ppermute(value, "tp", shift(1)).astype(jnp.float32)
    left = lax.ppermute(value, "tp", shift(3)).astype(jnp.float32)
    return ((value.astype(jnp.float32) + far) + (right + left)).astype(jnp.bfloat16)


def on_device(
    latent_rows,
    index_keys,
    queries,
    index_queries,
    index_gates,
    value_proj,
    out_proj,
    block_rows,
    block_owner,
    block_count,
):
    me_pre = lax.axis_index("pre")
    me_tp = lax.axis_index("tp")

    own_queries = queries.reshape(PAIRS * HEADS, KV)
    all_queries = lax.all_to_all(
        jnp.broadcast_to(own_queries[None], (TP, PAIRS * HEADS, KV)), "tp", 0, 0
    ).reshape(QROWS, KV)

    block = latent_rows.T.astype(jnp.bfloat16)
    low, high = block[:, :HALF], block[:, HALF:]
    fwd_low = lax.ppermute(low, "pre", x_shift(1))
    bwd_high = lax.ppermute(high, "pre", x_shift(3))
    fwd_high = lax.ppermute(high, "pre", x_shift(1))
    bwd_low = lax.ppermute(low, "pre", x_shift(3))
    far_low = lax.ppermute(fwd_low, "pre", x_shift(1))
    far_high = lax.ppermute(bwd_high, "pre", x_shift(3))
    near = [low, high]
    sides = [fwd_low, fwd_high, bwd_low, bwd_high]
    far = [far_low, far_high]

    def swapped(parts):
        return [lax.ppermute(part, "pre", CORE_SWAP) for part in parts]

    near = near + swapped(near)
    sides = sides + swapped(sides)
    far = far + swapped(far)

    valid = (jnp.arange(BLOCK, dtype=jnp.int32) < block_count[..., None]) & (block_owner == me_tp)[..., None]
    effective = jnp.where(valid, block_rows, -1).reshape(PAIRS, -1)
    masks, positions, counts = make_tables(effective)
    counts = counts[:, 0]
    my_x, my_core = me_pre // 2, me_pre % 2

    def picked(pre_ids):
        ids = jnp.stack(pre_ids)
        return counts[ids], masks[ids], positions[ids][:, None, :]

    def ident(shift, core):
        return ((my_x + shift) % 4) * 2 + core

    other = 1 - my_core
    sets = [
        ([ident(0, my_core), ident(0, other)], near),
        ([ident(3, my_core), ident(1, my_core), ident(3, other), ident(1, other)], sides),
        ([ident(2, my_core), ident(2, other)], far),
    ]
    state = None
    for number, (ids, halves) in enumerate(sets):
        count, mask, position = picked(ids)
        state = attend(count, all_queries, mask, position, halves, state, last=number == 2)
    received = lax.all_to_all(state.reshape(TP, PAIRS * HEADS, LAT + STAT), "tp", 0, 0)

    slice_rows = lax.dynamic_slice_in_dim(index_queries.reshape(PAIRS * 64, IDX), me_tp * 32, 32, 0)
    gate_rows = jnp.pad(index_gates.reshape(4, IDX), ((0, 12), (0, 0)))
    index_piece = jnp.concatenate([slice_rows, gate_rows], axis=0)
    groups = lax.all_to_all(jnp.broadcast_to(index_piece[None], (PRE, 48, IDX)), "pre", 0, 0)
    gates = groups[:, 32:36].reshape(PRE, PAIRS, 2, 32)
    index_slab, _ = lax.optimization_barrier((groups[:, :32], all_queries[0, 0]))
    slabs = lax.all_to_all(jnp.broadcast_to(index_slab[None], (TP, PRE, 32, IDX)), "tp", 0, 0)
    partial = index_partial(slabs, gates, index_keys.astype(jnp.bfloat16))
    partial = jnp.broadcast_to(partial.T[:, None, :], (PRE, TP, PAIRS)).reshape(PRE * TP, PAIRS)
    partials = lax.all_to_all(partial, ("pre", "tp"), 0, 0, tiled=True)
    top = jnp.max(partials, axis=0)
    index_total = top + jnp.log(jnp.sum(jnp.exp(partials - top), axis=0))

    part_out = project(received, value_proj, out_proj)
    attended = summed_over(summed_over(part_out, y_shift), z_shift)
    steps, queries_local = queries.shape[0], queries.shape[1]
    return (
        attended.reshape(steps, queries_local, out_proj.shape[1]),
        index_total.reshape(steps, queries_local),
    )


def solution(mesh):
    placed = (
        P(("pre", "tp"), None),
        P(("pre", "tp"), None),
        P(None, "pre", "tp", None),
        P(None, "pre", None, None),
        P(None, "pre", None),
        P("tp", None, None),
        P("tp", None),
        P(None, "pre", None, None),
        P(None, "pre", None),
        P(None, "pre", None),
    )
    return jax.shard_map(
        on_device,
        mesh=mesh,
        in_specs=placed,
        out_specs=(P(None, "pre", None), P(None, "pre")),
        check_vma=False,
    )
```

```python
import jax
import jax.numpy as jnp
from jax import lax
from jax.experimental import pallas as pl
from jax.experimental.pallas import tpu as pltpu
from jax.sharding import PartitionSpec as P

IDX = 128
LAT = 512
KV = 576
BLOCK = 64
PRE = 8
TP = 16
PAIRS = 8
HEADS = 8
ROWS = 1024
HALF = 512
PACK = 256
QTILE = 256
PIECES = 4
STAT = 128
QROWS = TP * PAIRS * HEADS
LOWEST = -3.0e38
SOFT_SCALE = 192.0 ** (-0.5)
LOG2E = 1.4426950408889634
SCORE_SCALE = SOFT_SCALE * LOG2E

NT = (((1,), (1,)), ((), ()))


def vmem():
    return pl.BlockSpec(memory_space=pltpu.VMEM)


def smem():
    return pl.BlockSpec(memory_space=pltpu.SMEM)


def table_kernel(rows_ref, mask_ref, pos_ref, count_ref):
    entries = rows_ref.shape[1]
    high_iota = lax.broadcasted_iota(jnp.int32, (PRE * 8, entries), 0)
    low_iota = lax.broadcasted_iota(jnp.int32, (128, entries), 0)
    for pair in range(PAIRS):
        rows = rows_ref[pair : pair + 1, :]
        high = jnp.where(high_iota == (rows >> 7), 1.0, 0.0).astype(jnp.bfloat16)
        low = jnp.where(low_iota == (rows & 127), 1.0, 0.0).astype(jnp.bfloat16)
        chosen = lax.dot_general(high, low, NT, preferred_element_type=jnp.float32)
        for block in range(PRE):
            for part in range(8):
                mask_ref[block, pair : pair + 1, part * 128 : (part + 1) * 128] = chosen[
                    block * 8 + part : block * 8 + part + 1, :
                ]
    union = jnp.concatenate([jnp.max(mask_ref[block], axis=0, keepdims=True) for block in range(PRE)], axis=0)
    before = (
        lax.broadcasted_iota(jnp.int32, (128, 128), 0) < lax.broadcasted_iota(jnp.int32, (128, 128), 1)
    ).astype(jnp.float32).astype(jnp.bfloat16)
    carry = jnp.zeros((PRE, 1), jnp.float32)
    for part in range(8):
        piece = union[:, part * 128 : (part + 1) * 128]
        ahead = jnp.dot(piece.astype(jnp.bfloat16), before, preferred_element_type=jnp.float32) + carry
        pos_ref[:, part * 128 : (part + 1) * 128] = jnp.where(piece > 0.0, ahead, -1.0)
        carry = carry + jnp.sum(piece, axis=1, keepdims=True)
    count_ref[...] = jnp.broadcast_to(carry, (PRE, 128)).astype(jnp.int32)


def make_tables(effective_rows):
    return pl.pallas_call(
        table_kernel,
        out_shape=(
            jax.ShapeDtypeStruct((PRE, PAIRS, ROWS), jnp.float32),
            jax.ShapeDtypeStruct((PRE, ROWS), jnp.float32),
            jax.ShapeDtypeStruct((PRE, 128), jnp.int32),
        ),
        in_specs=[vmem()],
        out_specs=(vmem(), vmem(), vmem()),
        compiler_params=pltpu.CompilerParams(vmem_limit_bytes=16 << 20),
        cost_estimate=pl.CostEstimate(flops=2 * 8 * 64 * 4096 * 128, bytes_accessed=1 << 19, transcendentals=0),
        name="row_tables",
    )(effective_rows)


def attend_kernel(base, blocks, first, last, count_ref, query_ref, mask_ref, pos_ref, *refs):
    halves, packed_ref = refs[: 2 * blocks], refs[-1]
    refs = refs[:-1]
    refs = refs[2 * blocks :]
    if not first:
        high_in, total_in, acc_in = refs[:3]
        refs = refs[3:]
    if last:
        (out_ref, high_ref, total_ref, acc_ref) = refs
    else:
        high_ref, total_ref, acc_ref = refs
    if first:
        high_ref[...] = jnp.full((QROWS, STAT), LOWEST, jnp.float32)
        total_ref[...] = jnp.zeros((QROWS, STAT), jnp.float32)
        acc_ref[...] = jnp.zeros((QROWS, LAT), jnp.float32)
    else:
        high_ref[...] = high_in[...]
        total_ref[...] = total_in[...]
        acc_ref[...] = acc_in[...]
    span = blocks * PACK
    rounds = count_ref[base, 0]
    for block in range(1, blocks):
        rounds = jnp.maximum(rounds, count_ref[base + block, 0])

    def one_round(number, carry):
        absent = []
        for block in range(blocks):
            left, right = halves[2 * block], halves[2 * block + 1]
            slot = (lax.broadcasted_iota(jnp.int32, (PACK, ROWS), 0) + number * PACK).astype(jnp.float32)
            pick = jnp.where(slot == pos_ref[base + block : base + block + 1, :], 1.0, 0.0).astype(jnp.bfloat16)
            packed = lax.dot_general(left[...], pick[:, :HALF], NT, preferred_element_type=jnp.float32)
            packed = packed + lax.dot_general(right[...], pick[:, HALF:], NT, preferred_element_type=jnp.float32)
            packed_ref[:, block * PACK : (block + 1) * PACK] = packed.astype(jnp.bfloat16)
            present = lax.dot_general(
                mask_ref[base + block].astype(jnp.bfloat16), pick, NT, preferred_element_type=jnp.float32
            )
            absent.append(jnp.where(present > 0.5, 0.0, -jnp.inf))
        absent = jnp.concatenate(absent, axis=1)
        for part in range(QROWS // QTILE):
            here = slice(part * QTILE, (part + 1) * QTILE)
            scores = jnp.dot(query_ref[here, :], packed_ref[...], preferred_element_type=jnp.float32)
            scores = scores.reshape(QTILE // 64, PAIRS, HEADS, span) * SCORE_SCALE + absent[None, :, None, :]
            scores = scores.reshape(QTILE, span)
            former = high_ref[here, :1]
            newer = jnp.maximum(former, jnp.max(scores, axis=1, keepdims=True))
            weights = jnp.exp2(scores - newer)
            decay = jnp.exp2(former - newer)
            total = total_ref[here, :1] * decay + jnp.sum(weights, axis=1, keepdims=True)
            added = lax.dot_general(
                weights.astype(jnp.bfloat16), packed_ref[:LAT, :], NT, preferred_element_type=jnp.float32
            )
            acc_ref[here, :] = acc_ref[here, :] * decay + added
            high_ref[here, :] = jnp.broadcast_to(newer, (QTILE, STAT))
            total_ref[here, :] = jnp.broadcast_to(total, (QTILE, STAT))
        return carry

    lax.fori_loop(0, (rounds + (PACK - 1)) // PACK, one_round, 0)
    if last:
        out_ref[:, :LAT] = acc_ref[...].astype(jnp.bfloat16)
        lane = lax.broadcasted_iota(jnp.int32, (QROWS, STAT), 1)
        stats = split_three(high_ref[...], lane, 0) + split_three(total_ref[...], lane, 3)
        out_ref[:, LAT:] = stats.astype(jnp.bfloat16)


def attend(base, counts, query_rows, masks, positions, halves, state=None, last=False):
    blocks = len(halves) // 2
    first = state is None
    state_shapes = (
        jax.ShapeDtypeStruct((QROWS, STAT), jnp.float32),
        jax.ShapeDtypeStruct((QROWS, STAT), jnp.float32),
        jax.ShapeDtypeStruct((QROWS, LAT), jnp.float32),
    )
    if last:
        out_shape = jax.ShapeDtypeStruct((QROWS, LAT + STAT), jnp.bfloat16)
        out_specs = vmem()
        scratch = [pltpu.VMEM(s.shape, s.dtype) for s in state_shapes]
    else:
        out_shape = state_shapes
        out_specs = (vmem(), vmem(), vmem())
        scratch = []
    scratch = scratch + [pltpu.VMEM((KV, blocks * PACK), jnp.bfloat16)]
    args = [counts, query_rows, masks, positions] + list(halves) + ([] if first else list(state))

    def body(*refs):
        attend_kernel(base, blocks, first, last, *refs)

    return pl.pallas_call(
        body,
        out_shape=out_shape,
        in_specs=[smem()] + [vmem()] * (len(args) - 1),
        out_specs=out_specs,
        scratch_shapes=scratch,
        compiler_params=pltpu.CompilerParams(vmem_limit_bytes=40 << 20),
        cost_estimate=pl.CostEstimate(
            flops=blocks * 2 * PACK * ROWS * (KV + KV + LAT), bytes_accessed=8 << 20, transcendentals=blocks * QROWS * PACK
        ),
        name="attend_%d" % blocks,
    )(*args)


def project_kernel(place_ref, recv_ref, value_ref, out_proj_ref, partial_ref, out_ref, weights, sems):
    depth = weights.shape[0] // PIECES
    copies = [
        pltpu.make_async_copy(
            out_proj_ref.at[pl.ds(piece * depth, depth)], weights.at[pl.ds(piece * depth, depth)], sems.at[piece]
        )
        for piece in range(PIECES)
    ]
    for copy in copies:
        copy.start()
    row = lax.broadcasted_iota(jnp.int32, (STAT, 2 * STAT), 0)
    col = lax.broadcasted_iota(jnp.int32, (STAT, 2 * STAT), 1)
    spread = jnp.where((row // 3) == (col // STAT), 1.0, 0.0).astype(jnp.bfloat16)
    stats = [
        jnp.dot(recv_ref[owner, :, LAT:], spread, preferred_element_type=jnp.float32) for owner in range(TP)
    ]
    highest = stats[0][:, :STAT]
    for owner in range(1, TP):
        highest = jnp.maximum(highest, stats[owner][:, :STAT])
    total = jnp.zeros((PAIRS * HEADS, STAT), jnp.float32)
    acc = jnp.zeros((PAIRS * HEADS, LAT), jnp.float32)
    for owner in range(TP):
        weight = jnp.exp2(stats[owner][:, :STAT] - highest)
        total = total + weight * stats[owner][:, STAT:]
        wide = jnp.concatenate([weight] * (LAT // STAT), axis=1)
        acc = acc + wide * recv_ref[owner, :, :LAT].astype(jnp.float32)
    attn = (acc / jnp.concatenate([total] * (LAT // STAT), axis=1)).astype(jnp.bfloat16)
    head_of = lax.broadcasted_iota(jnp.int32, (PAIRS, HEADS, 128), 1)
    pieces = []
    for head in range(HEADS):
        product = jnp.dot(attn, value_ref[head], preferred_element_type=jnp.float32)
        product = jnp.where(head_of == head, product.reshape(PAIRS, HEADS, 128), 0.0)
        pieces.append(jnp.sum(product, axis=1))
    values = jnp.concatenate(pieces, axis=1).astype(jnp.bfloat16)
    width = weights.shape[1]
    result = jnp.zeros((PAIRS, width), jnp.float32)
    for piece, copy in enumerate(copies):
        copy.wait()
        here = slice(piece * depth, (piece + 1) * depth)
        result = result + jnp.dot(values[:, here], weights[here, :], preferred_element_type=jnp.float32)
    out_ref[:, :width] = result.astype(jnp.bfloat16)
    lane = lax.broadcasted_iota(jnp.int32, (PAIRS, STAT), 1)
    group = place_ref[0] * 2 + place_ref[1]
    mine = jnp.sum(jnp.where(lane == group, partial_ref[...], 0.0), axis=1, keepdims=True)
    out_ref[:, width:] = split_three(mine, lane, 0).astype(jnp.bfloat16)


def project(place, received, value_proj, out_proj, partial):
    return pl.pallas_call(
        project_kernel,
        out_shape=jax.ShapeDtypeStruct((PAIRS, out_proj.shape[1] + STAT), jnp.bfloat16),
        in_specs=[smem(), vmem(), vmem(), pl.BlockSpec(memory_space=pltpu.HBM), vmem()],
        out_specs=vmem(),
        scratch_shapes=[pltpu.VMEM(out_proj.shape, out_proj.dtype), pltpu.SemaphoreType.DMA((PIECES,))],
        compiler_params=pltpu.CompilerParams(vmem_limit_bytes=60 << 20),
        cost_estimate=pl.CostEstimate(flops=2 * 8 * 1024 * 7168, bytes_accessed=18 << 20, transcendentals=0),
        name="project",
    )(place, received, value_proj, out_proj, partial)


def gather_kernel(own_ref, other_ref, unused_low, unused_high, out_ref):
    out_ref[0] = own_ref[...]
    out_ref[1] = other_ref[...]


def paired(own, other, far):
    return pl.pallas_call(
        gather_kernel,
        out_shape=jax.ShapeDtypeStruct((2,) + own.shape, own.dtype),
        in_specs=[vmem(), vmem()] + [pl.BlockSpec(memory_space=pl.ANY)] * 2,
        out_specs=vmem(),
        compiler_params=pltpu.CompilerParams(vmem_limit_bytes=4 << 20),
        cost_estimate=pl.CostEstimate(flops=1000, bytes_accessed=1 << 19, transcendentals=0),
        name="index_pair",
    )(own, other, *far)


def index_kernel(place_ref, here_ref, one_ref, two_ref, three_ref, key_ref, unused_ref, out_ref):
    keys = key_ref[...].astype(jnp.bfloat16)
    slabs = (here_ref, one_ref, two_ref, three_ref)
    gates = jnp.concatenate([ref[core, PAIRS * 64 :, :] for ref in slabs for core in range(2)], axis=0)
    gates = gates.astype(jnp.float32).T
    lane = lax.broadcasted_iota(jnp.int32, (PAIRS, 128), 1)
    result = jnp.zeros((PAIRS, 128), jnp.float32)
    for step, ref in enumerate(slabs):
        chip = (place_ref[0] + step) & 3
        for core in range(2):
            group = chip * 2 + (core ^ place_ref[1])
            scores = []
            for part in range(4):
                logits = lax.dot_general(
                    ref[core, part * 128 : (part + 1) * 128, :], keys, NT, preferred_element_type=jnp.float32
                )
                column = (step * 2 + core) * 16 + part
                gated = jnp.maximum(logits, 0.0) * gates[:, column : column + 1]
                scores.append(jnp.sum(gated.reshape(2, 64, ROWS), axis=1))
            scores = jnp.concatenate(scores, axis=0) * IDX ** (-0.5)
            largest = jnp.max(scores, axis=1, keepdims=True)
            summed = jnp.sum(jnp.exp(scores - largest), axis=1, keepdims=True)
            result = jnp.where(lane == group, largest + jnp.log(summed), result)
    out_ref[...] = result


def index_partial(place, slabs, index_keys, payload):
    return pl.pallas_call(
        index_kernel,
        out_shape=jax.ShapeDtypeStruct((PAIRS, 128), jnp.float32),
        in_specs=[smem()] + [vmem()] * 5 + [pl.BlockSpec(memory_space=pl.ANY)],
        out_specs=vmem(),
        compiler_params=pltpu.CompilerParams(vmem_limit_bytes=16 << 20),
        cost_estimate=pl.CostEstimate(flops=2 * 4096 * 1024 * 256, bytes_accessed=2 << 20, transcendentals=0),
        name="index_partial",
    )(place, *slabs, index_keys, payload)


def log_add(one, two):
    top = jnp.maximum(one, two)
    return top + jnp.log(jnp.exp(one - top) + jnp.exp(two - top))


def split_three(value, lane, start):
    pieces = jnp.zeros(lane.shape, jnp.float32)
    for step in range(3):
        piece = value.astype(jnp.bfloat16).astype(jnp.float32)
        pieces = jnp.where(lane == start + step, piece, pieces)
        value = value - piece
    return pieces


def join_three(pieces, start):
    wide = pieces.astype(jnp.float32)
    return wide[:, start : start + 1] + wide[:, start + 1 : start + 2] + wide[:, start + 2 : start + 3]


def four_sum(refs):
    width = refs[0].shape[1] - STAT
    parts = [ref[:, :width].astype(jnp.float32) for ref in refs]
    logs = [join_three(ref[:, width:], 0) for ref in refs]
    return (parts[0] + parts[1]) + (parts[2] + parts[3]), log_add(log_add(logs[0], logs[1]), log_add(logs[2], logs[3]))


def middle_kernel(own_ref, far_ref, right_ref, left_ref, out_ref):
    summed, logs = four_sum((own_ref, far_ref, right_ref, left_ref))
    width = summed.shape[1]
    out_ref[:, :width] = summed.astype(jnp.bfloat16)
    lane = lax.broadcasted_iota(jnp.int32, (PAIRS, STAT), 1)
    out_ref[:, width:] = split_three(logs, lane, 0).astype(jnp.bfloat16)


def final_kernel(own_ref, far_ref, right_ref, left_ref, out_ref, log_ref):
    summed, logs = four_sum((own_ref, far_ref, right_ref, left_ref))
    out_ref[...] = summed.astype(jnp.bfloat16)
    log_ref[...] = jnp.broadcast_to(logs, log_ref.shape)


def summed_over(value, shift, final):
    parts = (value,) + tuple(lax.ppermute(value, "tp", shift(step)) for step in (2, 1, 3))
    if final:
        out_shape = (
            jax.ShapeDtypeStruct((PAIRS, value.shape[1] - STAT), jnp.bfloat16),
            jax.ShapeDtypeStruct((PAIRS, STAT), jnp.float32),
        )
        out_specs = (vmem(), vmem())
    else:
        out_shape = jax.ShapeDtypeStruct(value.shape, jnp.bfloat16)
        out_specs = vmem()
    return pl.pallas_call(
        final_kernel if final else middle_kernel,
        out_shape=out_shape,
        in_specs=[vmem()] * 4,
        out_specs=out_specs,
        compiler_params=pltpu.CompilerParams(vmem_limit_bytes=4 << 20),
        cost_estimate=pl.CostEstimate(flops=1 << 18, bytes_accessed=1 << 19, transcendentals=0),
        name="sum_last" if final else "sum_first",
    )(*parts)


def x_shift(step):
    return [(x * 2 + c, ((x + step) % 4) * 2 + c) for x in range(4) for c in range(2)]


def y_shift(step):
    return [(z * 4 + y, z * 4 + (y + step) % 4) for z in range(4) for y in range(4)]


def z_shift(step):
    return [(z * 4 + y, ((z + step) % 4) * 4 + y) for z in range(4) for y in range(4)]


CORE_SWAP = [(i, i ^ 1) for i in range(PRE)]


def on_device(
    latent_rows,
    index_keys,
    queries,
    index_queries,
    index_gates,
    value_proj,
    out_proj,
    block_rows,
    block_owner,
    block_count,
):
    me_pre = lax.axis_index("pre")
    me_tp = lax.axis_index("tp")

    block = latent_rows.T.astype(jnp.bfloat16)
    low, high = block[:, :HALF], block[:, HALF:]
    fwd_low = lax.ppermute(low, "pre", x_shift(1))
    bwd_high = lax.ppermute(high, "pre", x_shift(3))
    fwd_high = lax.ppermute(high, "pre", x_shift(1))
    bwd_low = lax.ppermute(low, "pre", x_shift(3))

    def with_swapped(parts):
        return parts + [lax.ppermute(part, "pre", CORE_SWAP) for part in parts]

    own_queries = queries.reshape(PAIRS * HEADS, KV)
    all_queries = lax.all_to_all(
        jnp.broadcast_to(own_queries[None], (TP, PAIRS * HEADS, KV)), "tp", 0, 0
    ).reshape(QROWS, KV)

    fwd_low, bwd_high, all_queries = lax.optimization_barrier((fwd_low, bwd_high, all_queries))
    far_low = lax.ppermute(fwd_low, "pre", x_shift(1))
    far_high = lax.ppermute(bwd_high, "pre", x_shift(3))

    valid = (jnp.arange(BLOCK, dtype=jnp.int32) < block_count[..., None]) & (block_owner == me_tp)[..., None]
    source = block_rows >> 10
    relative = ((((source >> 1) - (me_pre >> 1) + 1) & 3) << 1) | ((source ^ me_pre) & 1)
    effective = jnp.where(valid, (relative << 10) | (block_rows & (ROWS - 1)), -1).reshape(PAIRS, -1)
    masks, positions, counts = make_tables(effective)

    near = with_swapped([fwd_low, fwd_high]) + with_swapped([low, high]) + with_swapped([bwd_low, bwd_high])
    state = attend(0, counts, all_queries, masks, positions, near)
    far_low, far_high, high, total, acc = lax.optimization_barrier((far_low, far_high) + tuple(state))
    state = (high, total, acc)
    far = with_swapped([far_low, far_high])
    payload = attend(6, counts, all_queries, masks, positions, far, state, last=True)
    received = lax.all_to_all(payload.reshape(TP, PAIRS * HEADS, LAT + STAT), "tp", 0, 0)

    gate_rows = jnp.pad(index_gates.reshape(4, IDX), ((0, 12), (0, 0)))
    piece = jnp.concatenate([index_queries.reshape(PAIRS * 64, IDX), gate_rows], axis=0)
    slab = paired(piece, lax.ppermute(piece, "pre", CORE_SWAP), far[:2])
    slabs = [slab] + [lax.ppermute(slab, "pre", x_shift(4 - step)) for step in (1, 2, 3)]
    place = jnp.stack([me_pre >> 1, me_pre & 1]).astype(jnp.int32)
    partial = index_partial(place, slabs, index_keys, payload)
    partial = log_add(partial, lax.ppermute(partial, "pre", CORE_SWAP))
    parts = [lax.ppermute(partial, "pre", x_shift(step)) for step in (2, 1, 3)]
    partial = log_add(log_add(partial, parts[0]), log_add(parts[1], parts[2]))
    part_out = project(place, received, value_proj, out_proj, partial)
    attended, index_total = summed_over(summed_over(part_out, y_shift, False), z_shift, True)
    index_total = index_total[:, 0]
    steps, queries_local = queries.shape[0], queries.shape[1]
    return (
        attended.reshape(steps, queries_local, out_proj.shape[1]),
        index_total.reshape(steps, queries_local),
    )


def solution(mesh):
    placed = (
        P(("pre", "tp"), None),
        P(("pre", "tp"), None),
        P(None, "pre", "tp", None),
        P(None, "pre", None, None),
        P(None, "pre", None),
        P("tp", None, None),
        P("tp", None),
        P(None, "pre", None, None),
        P(None, "pre", None),
        P(None, "pre", None),
    )
    return jax.shard_map(
        on_device,
        mesh=mesh,
        in_specs=placed,
        out_specs=(P(None, "pre", None), P(None, "pre")),
        check_vma=False,
    )
```

```python
import jax
import jax.numpy as jnp
from jax import lax
from jax.experimental import pallas as pl
from jax.experimental.pallas import tpu as pltpu
from jax.sharding import PartitionSpec as P

IDX = 128
LAT = 512
KV = 576
BLOCK = 64
PRE = 8
TP = 16
PAIRS = 8
HEADS = 8
ROWS = 1024
PACK = 256
QTILE = 256
PIECES = 4
STAT = 128
QROWS = TP * PAIRS * HEADS
LOWEST = -3.0e38
SOFT_SCALE = 192.0 ** (-0.5)
LOG2E = 1.4426950408889634
SCORE_SCALE = SOFT_SCALE * LOG2E

NT = (((1,), (1,)), ((), ()))


def vmem():
    return pl.BlockSpec(memory_space=pltpu.VMEM)


def smem():
    return pl.BlockSpec(memory_space=pltpu.SMEM)


def table_kernel(rows_ref, mask_ref, pos_ref, count_ref):
    entries = rows_ref.shape[1]
    high_iota = lax.broadcasted_iota(jnp.int32, (PRE * 8, entries), 0)
    low_iota = lax.broadcasted_iota(jnp.int32, (128, entries), 0)
    for pair in range(PAIRS):
        rows = rows_ref[pair : pair + 1, :]
        high = jnp.where(high_iota == (rows >> 7), 1.0, 0.0).astype(jnp.bfloat16)
        low = jnp.where(low_iota == (rows & 127), 1.0, 0.0).astype(jnp.bfloat16)
        chosen = lax.dot_general(high, low, NT, preferred_element_type=jnp.float32)
        for block in range(PRE):
            for part in range(8):
                mask_ref[block, pair : pair + 1, part * 128 : (part + 1) * 128] = chosen[
                    block * 8 + part : block * 8 + part + 1, :
                ]
    union = jnp.concatenate([jnp.max(mask_ref[block], axis=0, keepdims=True) for block in range(PRE)], axis=0)
    before = (
        lax.broadcasted_iota(jnp.int32, (128, 128), 0) < lax.broadcasted_iota(jnp.int32, (128, 128), 1)
    ).astype(jnp.float32).astype(jnp.bfloat16)
    carry = jnp.zeros((PRE, 1), jnp.float32)
    for part in range(8):
        piece = union[:, part * 128 : (part + 1) * 128]
        ahead = jnp.dot(piece.astype(jnp.bfloat16), before, preferred_element_type=jnp.float32) + carry
        pos_ref[:, part * 128 : (part + 1) * 128] = jnp.where(piece > 0.0, ahead, -1.0)
        carry = carry + jnp.sum(piece, axis=1, keepdims=True)
    count_ref[...] = jnp.broadcast_to(carry, (PRE, 128)).astype(jnp.int32)


def make_tables(effective_rows):
    return pl.pallas_call(
        table_kernel,
        out_shape=(
            jax.ShapeDtypeStruct((PRE, PAIRS, ROWS), jnp.float32),
            jax.ShapeDtypeStruct((PRE, ROWS), jnp.float32),
            jax.ShapeDtypeStruct((PRE, 128), jnp.int32),
        ),
        in_specs=[vmem()],
        out_specs=(vmem(), vmem(), vmem()),
        compiler_params=pltpu.CompilerParams(vmem_limit_bytes=16 << 20),
        cost_estimate=pl.CostEstimate(flops=2 * 8 * 64 * 4096 * 128, bytes_accessed=1 << 19, transcendentals=0),
        name="row_tables",
    )(effective_rows)


def attend_kernel(base, parts, first, last, count_ref, query_ref, mask_ref, pos_ref, *refs):
    blocks = len(parts)
    sources = []
    for number in parts:
        sources.append(refs[:number])
        refs = refs[number:]
    if not first:
        stat_in, acc_in = refs[:2]
        refs = refs[2:]
    if last:
        out_ref, stat_ref, acc_ref = refs[:3]
        refs = refs[3:]
    else:
        stat_ref, acc_ref = refs[:2]
        refs = refs[2:]
    (packed_ref,) = refs
    if first:
        column = lax.broadcasted_iota(jnp.int32, (QROWS, STAT), 1)
        stat_ref[...] = jnp.where(column < STAT // 2, LOWEST, 0.0)
        acc_ref[...] = jnp.zeros((QROWS, LAT), jnp.float32)
    else:
        stat_ref[...] = stat_in[...]
        acc_ref[...] = acc_in[...]
    span = blocks * PACK
    rounds = count_ref[base, 0]
    for block in range(1, blocks):
        rounds = jnp.maximum(rounds, count_ref[base + block, 0])

    def one_round(number):
        absent = []
        for block in range(blocks):
            slot = (lax.broadcasted_iota(jnp.int32, (PACK, ROWS), 0) + number * PACK).astype(jnp.float32)
            pick = jnp.where(slot == pos_ref[base + block : base + block + 1, :], 1.0, 0.0).astype(jnp.bfloat16)
            depth = KV // len(sources[block])
            for number_in, piece in enumerate(sources[block]):
                packed = lax.dot_general(piece[...], pick, NT, preferred_element_type=jnp.float32)
                packed_ref[number_in * depth : (number_in + 1) * depth, block * PACK : (block + 1) * PACK] = (
                    packed.astype(jnp.bfloat16)
                )
            present = lax.dot_general(
                mask_ref[base + block].astype(jnp.bfloat16), pick, NT, preferred_element_type=jnp.float32
            )
            absent.append(jnp.where(present > 0.5, 0.0, -jnp.inf))
        absent = jnp.concatenate(absent, axis=1)
        column = lax.broadcasted_iota(jnp.int32, (QTILE, STAT), 1)
        for part in range(QROWS // QTILE):
            here = slice(part * QTILE, (part + 1) * QTILE)
            scores = jnp.dot(query_ref[here, :], packed_ref[...], preferred_element_type=jnp.float32)
            scores = scores.reshape(QTILE // 64, PAIRS, HEADS, span) * SCORE_SCALE + absent[None, :, None, :]
            scores = scores.reshape(QTILE, span)
            former = stat_ref[here, :1]
            newer = jnp.maximum(former, jnp.max(scores, axis=1, keepdims=True))
            weights = jnp.exp2(scores - newer)
            decay = jnp.exp2(former - newer)
            total = stat_ref[here, STAT // 2 : STAT // 2 + 1] * decay + jnp.sum(weights, axis=1, keepdims=True)
            added = lax.dot_general(
                weights.astype(jnp.bfloat16), packed_ref[:LAT, :], NT, preferred_element_type=jnp.float32
            )
            acc_ref[here, :] = acc_ref[here, :] * decay + added
            stat_ref[here, :] = jnp.where(column < STAT // 2, newer, total)

    pl.loop(0, (rounds + (PACK - 1)) // PACK)(one_round)

    if last:
        column = lax.broadcasted_iota(jnp.int32, (QTILE, STAT), 1)
        for part in range(QROWS // QTILE):
            here = slice(part * QTILE, (part + 1) * QTILE)
            out_ref[here, :LAT] = acc_ref[here, :].astype(jnp.bfloat16)
            stats = split_three(stat_ref[here, :1], column, 0) + split_three(
                stat_ref[here, STAT // 2 : STAT // 2 + 1], column, 3
            )
            out_ref[here, LAT:] = stats.astype(jnp.bfloat16)


def attend(base, counts, query_rows, masks, positions, sources, state=None, last=False):
    parts = [len(pieces) for pieces in sources]
    blocks = len(parts)
    first = state is None
    state_shapes = (
        jax.ShapeDtypeStruct((QROWS, STAT), jnp.float32),
        jax.ShapeDtypeStruct((QROWS, LAT), jnp.float32),
    )
    if last:
        out_shape = jax.ShapeDtypeStruct((QROWS, LAT + STAT), jnp.bfloat16)
        out_specs = vmem()
        scratch = [pltpu.VMEM(s.shape, s.dtype) for s in state_shapes]
    else:
        out_shape = state_shapes
        out_specs = (vmem(), vmem())
        scratch = []
    scratch = scratch + [pltpu.VMEM((KV, blocks * PACK), jnp.bfloat16)]
    moved = sum([list(pieces) for pieces in sources], []) + ([] if first else list(state))

    def body(*refs):
        attend_kernel(base, parts, first, last, *refs)

    return pl.pallas_call(
        body,
        out_shape=out_shape,
        in_specs=[smem()] + [vmem()] * (3 + len(moved)),
        out_specs=out_specs,
        scratch_shapes=scratch,
        compiler_params=pltpu.CompilerParams(vmem_limit_bytes=24 << 20),
        cost_estimate=pl.CostEstimate(
            flops=blocks * 2 * PACK * ROWS * (KV + KV + LAT), bytes_accessed=8 << 20, transcendentals=blocks * QROWS * PACK
        ),
        name="attend_%d" % blocks,
    )(counts, query_rows, masks, positions, *moved)


def project_kernel(place_ref, recv_ref, value_ref, out_proj_ref, partial_ref, out_ref, weights, sems):
    depth = weights.shape[0] // PIECES
    copies = [
        pltpu.make_async_copy(
            out_proj_ref.at[pl.ds(piece * depth, depth)], weights.at[pl.ds(piece * depth, depth)], sems.at[piece]
        )
        for piece in range(PIECES)
    ]
    for copy in copies:
        copy.start()
    row = lax.broadcasted_iota(jnp.int32, (STAT, 2 * STAT), 0)
    col = lax.broadcasted_iota(jnp.int32, (STAT, 2 * STAT), 1)
    spread = jnp.where((row // 3) == (col // STAT), 1.0, 0.0).astype(jnp.bfloat16)
    stats = [
        jnp.dot(recv_ref[owner, :, LAT:], spread, preferred_element_type=jnp.float32) for owner in range(TP)
    ]
    highest = stats[0][:, :STAT]
    for owner in range(1, TP):
        highest = jnp.maximum(highest, stats[owner][:, :STAT])
    total = jnp.zeros((PAIRS * HEADS, STAT), jnp.float32)
    acc = jnp.zeros((PAIRS * HEADS, LAT), jnp.float32)
    for owner in range(TP):
        weight = jnp.exp2(stats[owner][:, :STAT] - highest)
        total = total + weight * stats[owner][:, STAT:]
        wide = jnp.concatenate([weight] * (LAT // STAT), axis=1)
        acc = acc + wide * recv_ref[owner, :, :LAT].astype(jnp.float32)
    attn = (acc / jnp.concatenate([total] * (LAT // STAT), axis=1)).astype(jnp.bfloat16)
    head_of = lax.broadcasted_iota(jnp.int32, (PAIRS, HEADS, 128), 1)
    pieces = []
    for head in range(HEADS):
        product = jnp.dot(attn, value_ref[head], preferred_element_type=jnp.float32)
        product = jnp.where(head_of == head, product.reshape(PAIRS, HEADS, 128), 0.0)
        pieces.append(jnp.sum(product, axis=1))
    values = jnp.concatenate(pieces, axis=1).astype(jnp.bfloat16)
    width = weights.shape[1]
    result = jnp.zeros((PAIRS, width), jnp.float32)
    for piece, copy in enumerate(copies):
        copy.wait()
        here = slice(piece * depth, (piece + 1) * depth)
        result = result + jnp.dot(values[:, here], weights[here, :], preferred_element_type=jnp.float32)
    out_ref[:, :width] = result.astype(jnp.bfloat16)
    lane = lax.broadcasted_iota(jnp.int32, (PAIRS, STAT), 1)
    group = place_ref[0] * 2 + place_ref[1]
    mine = jnp.sum(jnp.where(lane == group, partial_ref[...], 0.0), axis=1, keepdims=True)
    out_ref[:, width:] = split_three(mine, lane, 0).astype(jnp.bfloat16)


def project(place, received, value_proj, out_proj, partial):
    return pl.pallas_call(
        project_kernel,
        out_shape=jax.ShapeDtypeStruct((PAIRS, out_proj.shape[1] + STAT), jnp.bfloat16),
        in_specs=[smem(), vmem(), vmem(), pl.BlockSpec(memory_space=pl.ANY), vmem()],
        out_specs=vmem(),
        scratch_shapes=[pltpu.VMEM(out_proj.shape, out_proj.dtype), pltpu.SemaphoreType.DMA((PIECES,))],
        compiler_params=pltpu.CompilerParams(vmem_limit_bytes=24 << 20),
        cost_estimate=pl.CostEstimate(flops=2 * 8 * 1024 * 7168, bytes_accessed=18 << 20, transcendentals=0),
        name="project",
    )(place, received, value_proj, pltpu.with_memory_space_constraint(out_proj, pltpu.HBM), partial)


def gather_kernel(own_ref, other_ref, out_ref):
    out_ref[0] = own_ref[...]
    out_ref[1] = other_ref[...]


def paired(own, other):
    return pl.pallas_call(
        gather_kernel,
        out_shape=jax.ShapeDtypeStruct((2,) + own.shape, own.dtype),
        in_specs=[vmem(), vmem()],
        out_specs=vmem(),
        compiler_params=pltpu.CompilerParams(vmem_limit_bytes=4 << 20),
        cost_estimate=pl.CostEstimate(flops=1000, bytes_accessed=1 << 19, transcendentals=0),
        name="index_pair",
    )(own, other)


def index_kernel(place_ref, here_ref, one_ref, two_ref, three_ref, key_ref, unused_ref, out_ref):
    keys = key_ref[...].astype(jnp.bfloat16)
    slabs = (here_ref, one_ref, two_ref, three_ref)
    gates = jnp.concatenate([ref[core, PAIRS * 64 :, :] for ref in slabs for core in range(2)], axis=0)
    gates = gates.astype(jnp.float32).T
    lane = lax.broadcasted_iota(jnp.int32, (PAIRS, 128), 1)
    result = jnp.zeros((PAIRS, 128), jnp.float32)
    for step, ref in enumerate(slabs):
        chip = (place_ref[0] + step) & 3
        for core in range(2):
            group = chip * 2 + (core ^ place_ref[1])
            scores = []
            for part in range(4):
                logits = lax.dot_general(
                    ref[core, part * 128 : (part + 1) * 128, :], keys, NT, preferred_element_type=jnp.float32
                )
                column = (step * 2 + core) * 16 + part
                gated = jnp.maximum(logits, 0.0) * gates[:, column : column + 1]
                scores.append(jnp.sum(gated.reshape(2, 64, ROWS), axis=1))
            scores = jnp.concatenate(scores, axis=0) * IDX ** (-0.5)
            largest = jnp.max(scores, axis=1, keepdims=True)
            summed = jnp.sum(jnp.exp(scores - largest), axis=1, keepdims=True)
            result = jnp.where(lane == group, largest + jnp.log(summed), result)
    out_ref[...] = result


def index_partial(place, slabs, index_keys, payload):
    return pl.pallas_call(
        index_kernel,
        out_shape=jax.ShapeDtypeStruct((PAIRS, 128), jnp.float32),
        in_specs=[smem()] + [vmem()] * 5 + [pl.BlockSpec(memory_space=pl.ANY)],
        out_specs=vmem(),
        compiler_params=pltpu.CompilerParams(vmem_limit_bytes=16 << 20),
        cost_estimate=pl.CostEstimate(flops=2 * 4096 * 1024 * 256, bytes_accessed=2 << 20, transcendentals=0),
        name="index_partial",
    )(place, *slabs, index_keys, payload)


def log_add(one, two):
    top = jnp.maximum(one, two)
    return top + jnp.log(jnp.exp(one - top) + jnp.exp(two - top))


def split_three(value, lane, start):
    pieces = jnp.zeros(lane.shape, jnp.float32)
    for step in range(3):
        piece = value.astype(jnp.bfloat16).astype(jnp.float32)
        pieces = jnp.where(lane == start + step, piece, pieces)
        value = value - piece
    return pieces


def join_three(pieces, start):
    wide = pieces.astype(jnp.float32)
    return wide[:, start : start + 1] + wide[:, start + 1 : start + 2] + wide[:, start + 2 : start + 3]


def four_sum(refs):
    width = refs[0].shape[1] - STAT
    parts = [ref[:, :width].astype(jnp.float32) for ref in refs]
    logs = [join_three(ref[:, width:], 0) for ref in refs]
    return (parts[0] + parts[1]) + (parts[2] + parts[3]), log_add(log_add(logs[0], logs[1]), log_add(logs[2], logs[3]))


def middle_kernel(own_ref, far_ref, right_ref, left_ref, out_ref):
    summed, logs = four_sum((own_ref, far_ref, right_ref, left_ref))
    width = summed.shape[1]
    out_ref[:, :width] = summed.astype(jnp.bfloat16)
    lane = lax.broadcasted_iota(jnp.int32, (PAIRS, STAT), 1)
    out_ref[:, width:] = split_three(logs, lane, 0).astype(jnp.bfloat16)


def final_kernel(own_ref, far_ref, right_ref, left_ref, out_ref, log_ref):
    summed, logs = four_sum((own_ref, far_ref, right_ref, left_ref))
    steps, local = log_ref.shape
    flat = jnp.broadcast_to(logs, (PAIRS, STAT)).T[:1, :]
    for step in range(steps):
        out_ref[step] = summed[step * local : (step + 1) * local, :].astype(jnp.bfloat16)
        log_ref[step : step + 1, :] = flat[:, step * local : (step + 1) * local]


def summed_over(value, shift, final):
    parts = (value,) + tuple(lax.ppermute(value, "tp", shift(step)) for step in (2, 1, 3))
    if final:
        out_shape = (
            jax.ShapeDtypeStruct(final + (value.shape[1] - STAT,), jnp.bfloat16),
            jax.ShapeDtypeStruct(final, jnp.float32),
        )
        out_specs = (vmem(), vmem())
    else:
        out_shape = jax.ShapeDtypeStruct(value.shape, jnp.bfloat16)
        out_specs = vmem()
    return pl.pallas_call(
        final_kernel if final else middle_kernel,
        out_shape=out_shape,
        in_specs=[vmem()] * 4,
        out_specs=out_specs,
        compiler_params=pltpu.CompilerParams(vmem_limit_bytes=4 << 20),
        cost_estimate=pl.CostEstimate(flops=1 << 18, bytes_accessed=1 << 19, transcendentals=0),
        name="sum_last" if final else "sum_first",
    )(*parts)


def prepare_kernel(latent_ref, query_ref, block_ref, copies_ref):
    block_ref[...] = latent_ref[...].astype(jnp.bfloat16)
    for owner in range(TP):
        copies_ref[owner] = query_ref[...]


def prepare(latent, own_queries):
    return pl.pallas_call(
        prepare_kernel,
        out_shape=(
            jax.ShapeDtypeStruct(latent.shape, jnp.bfloat16),
            jax.ShapeDtypeStruct((TP,) + own_queries.shape, own_queries.dtype),
        ),
        in_specs=[vmem(), vmem()],
        out_specs=(vmem(), vmem()),
        compiler_params=pltpu.CompilerParams(vmem_limit_bytes=16 << 20),
        cost_estimate=pl.CostEstimate(flops=1000, bytes_accessed=5 << 20, transcendentals=0),
        name="prepare",
    )(latent, own_queries)


def x_shift(step):
    return [(x * 2 + c, ((x + step) % 4) * 2 + c) for x in range(4) for c in range(2)]


def y_shift(step):
    return [(z * 4 + y, z * 4 + (y + step) % 4) for z in range(4) for y in range(4)]


def z_shift(step):
    return [(z * 4 + y, ((z + step) % 4) * 4 + y) for z in range(4) for y in range(4)]


CORE_SWAP = [(i, i ^ 1) for i in range(PRE)]


def on_device(
    latent_rows,
    index_keys,
    queries,
    index_queries,
    index_gates,
    value_proj,
    out_proj,
    block_rows,
    block_owner,
    block_count,
):
    me_pre = lax.axis_index("pre")
    me_tp = lax.axis_index("tp")

    block, copies = prepare(latent_rows.T, queries.reshape(PAIRS * HEADS, KV))
    forward = lax.ppermute(block, "pre", x_shift(1))
    backward = lax.ppermute(block, "pre", x_shift(3))
    all_queries = lax.all_to_all(copies, "tp", 0, 0).reshape(QROWS, KV)

    def swapped(part):
        return lax.ppermute(part, "pre", CORE_SWAP)

    forward, backward, all_queries = lax.optimization_barrier((forward, backward, all_queries))
    far = [
        lax.ppermute(forward[: KV // 2], "pre", x_shift(1)),
        lax.ppermute(backward[KV // 2 :], "pre", x_shift(3)),
    ]

    valid = (jnp.arange(BLOCK, dtype=jnp.int32) < block_count[..., None]) & (block_owner == me_tp)[..., None]
    source = block_rows >> 10
    relative = ((((source >> 1) - (me_pre >> 1) + 1) & 3) << 1) | ((source ^ me_pre) & 1)
    effective = jnp.where(valid, (relative << 10) | (block_rows & (ROWS - 1)), -1).reshape(PAIRS, -1)
    masks, positions, counts = make_tables(effective)

    gate_rows = jnp.pad(index_gates.reshape(4, IDX), ((0, 12), (0, 0)))
    piece = jnp.concatenate([index_queries.reshape(PAIRS * 64, IDX), gate_rows], axis=0)
    slab = paired(piece, swapped(piece))
    slabs = [slab] + [lax.ppermute(slab, "pre", x_shift(4 - step)) for step in (1, 2, 3)]
    place = jnp.stack([me_pre >> 1, me_pre & 1]).astype(jnp.int32)

    near = [[part] for whole in (forward, block, backward) for part in (whole, swapped(whole))]
    state = attend(0, counts, all_queries, masks, positions, near)
    far, slabs, state = lax.optimization_barrier((far, slabs, state))
    far = [far, [swapped(part) for part in far]]
    payload = attend(6, counts, all_queries, masks, positions, far, state, last=True)
    received = lax.all_to_all(payload.reshape(TP, PAIRS * HEADS, LAT + STAT), "tp", 0, 0)
    partial = index_partial(place, slabs, index_keys, payload)
    partial = log_add(partial, lax.ppermute(partial, "pre", CORE_SWAP))
    parts = [lax.ppermute(partial, "pre", x_shift(step)) for step in (2, 1, 3)]
    partial = log_add(log_add(partial, parts[0]), log_add(parts[1], parts[2]))
    part_out = project(place, received, value_proj, out_proj, partial)
    return summed_over(summed_over(part_out, y_shift, None), z_shift, queries.shape[:2])


def solution(mesh):
    placed = (
        P(("pre", "tp"), None),
        P(("pre", "tp"), None),
        P(None, "pre", "tp", None),
        P(None, "pre", None, None),
        P(None, "pre", None),
        P("tp", None, None),
        P("tp", None),
        P(None, "pre", None, None),
        P(None, "pre", None),
        P(None, "pre", None),
    )
    return jax.shard_map(
        on_device,
        mesh=mesh,
        in_specs=placed,
        out_specs=(P(None, "pre", None), P(None, "pre")),
        check_vma=False,
    )
```

```python
import jax
import jax.numpy as jnp
from jax import lax
from jax.experimental import pallas as pl
from jax.experimental.pallas import tpu as pltpu
from jax.sharding import PartitionSpec as P

IDX = 128
LAT = 512
KV = 576
BLOCK = 64
PRE = 8
TP = 16
PAIRS = 8
HEADS = 8
ROWS = 1024
PACK = 256
QTILE = 256
PIECES = 4
PARTS = 4
STAT = 128
QROWS = TP * PAIRS * HEADS
LOWEST = -3.0e38
SOFT_SCALE = 192.0 ** (-0.5)
LOG2E = 1.4426950408889634
SCORE_SCALE = SOFT_SCALE * LOG2E

NT = (((1,), (1,)), ((), ()))


CHEAP = pl.CostEstimate(flops=1000, bytes_accessed=1000, transcendentals=0)


def vmem():
    return pl.BlockSpec(memory_space=pltpu.VMEM)


def smem():
    return pl.BlockSpec(memory_space=pltpu.SMEM)


def table_kernel(rows_ref, owner_ref, count_ref, mask_ref, pos_ref, total_ref):
    me_pre = lax.axis_index("pre")
    me_tp = lax.axis_index("tp")
    number = rows_ref.shape[2]
    before = (
        lax.broadcasted_iota(jnp.int32, (number, number), 0) < lax.broadcasted_iota(jnp.int32, (number, number), 1)
    ).astype(jnp.float32).astype(jnp.bfloat16)
    slot = lax.broadcasted_iota(jnp.int32, (8, number), 0).astype(jnp.float32)
    entry = lax.broadcasted_iota(jnp.int32, (8, BLOCK), 1).astype(jnp.float32)
    high_iota = lax.broadcasted_iota(jnp.int32, (PRE * 8, BLOCK), 0).astype(jnp.float32)
    low_iota = lax.broadcasted_iota(jnp.int32, (128, BLOCK), 0).astype(jnp.float32)
    for pair in range(PAIRS):
        step, local = pair // rows_ref.shape[1], pair % rows_ref.shape[1]
        rows = rows_ref[step, local]
        source = rows >> 10
        relative = ((((source >> 1) - (me_pre >> 1) + 1) & 3) << 1) | ((source ^ me_pre) & 1)
        high = ((relative << 3) | ((rows >> 7) & 7)).astype(jnp.float32).astype(jnp.bfloat16)
        low = (rows & 127).astype(jnp.float32).astype(jnp.bfloat16)
        owned = jnp.where(owner_ref[step, local : local + 1, :] == me_tp, 1.0, 0.0)
        rank = jnp.dot(owned.astype(jnp.bfloat16), before, preferred_element_type=jnp.float32)
        choose = jnp.where(slot == rank, owned, 0.0)
        limit = jnp.sum(choose * count_ref[step, local : local + 1, :].astype(jnp.float32), axis=1, keepdims=True)
        choose = choose.astype(jnp.bfloat16)
        valid = entry < limit
        high = jnp.where(valid, jnp.dot(choose, high, preferred_element_type=jnp.float32), -1.0)
        low = jnp.dot(choose, low, preferred_element_type=jnp.float32)
        chosen = jnp.zeros((PRE * 8, 128), jnp.float32)
        for block in range(number // TP):
            high_one = jnp.where(high_iota == high[block : block + 1, :], 1.0, 0.0).astype(jnp.bfloat16)
            low_one = jnp.where(low_iota == low[block : block + 1, :], 1.0, 0.0).astype(jnp.bfloat16)
            chosen = chosen + lax.dot_general(high_one, low_one, NT, preferred_element_type=jnp.float32)
        for block in range(PRE):
            for part in range(8):
                mask_ref[block, pair : pair + 1, part * 128 : (part + 1) * 128] = chosen[
                    block * 8 + part : block * 8 + part + 1, :
                ]
    union = jnp.concatenate([jnp.max(mask_ref[block], axis=0, keepdims=True) for block in range(PRE)], axis=0)
    before = (
        lax.broadcasted_iota(jnp.int32, (128, 128), 0) < lax.broadcasted_iota(jnp.int32, (128, 128), 1)
    ).astype(jnp.float32).astype(jnp.bfloat16)
    carry = jnp.zeros((PRE, 1), jnp.float32)
    for part in range(8):
        piece = union[:, part * 128 : (part + 1) * 128]
        ahead = jnp.dot(piece.astype(jnp.bfloat16), before, preferred_element_type=jnp.float32) + carry
        pos_ref[:, part * 128 : (part + 1) * 128] = jnp.where(piece > 0.0, ahead, -1.0)
        carry = carry + jnp.sum(piece, axis=1, keepdims=True)
    total_ref[...] = jnp.broadcast_to(carry, (PRE, 128)).astype(jnp.int32)


def make_tables(block_rows, block_owner, block_count):
    return pl.pallas_call(
        table_kernel,
        out_shape=(
            jax.ShapeDtypeStruct((PRE, PAIRS, ROWS), jnp.float32),
            jax.ShapeDtypeStruct((PRE, ROWS), jnp.float32),
            jax.ShapeDtypeStruct((PRE, 128), jnp.int32),
        ),
        in_specs=[vmem()] * 3,
        out_specs=(vmem(), vmem(), vmem()),
        compiler_params=pltpu.CompilerParams(vmem_limit_bytes=8 << 20),
        cost_estimate=CHEAP,
        name="row_tables",
    )(block_rows, block_owner, block_count)


def piece_kernel(query_ref, gate_ref, out_ref):
    pairs = [(step, local) for step in range(query_ref.shape[0]) for local in range(query_ref.shape[1])]
    heads = query_ref.shape[2]
    for pair, (step, local) in enumerate(pairs):
        out_ref[pair * heads : (pair + 1) * heads, :] = query_ref[step, local]
    gates = [gate_ref[step, local : local + 1, :].astype(jnp.float32) for step, local in pairs]
    lines = [jnp.concatenate(gates[2 * line : 2 * line + 2], axis=1) for line in range(4)]
    lines = jnp.concatenate(lines + [jnp.zeros((12, IDX), jnp.float32)], axis=0)
    out_ref[PAIRS * heads :, :] = lines.astype(jnp.bfloat16)


def index_piece(index_queries, index_gates):
    return pl.pallas_call(
        piece_kernel,
        out_shape=jax.ShapeDtypeStruct((PAIRS * index_queries.shape[2] + 16, IDX), jnp.bfloat16),
        in_specs=[vmem()] * 2,
        out_specs=vmem(),
        compiler_params=pltpu.CompilerParams(vmem_limit_bytes=4 << 20),
        cost_estimate=CHEAP,
        name="index_piece",
    )(index_queries, index_gates)


TOKEN = jax.ShapeDtypeStruct((8, 128), jnp.float32)


def token_kernel(*refs):
    refs[-1][...] = jnp.zeros(refs[-1].shape, jnp.float32)


def arrived(values):
    return pl.pallas_call(
        token_kernel,
        out_shape=TOKEN,
        in_specs=[pl.BlockSpec(memory_space=pl.ANY)] * len(values),
        out_specs=vmem(),
        compiler_params=pltpu.CompilerParams(vmem_limit_bytes=2 << 20),
        cost_estimate=CHEAP,
        name="arrived",
    )(*values)


def halves_kernel(forward_ref, backward_ref, top_ref, low_ref):
    top_ref[...] = forward_ref[...]
    low_ref[...] = backward_ref[...]


def halves(forward, backward):
    half = (forward.shape[0] // 2, forward.shape[1])
    out = jax.ShapeDtypeStruct(half, forward.dtype)
    return pl.pallas_call(
        halves_kernel,
        grid=(1,),
        out_shape=(out, out),
        in_specs=[pl.BlockSpec(half, lambda part: (0, 0)), pl.BlockSpec(half, lambda part: (1, 0))],
        out_specs=(pl.BlockSpec(half, lambda part: (0, 0)),) * 2,
        compiler_params=pltpu.CompilerParams(vmem_limit_bytes=8 << 20),
        cost_estimate=CHEAP,
        name="halves",
    )(forward, backward)


def pack_block(number, pieces, mask_row, pos_row, packed_ref, first_lane):
    slot = (lax.broadcasted_iota(jnp.int32, (PACK, ROWS), 0) + number * PACK).astype(jnp.float32)
    pick = jnp.where(slot == pos_row, 1.0, 0.0).astype(jnp.bfloat16)
    depth = KV // len(pieces)
    for order, piece in enumerate(pieces):
        packed = lax.dot_general(piece[...], pick, NT, preferred_element_type=jnp.float32)
        packed_ref[order * depth : (order + 1) * depth, first_lane : first_lane + PACK] = packed.astype(jnp.bfloat16)
    present = lax.dot_general(mask_row.astype(jnp.bfloat16), pick, NT, preferred_element_type=jnp.float32)
    return jnp.where(present > 0.5, 0.0, -jnp.inf)


def pack_kernel(base, parts, unused_ref, mask_ref, pos_ref, *refs):
    packed_ref, absent_ref = refs[-2:]
    for block, number in enumerate(parts):
        pieces, refs = refs[:number], refs[number:]
        row = base + block
        absent_ref[:, block * PACK : (block + 1) * PACK] = pack_block(
            0, pieces, mask_ref[row], pos_ref[row : row + 1, :], packed_ref, block * PACK
        )


def pack(base, token, masks, positions, sources):
    parts = [len(pieces) for pieces in sources]
    rows = sum([list(pieces) for pieces in sources], [])

    def body(*refs):
        pack_kernel(base, parts, *refs)

    return pl.pallas_call(
        body,
        out_shape=(
            jax.ShapeDtypeStruct((KV, len(parts) * PACK), jnp.bfloat16),
            jax.ShapeDtypeStruct((PAIRS, len(parts) * PACK), jnp.float32),
        ),
        in_specs=[pl.BlockSpec(memory_space=pl.ANY)] + [vmem()] * (2 + len(rows)),
        out_specs=(vmem(), vmem()),
        compiler_params=pltpu.CompilerParams(vmem_limit_bytes=16 << 20),
        cost_estimate=CHEAP,
        name="pack_%d" % len(parts),
    )(token, masks, positions, *rows)


def attend_kernel(base, parts, shapes, first, last, count_ref, mask_ref, pos_ref, *refs):
    queries, refs = refs[: shapes[0]], refs[shapes[0] :]
    packs, refs = refs[: 2 * shapes[1]], refs[2 * shapes[1] :]
    sources = []
    for number in parts:
        sources.append(refs[:number])
        refs = refs[number:]
    groups = len(queries)
    if not first:
        former_state, refs = refs[: 2 * groups], refs[2 * groups :]
    if last:
        outs, refs = refs[:groups], refs[groups:]
    state, refs = refs[: 2 * groups], refs[2 * groups :]
    if not last:
        refs[0][...] = jnp.zeros(refs[0].shape, jnp.float32)
        refs = refs[1:]
    packed_ref, rows_ref, sem = refs
    column = lax.broadcasted_iota(jnp.int32, (QTILE, STAT), 1)

    def attention(packed, absent, fresh):
        span = absent.shape[1]
        for group in range(groups):
            stat_ref, acc_ref = state[2 * group], state[2 * group + 1]
            query = queries[group][...]
            scores = [jnp.dot(query, ref[...], preferred_element_type=jnp.float32) for ref in packed]
            scores = scores[0] if len(scores) == 1 else jnp.concatenate(scores, axis=1)
            scores = scores.reshape(QTILE // 64, PAIRS, HEADS, span) * SCORE_SCALE + absent[None, :, None, :]
            scores = scores.reshape(QTILE, span)
            newer = jnp.max(scores, axis=1, keepdims=True)
            if fresh and first:
                newer = jnp.maximum(newer, LOWEST)
            else:
                stats, acc = (former_state[2 * group], former_state[2 * group + 1]) if fresh else (stat_ref, acc_ref)
                former = stats[:, :1]
                newer = jnp.maximum(former, newer)
                decay = jnp.exp2(former - newer)
            weights = jnp.exp2(scores - newer)
            total = jnp.sum(weights, axis=1, keepdims=True)
            weights = weights.astype(jnp.bfloat16)
            added, start = None, 0
            for ref in packed:
                width = ref.shape[1]
                piece = lax.dot_general(
                    weights[:, start : start + width], ref[:LAT, :], NT, preferred_element_type=jnp.float32
                )
                added = piece if added is None else added + piece
                start += width
            if not (fresh and first):
                total = stats[:, STAT // 2 : STAT // 2 + 1] * decay + total
                added = acc[...] * decay + added
            acc_ref[...] = added
            stat_ref[...] = jnp.where(column < STAT // 2, newer, total)

    attention(packs[::2], jnp.concatenate([ref[...] for ref in packs[1::2]], axis=1), True)

    for block in range(len(parts)):
        row = base + block
        rounds = (count_ref[row, 0] + (PACK - 1)) // PACK

        @pl.when(rounds > 1)
        def _(block=block, row=row, rounds=rounds):
            depth = KV // len(sources[block])
            for order, piece in enumerate(sources[block]):
                copy = pltpu.make_async_copy(piece, rows_ref.at[pl.ds(order * depth, depth), :], sem)
                copy.start()
                copy.wait()

            @pl.loop(1, rounds)
            def _(number):
                absent = pack_block(
                    number, [rows_ref], mask_ref[row], pos_ref[row : row + 1, :], packed_ref, 0
                )
                attention([packed_ref], absent, False)

    if last:
        for group in range(groups):
            stat_ref, acc_ref = state[2 * group], state[2 * group + 1]
            write_payload(outs[group], stat_ref[:, :1], stat_ref[:, STAT // 2 : STAT // 2 + 1], acc_ref[...])


def write_payload(out_ref, highest, total, acc):
    lane = lax.broadcasted_iota(jnp.int32, (acc.shape[0], STAT), 1)
    out_ref[:, :LAT] = acc.astype(jnp.bfloat16)
    out_ref[:, LAT:] = (split_three(highest, lane, 0) + split_three(total, lane, 3)).astype(jnp.bfloat16)


def attend(base, counts, queries, masks, positions, packs, sources, states=None, last=False):
    parts = [len(pieces) for pieces in sources]
    first = states is None
    groups = len(queries)
    shapes = (
        jax.ShapeDtypeStruct((QTILE, STAT), jnp.float32),
        jax.ShapeDtypeStruct((QTILE, LAT), jnp.float32),
    ) * groups
    if last:
        out_shape = (jax.ShapeDtypeStruct((QTILE, LAT + STAT), jnp.bfloat16),) * groups
        scratch = [pltpu.VMEM(s.shape, s.dtype) for s in shapes]
    else:
        out_shape = shapes + (TOKEN,)
        scratch = []
    scratch = scratch + [
        pltpu.VMEM((KV, PACK), jnp.bfloat16),
        pltpu.VMEM((KV, ROWS), jnp.bfloat16),
        pltpu.SemaphoreType.DMA(()),
    ]
    packed = sum([list(pair) for pair in packs], [])
    rows = [pltpu.with_memory_space_constraint(piece, pltpu.HBM) for pieces in sources for piece in pieces]
    former = [] if first else [part for state in states for part in state]

    def body(*refs):
        attend_kernel(base, parts, (groups, len(packs)), first, last, *refs)

    in_specs = [smem()] + [vmem()] * (2 + groups + len(packed))
    in_specs = in_specs + [pl.BlockSpec(memory_space=pl.ANY)] * len(rows) + [vmem()] * len(former)
    outs = pl.pallas_call(
        body,
        out_shape=out_shape,
        in_specs=in_specs,
        out_specs=(vmem(),) * len(out_shape),
        scratch_shapes=scratch,
        compiler_params=pltpu.CompilerParams(vmem_limit_bytes=16 << 20),
        cost_estimate=CHEAP,
        name="attend_%d_%d" % (len(parts), groups),
    )(counts, masks, positions, *queries, *packed, *rows, *former)
    if last:
        return list(outs)
    return [tuple(outs[2 * group : 2 * group + 2]) for group in range(groups)], outs[-1]


def combined(refs):
    row = lax.broadcasted_iota(jnp.int32, (STAT, 2 * STAT), 0)
    col = lax.broadcasted_iota(jnp.int32, (STAT, 2 * STAT), 1)
    spread = jnp.where((row // 3) == (col // STAT), 1.0, 0.0).astype(jnp.bfloat16)
    stats = [jnp.dot(ref[:, LAT:], spread, preferred_element_type=jnp.float32) for ref in refs]
    highest = stats[0][:, :STAT]
    for stat in stats[1:]:
        highest = jnp.maximum(highest, stat[:, :STAT])
    total, acc = None, None
    for ref, stat in zip(refs, stats):
        weight = jnp.exp2(stat[:, :STAT] - highest)
        wide = jnp.concatenate([weight] * (LAT // STAT), axis=1) * ref[:, :LAT].astype(jnp.float32)
        total = weight * stat[:, STAT:] if total is None else total + weight * stat[:, STAT:]
        acc = wide if acc is None else acc + wide
    return highest, total, acc


def combine_kernel(*refs):
    highest, total, acc = combined(refs[:4])
    for part, out_ref in enumerate(refs[4:]):
        here = slice(part * PAIRS * HEADS, (part + 1) * PAIRS * HEADS)
        write_payload(out_ref, highest[here, :1], total[here, :1], acc[here, :])


def combine(parts):
    return pl.pallas_call(
        combine_kernel,
        out_shape=(jax.ShapeDtypeStruct((PAIRS * HEADS, LAT + STAT), jnp.bfloat16),) * 4,
        in_specs=[vmem()] * 4,
        out_specs=(vmem(),) * 4,
        compiler_params=pltpu.CompilerParams(vmem_limit_bytes=8 << 20),
        cost_estimate=CHEAP,
        name="combine",
    )(*parts)


def fetch_kernel(source_ref, unused_ref, out_ref, sems):
    depth = out_ref.shape[0] // PIECES
    copies = [
        pltpu.make_async_copy(
            source_ref.at[pl.ds(piece * depth, depth)], out_ref.at[pl.ds(piece * depth, depth)], sems.at[piece]
        )
        for piece in range(PIECES)
    ]
    for copy in copies:
        copy.start()
    for copy in copies:
        copy.wait()


def fetched(weights, payload):
    return pl.pallas_call(
        fetch_kernel,
        out_shape=pltpu.VMEM(weights.shape, weights.dtype),
        in_specs=[pl.BlockSpec(memory_space=pl.ANY)] * 2,
        out_specs=vmem(),
        scratch_shapes=[pltpu.SemaphoreType.DMA((PIECES,))],
        compiler_params=pltpu.CompilerParams(vmem_limit_bytes=16 << 20),
        cost_estimate=CHEAP,
        name="fetch_out_proj",
    )(pltpu.with_memory_space_constraint(weights, pltpu.HBM), payload)


def project_kernel(value_ref, weights, partial_ref, *refs):
    out_ref = refs[4]
    highest, total, acc = combined(refs[:4])
    attn = (acc / jnp.concatenate([total] * (LAT // STAT), axis=1)).astype(jnp.bfloat16)
    head_of = lax.broadcasted_iota(jnp.int32, (PAIRS, HEADS, 128), 1)
    pieces = []
    for head in range(HEADS):
        product = jnp.dot(attn, value_ref[head], preferred_element_type=jnp.float32)
        product = jnp.where(head_of == head, product.reshape(PAIRS, HEADS, 128), 0.0)
        pieces.append(jnp.sum(product, axis=1))
    values = jnp.concatenate(pieces, axis=1).astype(jnp.bfloat16)
    width = weights.shape[1]
    result = jnp.dot(values, weights[...], preferred_element_type=jnp.float32)
    out_ref[:, :width] = result.astype(jnp.bfloat16)
    lane = lax.broadcasted_iota(jnp.int32, (PAIRS, STAT), 1)
    group = lax.axis_index("pre")
    mine = jnp.sum(jnp.where(lane == group, partial_ref[...], 0.0), axis=1, keepdims=True)
    out_ref[:, width:] = split_three(mine, lane, 0).astype(jnp.bfloat16)


def project(received, value_proj, out_proj, partial):
    return pl.pallas_call(
        project_kernel,
        out_shape=jax.ShapeDtypeStruct((PAIRS, out_proj.shape[1] + STAT), jnp.bfloat16),
        in_specs=[vmem()] * 7,
        out_specs=vmem(),
        compiler_params=pltpu.CompilerParams(vmem_limit_bytes=16 << 20),
        cost_estimate=CHEAP,
        name="project",
    )(value_proj, pltpu.with_memory_space_constraint(out_proj, pltpu.VMEM), partial, *received)


def index_kernel(*refs):
    place = lax.axis_index("pre")
    slabs, (key_ref, unused_ref, out_ref) = refs[:PRE], refs[PRE:]
    keys = key_ref[...].astype(jnp.bfloat16)
    gates = jnp.concatenate([ref[PAIRS * 64 :, :] for ref in slabs], axis=0)
    gates = gates.astype(jnp.float32).T
    lane = lax.broadcasted_iota(jnp.int32, (PAIRS, 128), 1)
    result = jnp.zeros((PAIRS, 128), jnp.float32)
    for core in range(2):
        for step in range(4):
            ref = slabs[core * 4 + step]
            group = (((place >> 1) + step) & 3) * 2 + (core ^ (place & 1))
            scores = []
            for part in range(4):
                logits = lax.dot_general(
                    ref[part * 128 : (part + 1) * 128, :], keys, NT, preferred_element_type=jnp.float32
                )
                column = (core * 4 + step) * 16 + part
                gated = jnp.maximum(logits, 0.0) * gates[:, column : column + 1]
                scores.append(jnp.sum(gated.reshape(2, 64, ROWS), axis=1))
            scores = jnp.concatenate(scores, axis=0) * IDX ** (-0.5)
            largest = jnp.max(scores, axis=1, keepdims=True)
            summed = jnp.sum(jnp.exp(scores - largest), axis=1, keepdims=True)
            result = jnp.where(lane == group, largest + jnp.log(summed), result)
    out_ref[...] = result


def index_partial(slabs, index_keys, payload):
    return pl.pallas_call(
        index_kernel,
        out_shape=jax.ShapeDtypeStruct((PAIRS, 128), jnp.float32),
        in_specs=[vmem()] * (PRE + 1) + [pl.BlockSpec(memory_space=pl.ANY)],
        out_specs=vmem(),
        compiler_params=pltpu.CompilerParams(vmem_limit_bytes=16 << 20),
        cost_estimate=CHEAP,
        name="index_partial",
    )(*slabs, index_keys, payload)


def log_add(one, two):
    top = jnp.maximum(one, two)
    return top + jnp.log(jnp.exp(one - top) + jnp.exp(two - top))


def split_three(value, lane, start):
    pieces = jnp.zeros(lane.shape, jnp.float32)
    for step in range(3):
        piece = value.astype(jnp.bfloat16).astype(jnp.float32)
        pieces = jnp.where(lane == start + step, piece, pieces)
        value = value - piece
    return pieces


def join_three(pieces, start):
    wide = pieces.astype(jnp.float32)
    return wide[:, start : start + 1] + wide[:, start + 1 : start + 2] + wide[:, start + 2 : start + 3]


def four_sum(refs):
    width = refs[0].shape[1] - STAT
    parts = [ref[:, :width].astype(jnp.float32) for ref in refs]
    logs = [join_three(ref[:, width:], 0) for ref in refs]
    return (parts[0] + parts[1]) + (parts[2] + parts[3]), log_add(log_add(logs[0], logs[1]), log_add(logs[2], logs[3]))


def middle_kernel(own_ref, far_ref, right_ref, left_ref, out_ref):
    summed, logs = four_sum((own_ref, far_ref, right_ref, left_ref))
    width = summed.shape[1]
    out_ref[:, :width] = summed.astype(jnp.bfloat16)
    lane = lax.broadcasted_iota(jnp.int32, (PAIRS, STAT), 1)
    out_ref[:, width:] = split_three(logs, lane, 0).astype(jnp.bfloat16)


def final_kernel(own_ref, far_ref, right_ref, left_ref, out_ref, log_ref):
    summed, logs = four_sum((own_ref, far_ref, right_ref, left_ref))
    steps, local = log_ref.shape
    flat = jnp.broadcast_to(logs, (PAIRS, STAT)).T[:1, :]
    for step in range(steps):
        out_ref[step] = summed[step * local : (step + 1) * local, :].astype(jnp.bfloat16)
        log_ref[step : step + 1, :] = flat[:, step * local : (step + 1) * local]


def summed_over(value, shift, final):
    parts = (value,) + tuple(lax.ppermute(value, "tp", shift(step)) for step in (2, 1, 3))
    if final:
        out_shape = (
            jax.ShapeDtypeStruct(final + (value.shape[1] - STAT,), jnp.bfloat16),
            jax.ShapeDtypeStruct(final, jnp.float32),
        )
        out_specs = (vmem(), vmem())
    else:
        out_shape = jax.ShapeDtypeStruct(value.shape, jnp.bfloat16)
        out_specs = vmem()
    return pl.pallas_call(
        final_kernel if final else middle_kernel,
        out_shape=out_shape,
        in_specs=[vmem()] * 4,
        out_specs=out_specs,
        compiler_params=pltpu.CompilerParams(vmem_limit_bytes=4 << 20),
        cost_estimate=CHEAP,
        name="sum_last" if final else "sum_first",
    )(*parts)


def prepare_kernel(latent_ref, block_ref):
    block_ref[...] = latent_ref[...].astype(jnp.bfloat16)


def prepare(latent):
    spec = pl.BlockSpec((KV // PARTS, ROWS), lambda part: (part, 0))
    return pl.pallas_call(
        prepare_kernel,
        grid=(PARTS,),
        out_shape=jax.ShapeDtypeStruct(latent.shape, jnp.bfloat16),
        in_specs=[spec],
        out_specs=spec,
        compiler_params=pltpu.CompilerParams(vmem_limit_bytes=8 << 20),
        cost_estimate=CHEAP,
        name="prepare",
    )(pltpu.with_memory_space_constraint(latent, pltpu.HBM))


def x_shift(step):
    return [(x * 2 + c, ((x + step) % 4) * 2 + c) for x in range(4) for c in range(2)]


def y_shift(step):
    return [(z * 4 + y, z * 4 + (y + step) % 4) for z in range(4) for y in range(4)]


def z_shift(step):
    return [(z * 4 + y, ((z + step) % 4) * 4 + y) for z in range(4) for y in range(4)]


CORE_SWAP = [(i, i ^ 1) for i in range(PRE)]


def on_device(
    latent_rows,
    index_keys,
    queries,
    index_queries,
    index_gates,
    value_proj,
    out_proj,
    block_rows,
    block_owner,
    block_count,
):
    block = prepare(latent_rows.T)
    forward = lax.ppermute(block, "pre", x_shift(1))
    backward = lax.ppermute(block, "pre", x_shift(3))

    own_queries = queries.reshape(PAIRS * HEADS, KV)
    row = jnp.concatenate(
        [own_queries] + [lax.ppermute(own_queries, "tp", y_shift(4 - step)) for step in (1, 2, 3)], axis=0
    )
    plane = [row] + [lax.ppermute(row, "tp", z_shift(4 - step)) for step in (1, 2, 3)]

    def swapped(part):
        return lax.ppermute(part, "pre", CORE_SWAP)

    def both(parts):
        return [list(parts), [swapped(part) for part in parts]]

    masks, positions, counts = make_tables(block_rows, block_owner, block_count)
    own = both([block])
    own_pack = pack(2, masks, masks, positions, own)
    piece = index_piece(index_queries, index_gates)

    token = arrived(plane[1:] + [own_pack[0], piece])
    forward, backward, token = lax.optimization_barrier((forward, backward, token))
    top, low = halves(forward, backward)
    far = [lax.ppermute(top, "pre", x_shift(1)), lax.ppermute(low, "pre", x_shift(3))]

    slabs = [piece] + [lax.ppermute(piece, "pre", x_shift(4 - step)) for step in (1, 2, 3)]

    sides = both([forward]) + both([backward])
    side_packs = [pack(base, token, masks, positions, rows) for base, rows in ((0, sides[:2]), (4, sides[2:]))]
    packs = [side_packs[0], own_pack, side_packs[1]]
    states, token = attend(0, counts, plane, masks, positions, packs, sides[:2] + own + sides[2:])
    far, slabs, token = lax.optimization_barrier((far, slabs, token))
    slabs = slabs + [swapped(part) for part in slabs]
    far = both(far)
    packs = [pack(6, token, masks, positions, far)]

    payloads = attend(6, counts, plane[1:], masks, positions, packs, far, states[1:], last=True)
    payload = attend(6, counts, plane[:1], masks, positions, packs, far, states[:1], last=True)
    parts = payload + [lax.ppermute(payloads[step - 1], "tp", z_shift(step)) for step in (1, 2, 3)]
    parts = combine(parts)
    received = [parts[0]] + [lax.ppermute(parts[step], "tp", y_shift(step)) for step in (1, 2, 3)]
    payload = payloads[0]
    weights = fetched(out_proj, payload)
    partial = index_partial(slabs, index_keys, payload)
    partial = log_add(partial, lax.ppermute(partial, "pre", CORE_SWAP))
    parts = [lax.ppermute(partial, "pre", x_shift(step)) for step in (2, 1, 3)]
    partial = log_add(log_add(partial, parts[0]), log_add(parts[1], parts[2]))
    part_out = project(received, value_proj, weights, partial)
    return summed_over(summed_over(part_out, y_shift, None), z_shift, queries.shape[:2])


def solution(mesh):
    placed = (
        P(("pre", "tp"), None),
        P(("pre", "tp"), None),
        P(None, "pre", "tp", None),
        P(None, "pre", None, None),
        P(None, "pre", None),
        P("tp", None, None),
        P("tp", None),
        P(None, "pre", None, None),
        P(None, "pre", None),
        P(None, "pre", None),
    )
    return jax.shard_map(
        on_device,
        mesh=mesh,
        in_specs=placed,
        out_specs=(P(None, "pre", None), P(None, "pre")),
        check_vma=False,
    )
```

```python
import jax
import jax.numpy as jnp
from jax import lax
from jax.experimental import pallas as pl
from jax.experimental.pallas import tpu as pltpu
from jax.sharding import PartitionSpec as P

IDX = 128
LAT = 512
KV = 576
BLOCK = 64
PRE = 8
TP = 16
PAIRS = 8
HEADS = 8
ROWS = 1024
PACK = 256
QTILE = 256
PARTS = 4
STAT = 128
QROWS = TP * PAIRS * HEADS
LOWEST = -3.0e38
SOFT_SCALE = 192.0 ** (-0.5)
LOG2E = 1.4426950408889634
SCORE_SCALE = SOFT_SCALE * LOG2E

NT = (((1,), (1,)), ((), ()))


CHEAP = pl.CostEstimate(flops=1000, bytes_accessed=1000, transcendentals=0)


def vmem():
    return pl.BlockSpec(memory_space=pltpu.VMEM)


def smem():
    return pl.BlockSpec(memory_space=pltpu.SMEM)


def table_kernel(rows_ref, owner_ref, count_ref, mask_ref, pos_ref, total_ref):
    me_pre = lax.axis_index("pre")
    me_tp = lax.axis_index("tp")
    number = rows_ref.shape[2]
    before = (
        lax.broadcasted_iota(jnp.int32, (number, number), 0) < lax.broadcasted_iota(jnp.int32, (number, number), 1)
    ).astype(jnp.float32).astype(jnp.bfloat16)
    slot = lax.broadcasted_iota(jnp.int32, (8, number), 0).astype(jnp.float32)
    entry = lax.broadcasted_iota(jnp.int32, (8, BLOCK), 1).astype(jnp.float32)
    high_iota = lax.broadcasted_iota(jnp.int32, (PRE * 8, BLOCK), 0).astype(jnp.float32)
    low_iota = lax.broadcasted_iota(jnp.int32, (128, BLOCK), 0).astype(jnp.float32)
    for pair in range(PAIRS):
        step, local = pair // rows_ref.shape[1], pair % rows_ref.shape[1]
        rows = rows_ref[step, local]
        source = rows >> 10
        relative = ((((source >> 1) - (me_pre >> 1) + 1) & 3) << 1) | ((source ^ me_pre) & 1)
        high = ((relative << 3) | ((rows >> 7) & 7)).astype(jnp.float32).astype(jnp.bfloat16)
        low = (rows & 127).astype(jnp.float32).astype(jnp.bfloat16)
        owned = jnp.where(owner_ref[step, local : local + 1, :] == me_tp, 1.0, 0.0)
        rank = jnp.dot(owned.astype(jnp.bfloat16), before, preferred_element_type=jnp.float32)
        choose = jnp.where(slot == rank, owned, 0.0)
        limit = jnp.sum(choose * count_ref[step, local : local + 1, :].astype(jnp.float32), axis=1, keepdims=True)
        choose = choose.astype(jnp.bfloat16)
        valid = entry < limit
        high = jnp.where(valid, jnp.dot(choose, high, preferred_element_type=jnp.float32), -1.0)
        low = jnp.dot(choose, low, preferred_element_type=jnp.float32)
        chosen = jnp.zeros((PRE * 8, 128), jnp.float32)
        for block in range(number // TP):
            high_one = jnp.where(high_iota == high[block : block + 1, :], 1.0, 0.0).astype(jnp.bfloat16)
            low_one = jnp.where(low_iota == low[block : block + 1, :], 1.0, 0.0).astype(jnp.bfloat16)
            chosen = chosen + lax.dot_general(high_one, low_one, NT, preferred_element_type=jnp.float32)
        for block in range(PRE):
            for part in range(8):
                mask_ref[block, pair : pair + 1, part * 128 : (part + 1) * 128] = chosen[
                    block * 8 + part : block * 8 + part + 1, :
                ]
    union = jnp.concatenate([jnp.max(mask_ref[block], axis=0, keepdims=True) for block in range(PRE)], axis=0)
    before = (
        lax.broadcasted_iota(jnp.int32, (128, 128), 0) < lax.broadcasted_iota(jnp.int32, (128, 128), 1)
    ).astype(jnp.float32).astype(jnp.bfloat16)
    carry = jnp.zeros((PRE, 1), jnp.float32)
    for part in range(8):
        piece = union[:, part * 128 : (part + 1) * 128]
        ahead = jnp.dot(piece.astype(jnp.bfloat16), before, preferred_element_type=jnp.float32) + carry
        pos_ref[:, part * 128 : (part + 1) * 128] = jnp.where(piece > 0.0, ahead, -1.0)
        carry = carry + jnp.sum(piece, axis=1, keepdims=True)
    total_ref[...] = jnp.broadcast_to(carry, (PRE, 128)).astype(jnp.int32)


def make_tables(block_rows, block_owner, block_count):
    return pl.pallas_call(
        table_kernel,
        out_shape=(
            jax.ShapeDtypeStruct((PRE, PAIRS, ROWS), jnp.float32),
            jax.ShapeDtypeStruct((PRE, ROWS), jnp.float32),
            jax.ShapeDtypeStruct((PRE, 128), jnp.int32),
        ),
        in_specs=[vmem()] * 3,
        out_specs=(vmem(), vmem(), vmem()),
        compiler_params=pltpu.CompilerParams(vmem_limit_bytes=8 << 20),
        cost_estimate=CHEAP,
        name="row_tables",
    )(block_rows, block_owner, block_count)


def piece_kernel(query_ref, gate_ref, key_ref, out_ref, key_out_ref):
    pairs = [(step, local) for step in range(query_ref.shape[0]) for local in range(query_ref.shape[1])]
    heads = query_ref.shape[2]
    for pair, (step, local) in enumerate(pairs):
        out_ref[pair * heads : (pair + 1) * heads, :] = query_ref[step, local]
    gates = [gate_ref[step, local : local + 1, :].astype(jnp.float32) for step, local in pairs]
    lines = [jnp.concatenate(gates[2 * line : 2 * line + 2], axis=1) for line in range(4)]
    lines = jnp.concatenate(lines + [jnp.zeros((12, IDX), jnp.float32)], axis=0)
    out_ref[PAIRS * heads :, :] = lines.astype(jnp.bfloat16)
    key_out_ref[...] = key_ref[...].astype(jnp.bfloat16)


def index_piece(index_queries, index_gates, index_keys):
    return pl.pallas_call(
        piece_kernel,
        out_shape=(
            jax.ShapeDtypeStruct((PAIRS * index_queries.shape[2] + 16, IDX), jnp.bfloat16),
            jax.ShapeDtypeStruct(index_keys.shape, jnp.bfloat16),
        ),
        in_specs=[vmem()] * 3,
        out_specs=(vmem(),) * 2,
        compiler_params=pltpu.CompilerParams(vmem_limit_bytes=4 << 20),
        cost_estimate=CHEAP,
        name="index_piece",
    )(index_queries, index_gates, index_keys)


TOKEN = jax.ShapeDtypeStruct((8, 128), jnp.float32)


def token_kernel(*refs):
    refs[-1][...] = jnp.zeros(refs[-1].shape, jnp.float32)


def arrived(values):
    return pl.pallas_call(
        token_kernel,
        out_shape=TOKEN,
        in_specs=[pl.BlockSpec(memory_space=pl.ANY)] * len(values),
        out_specs=vmem(),
        compiler_params=pltpu.CompilerParams(vmem_limit_bytes=2 << 20),
        cost_estimate=CHEAP,
        name="arrived",
    )(*values)


def halves_kernel(forward_ref, backward_ref, top_ref, low_ref):
    top_ref[...] = forward_ref[...]
    low_ref[...] = backward_ref[...]


def halves(forward, backward):
    half = (forward.shape[0] // 2, forward.shape[1])
    out = jax.ShapeDtypeStruct(half, forward.dtype)
    return pl.pallas_call(
        halves_kernel,
        grid=(1,),
        out_shape=(out, out),
        in_specs=[pl.BlockSpec(half, lambda part: (0, 0)), pl.BlockSpec(half, lambda part: (1, 0))],
        out_specs=(pl.BlockSpec(half, lambda part: (0, 0)),) * 2,
        compiler_params=pltpu.CompilerParams(vmem_limit_bytes=8 << 20),
        cost_estimate=CHEAP,
        name="halves",
    )(forward, backward)


def pack_block(number, pieces, mask_row, pos_row, packed_ref, first_lane):
    slot = (lax.broadcasted_iota(jnp.int32, (PACK, ROWS), 0) + number * PACK).astype(jnp.float32)
    pick = jnp.where(slot == pos_row, 1.0, 0.0).astype(jnp.bfloat16)
    depth = KV // len(pieces)
    for order, piece in enumerate(pieces):
        packed = lax.dot_general(piece[...], pick, NT, preferred_element_type=jnp.float32)
        packed_ref[order * depth : (order + 1) * depth, first_lane : first_lane + PACK] = packed.astype(jnp.bfloat16)
    present = lax.dot_general(mask_row.astype(jnp.bfloat16), pick, NT, preferred_element_type=jnp.float32)
    return jnp.where(present > 0.5, 0.0, -jnp.inf)


def pack_kernel(base, parts, unused_ref, mask_ref, pos_ref, *refs):
    packed_ref, absent_ref = refs[-2:]
    for block, number in enumerate(parts):
        pieces, refs = refs[:number], refs[number:]
        row = base + block
        absent_ref[:, block * PACK : (block + 1) * PACK] = pack_block(
            0, pieces, mask_ref[row], pos_ref[row : row + 1, :], packed_ref, block * PACK
        )


def pack(base, token, masks, positions, sources):
    parts = [len(pieces) for pieces in sources]
    rows = sum([list(pieces) for pieces in sources], [])

    def body(*refs):
        pack_kernel(base, parts, *refs)

    return pl.pallas_call(
        body,
        out_shape=(
            jax.ShapeDtypeStruct((KV, len(parts) * PACK), jnp.bfloat16),
            jax.ShapeDtypeStruct((PAIRS, len(parts) * PACK), jnp.float32),
        ),
        in_specs=[pl.BlockSpec(memory_space=pl.ANY)] + [vmem()] * (2 + len(rows)),
        out_specs=(vmem(), vmem()),
        compiler_params=pltpu.CompilerParams(vmem_limit_bytes=16 << 20),
        cost_estimate=CHEAP,
        name="pack_%d" % len(parts),
    )(token, masks, positions, *rows)


def attend_kernel(base, parts, shapes, first, last, count_ref, mask_ref, pos_ref, *refs):
    queries, refs = refs[: shapes[0]], refs[shapes[0] :]
    packs, refs = refs[: 2 * shapes[1]], refs[2 * shapes[1] :]
    sources = []
    for number in parts:
        sources.append(refs[:number])
        refs = refs[number:]
    groups = len(queries)
    if not first:
        former_state, refs = refs[: 2 * groups], refs[2 * groups :]
    if last:
        outs, refs = refs[:groups], refs[groups:]
    state, refs = refs[: 2 * groups], refs[2 * groups :]
    if not last:
        refs[0][...] = jnp.zeros(refs[0].shape, jnp.float32)
        refs = refs[1:]
    packed_ref, rows_ref, sem = refs
    column = lax.broadcasted_iota(jnp.int32, (QTILE, STAT), 1)

    def attention(packed, absent, fresh):
        span = absent.shape[1]
        for group in range(groups):
            stat_ref, acc_ref = state[2 * group], state[2 * group + 1]
            query = queries[group][...]
            scores = [jnp.dot(query, ref[...], preferred_element_type=jnp.float32) for ref in packed]
            scores = scores[0] if len(scores) == 1 else jnp.concatenate(scores, axis=1)
            scores = scores.reshape(QTILE // 64, PAIRS, HEADS, span) * SCORE_SCALE + absent[None, :, None, :]
            scores = scores.reshape(QTILE, span)
            newer = jnp.max(scores, axis=1, keepdims=True)
            if fresh and first:
                newer = jnp.maximum(newer, LOWEST)
            else:
                stats, acc = (former_state[2 * group], former_state[2 * group + 1]) if fresh else (stat_ref, acc_ref)
                former = stats[:, :1]
                newer = jnp.maximum(former, newer)
                decay = jnp.exp2(former - newer)
            weights = jnp.exp2(scores - newer)
            total = jnp.sum(weights, axis=1, keepdims=True)
            weights = weights.astype(jnp.bfloat16)
            added, start = None, 0
            for ref in packed:
                width = ref.shape[1]
                piece = lax.dot_general(
                    weights[:, start : start + width], ref[:LAT, :], NT, preferred_element_type=jnp.float32
                )
                added = piece if added is None else added + piece
                start += width
            if not (fresh and first):
                total = stats[:, STAT // 2 : STAT // 2 + 1] * decay + total
                added = acc[...] * decay + added
            acc_ref[...] = added
            stat_ref[...] = jnp.where(column < STAT // 2, newer, total)

    attention(packs[::2], jnp.concatenate([ref[...] for ref in packs[1::2]], axis=1), True)

    for block in range(len(parts)):
        row = base + block
        rounds = (count_ref[row, 0] + (PACK - 1)) // PACK

        @pl.when(rounds > 1)
        def _(block=block, row=row, rounds=rounds):
            depth = KV // len(sources[block])
            for order, piece in enumerate(sources[block]):
                copy = pltpu.make_async_copy(piece, rows_ref.at[pl.ds(order * depth, depth), :], sem)
                copy.start()
                copy.wait()

            @pl.loop(1, rounds)
            def _(number):
                absent = pack_block(
                    number, [rows_ref], mask_ref[row], pos_ref[row : row + 1, :], packed_ref, 0
                )
                attention([packed_ref], absent, False)

    if last:
        for group in range(groups):
            stat_ref, acc_ref = state[2 * group], state[2 * group + 1]
            write_payload(outs[group], stat_ref[:, :1], stat_ref[:, STAT // 2 : STAT // 2 + 1], acc_ref[...])


def write_payload(out_ref, highest, total, acc):
    lane = lax.broadcasted_iota(jnp.int32, (acc.shape[0], STAT), 1)
    out_ref[:, :LAT] = acc.astype(jnp.bfloat16)
    out_ref[:, LAT:] = (split_three(highest, lane, 0) + split_three(total, lane, 3)).astype(jnp.bfloat16)


def attend(base, counts, queries, masks, positions, packs, sources, states=None, last=False):
    parts = [len(pieces) for pieces in sources]
    first = states is None
    groups = len(queries)
    shapes = (
        jax.ShapeDtypeStruct((QTILE, STAT), jnp.float32),
        jax.ShapeDtypeStruct((QTILE, LAT), jnp.float32),
    ) * groups
    if last:
        out_shape = (jax.ShapeDtypeStruct((QTILE, LAT + STAT), jnp.bfloat16),) * groups
        scratch = [pltpu.VMEM(s.shape, s.dtype) for s in shapes]
    else:
        out_shape = shapes + (TOKEN,)
        scratch = []
    scratch = scratch + [
        pltpu.VMEM((KV, PACK), jnp.bfloat16),
        pltpu.VMEM((KV, ROWS), jnp.bfloat16),
        pltpu.SemaphoreType.DMA(()),
    ]
    packed = sum([list(pair) for pair in packs], [])
    rows = [pltpu.with_memory_space_constraint(piece, pltpu.HBM) for pieces in sources for piece in pieces]
    former = [] if first else [part for state in states for part in state]

    def body(*refs):
        attend_kernel(base, parts, (groups, len(packs)), first, last, *refs)

    in_specs = [smem()] + [vmem()] * (2 + groups + len(packed))
    in_specs = in_specs + [pl.BlockSpec(memory_space=pl.ANY)] * len(rows) + [vmem()] * len(former)
    outs = pl.pallas_call(
        body,
        out_shape=out_shape,
        in_specs=in_specs,
        out_specs=(vmem(),) * len(out_shape),
        scratch_shapes=scratch,
        compiler_params=pltpu.CompilerParams(vmem_limit_bytes=16 << 20),
        cost_estimate=CHEAP,
        name="attend_%d_%d" % (len(parts), groups),
    )(counts, masks, positions, *queries, *packed, *rows, *former)
    if last:
        return list(outs)
    return [tuple(outs[2 * group : 2 * group + 2]) for group in range(groups)], outs[-1]


def combined(refs):
    row = lax.broadcasted_iota(jnp.int32, (STAT, 2 * STAT), 0)
    col = lax.broadcasted_iota(jnp.int32, (STAT, 2 * STAT), 1)
    spread = jnp.where((row // 3) == (col // STAT), 1.0, 0.0).astype(jnp.bfloat16)
    stats = [jnp.dot(ref[:, LAT:], spread, preferred_element_type=jnp.float32) for ref in refs]
    highest = stats[0][:, :STAT]
    for stat in stats[1:]:
        highest = jnp.maximum(highest, stat[:, :STAT])
    total, acc = None, None
    for ref, stat in zip(refs, stats):
        weight = jnp.exp2(stat[:, :STAT] - highest)
        wide = jnp.concatenate([weight] * (LAT // STAT), axis=1) * ref[:, :LAT].astype(jnp.float32)
        total = weight * stat[:, STAT:] if total is None else total + weight * stat[:, STAT:]
        acc = wide if acc is None else acc + wide
    return highest, total, acc


def combine_kernel(*refs):
    highest, total, acc = combined(refs[:4])
    for part, out_ref in enumerate(refs[4:]):
        here = slice(part * PAIRS * HEADS, (part + 1) * PAIRS * HEADS)
        write_payload(out_ref, highest[here, :1], total[here, :1], acc[here, :])


def combine(parts):
    return pl.pallas_call(
        combine_kernel,
        out_shape=(jax.ShapeDtypeStruct((PAIRS * HEADS, LAT + STAT), jnp.bfloat16),) * 4,
        in_specs=[vmem()] * 4,
        out_specs=(vmem(),) * 4,
        compiler_params=pltpu.CompilerParams(vmem_limit_bytes=8 << 20),
        cost_estimate=CHEAP,
        name="combine",
    )(*parts)


def project_kernel(value_ref, weights, partial_ref, *refs):
    out_ref = refs[4]
    highest, total, acc = combined(refs[:4])
    attn = (acc / jnp.concatenate([total] * (LAT // STAT), axis=1)).astype(jnp.bfloat16)
    head_of = lax.broadcasted_iota(jnp.int32, (PAIRS, HEADS, 128), 1)
    pieces = []
    for head in range(HEADS):
        product = jnp.dot(attn, value_ref[head], preferred_element_type=jnp.float32)
        product = jnp.where(head_of == head, product.reshape(PAIRS, HEADS, 128), 0.0)
        pieces.append(jnp.sum(product, axis=1))
    values = jnp.concatenate(pieces, axis=1).astype(jnp.bfloat16)
    width = weights.shape[1]
    result = jnp.dot(values, weights[...], preferred_element_type=jnp.float32)
    out_ref[:, :width] = result.astype(jnp.bfloat16)
    lane = lax.broadcasted_iota(jnp.int32, (PAIRS, STAT), 1)
    group = lax.axis_index("pre")
    mine = jnp.sum(jnp.where(lane == group, partial_ref[...], 0.0), axis=1, keepdims=True)
    out_ref[:, width:] = split_three(mine, lane, 0).astype(jnp.bfloat16)


def project(received, value_proj, out_proj, partial):
    return pl.pallas_call(
        project_kernel,
        out_shape=jax.ShapeDtypeStruct((PAIRS, out_proj.shape[1] + STAT), jnp.bfloat16),
        in_specs=[vmem()] * 7,
        out_specs=vmem(),
        compiler_params=pltpu.CompilerParams(vmem_limit_bytes=16 << 20),
        cost_estimate=CHEAP,
        name="project",
    )(value_proj, pltpu.with_memory_space_constraint(out_proj, pltpu.VMEM), partial, *received)


def index_kernel(*refs):
    place = lax.axis_index("pre")
    slabs, key_refs, out_ref = refs[:4], refs[4:6], refs[7]
    gates = jnp.concatenate([ref[PAIRS * 64 :, :] for ref in slabs], axis=0)
    gates = jnp.concatenate([gates, jnp.zeros_like(gates)], axis=0).astype(jnp.float32).T
    lane = lax.broadcasted_iota(jnp.int32, (PAIRS, 128), 1)
    result = jnp.zeros((PAIRS, 128), jnp.float32)
    for step, ref in enumerate(slabs):
        group = (((place >> 1) + step) & 3) * 2 + (place & 1)
        sums = []
        for keys in key_refs:
            scores = []
            for part in range(4):
                logits = lax.dot_general(
                    ref[part * 128 : (part + 1) * 128, :], keys[...], NT, preferred_element_type=jnp.float32
                )
                column = step * 16 + part
                gated = jnp.maximum(logits, 0.0) * gates[:, column : column + 1]
                scores.append(jnp.sum(gated.reshape(2, 64, ROWS), axis=1))
            scores = jnp.concatenate(scores, axis=0) * IDX ** (-0.5)
            largest = jnp.max(scores, axis=1, keepdims=True)
            sums.append(largest + jnp.log(jnp.sum(jnp.exp(scores - largest), axis=1, keepdims=True)))
        result = jnp.where(lane == group, log_add(sums[0], sums[1]), result)
    out_ref[...] = result


def index_partial(slabs, keys, payload):
    return pl.pallas_call(
        index_kernel,
        out_shape=jax.ShapeDtypeStruct((PAIRS, 128), jnp.float32),
        in_specs=[vmem()] * 6 + [pl.BlockSpec(memory_space=pl.ANY)],
        out_specs=vmem(),
        compiler_params=pltpu.CompilerParams(vmem_limit_bytes=16 << 20),
        cost_estimate=CHEAP,
        name="index_partial",
    )(*slabs, *keys, payload)


def log_add(one, two):
    top = jnp.maximum(one, two)
    return top + jnp.log(jnp.exp(one - top) + jnp.exp(two - top))


def split_three(value, lane, start):
    pieces = jnp.zeros(lane.shape, jnp.float32)
    for step in range(3):
        piece = value.astype(jnp.bfloat16).astype(jnp.float32)
        pieces = jnp.where(lane == start + step, piece, pieces)
        value = value - piece
    return pieces


def join_three(pieces, start):
    wide = pieces.astype(jnp.float32)
    return wide[:, start : start + 1] + wide[:, start + 1 : start + 2] + wide[:, start + 2 : start + 3]


def four_sum(refs):
    width = refs[0].shape[1] - STAT
    parts = [ref[:, :width].astype(jnp.float32) for ref in refs]
    logs = [join_three(ref[:, width:], 0) for ref in refs]
    return (parts[0] + parts[1]) + (parts[2] + parts[3]), log_add(log_add(logs[0], logs[1]), log_add(logs[2], logs[3]))


def middle_kernel(own_ref, far_ref, right_ref, left_ref, out_ref):
    summed, logs = four_sum((own_ref, far_ref, right_ref, left_ref))
    width = summed.shape[1]
    out_ref[:, :width] = summed.astype(jnp.bfloat16)
    lane = lax.broadcasted_iota(jnp.int32, (PAIRS, STAT), 1)
    out_ref[:, width:] = split_three(logs, lane, 0).astype(jnp.bfloat16)


def final_kernel(own_ref, far_ref, right_ref, left_ref, out_ref, log_ref):
    summed, logs = four_sum((own_ref, far_ref, right_ref, left_ref))
    steps, local = log_ref.shape
    flat = jnp.broadcast_to(logs, (PAIRS, STAT)).T[:1, :]
    for step in range(steps):
        out_ref[step] = summed[step * local : (step + 1) * local, :].astype(jnp.bfloat16)
        log_ref[step : step + 1, :] = flat[:, step * local : (step + 1) * local]


def summed_over(value, shift, final):
    parts = (value,) + tuple(lax.ppermute(value, BOTH, shift(step)) for step in (2, 1, 3))
    if final:
        out_shape = (
            jax.ShapeDtypeStruct(final + (value.shape[1] - STAT,), jnp.bfloat16),
            jax.ShapeDtypeStruct(final, jnp.float32),
        )
        out_specs = (vmem(), vmem())
    else:
        out_shape = jax.ShapeDtypeStruct(value.shape, jnp.bfloat16)
        out_specs = vmem()
    return pl.pallas_call(
        final_kernel if final else middle_kernel,
        out_shape=out_shape,
        in_specs=[vmem()] * 4,
        out_specs=out_specs,
        compiler_params=pltpu.CompilerParams(vmem_limit_bytes=4 << 20),
        cost_estimate=CHEAP,
        name="sum_last" if final else "sum_first",
    )(*parts)


def prepare_kernel(latent_ref, block_ref):
    block_ref[...] = latent_ref[...].astype(jnp.bfloat16)


def prepare(latent):
    spec = pl.BlockSpec((KV // PARTS, ROWS), lambda part: (part, 0))
    return pl.pallas_call(
        prepare_kernel,
        grid=(PARTS,),
        out_shape=jax.ShapeDtypeStruct(latent.shape, jnp.bfloat16),
        in_specs=[spec],
        out_specs=spec,
        compiler_params=pltpu.CompilerParams(vmem_limit_bytes=8 << 20),
        cost_estimate=CHEAP,
        name="prepare",
    )(pltpu.with_memory_space_constraint(latent, pltpu.HBM))


def x_shift(step):
    return [(x * 2 + c, ((x + step) % 4) * 2 + c) for x in range(4) for c in range(2)]


BOTH = ("pre", "tp")


def plane_shift(step, along_y):
    pairs = []
    for p in range(PRE):
        for z in range(4):
            for y in range(4):
                to_y = along_y == (p % 2 == 0)
                there = z * 4 + (y + step) % 4 if to_y else ((z + step) % 4) * 4 + y
                pairs.append((p * TP + z * 4 + y, p * TP + there))
    return pairs


def first_shift(step):
    return plane_shift(step, True)


def second_shift(step):
    return plane_shift(step, False)


CORE_SWAP = [(i, i ^ 1) for i in range(PRE)]


def on_device(
    latent_rows,
    index_keys,
    queries,
    index_queries,
    index_gates,
    value_proj,
    out_proj,
    block_rows,
    block_owner,
    block_count,
):
    block = prepare(latent_rows.T)
    forward = lax.ppermute(block, "pre", x_shift(1))
    backward = lax.ppermute(block, "pre", x_shift(3))

    own_queries = queries.reshape(PAIRS * HEADS, KV)
    row = jnp.concatenate(
        [own_queries] + [lax.ppermute(own_queries, BOTH, first_shift(4 - step)) for step in (1, 2, 3)], axis=0
    )
    plane = [row] + [lax.ppermute(row, BOTH, second_shift(4 - step)) for step in (1, 2, 3)]

    def swapped(part):
        return lax.ppermute(part, "pre", CORE_SWAP)

    def both(parts):
        return [list(parts), [swapped(part) for part in parts]]

    masks, positions, counts = make_tables(block_rows, block_owner, block_count)
    piece, keys = index_piece(index_queries, index_gates, index_keys)

    token = arrived(plane[1:] + [masks, keys])
    forward, backward, block, keys, token = lax.optimization_barrier((forward, backward, block, keys, token))
    top, low = halves(forward, backward)
    far = [lax.ppermute(top, "pre", x_shift(1)), lax.ppermute(low, "pre", x_shift(3))]

    own, sides = both([block]), both([forward]) + both([backward])
    packs = [
        pack(base, token, masks, positions, rows) for base, rows in ((0, sides[:2]), (2, own), (4, sides[2:]))
    ]
    keys = [keys, swapped(keys)]
    states, token = attend(0, counts, plane, masks, positions, packs, sides[:2] + own + sides[2:])
    far, token = lax.optimization_barrier((far, token))
    far = both(far)
    packs = [pack(6, token, masks, positions, far)]

    piece, absent = lax.optimization_barrier((piece, packs[0][1]))
    packs = [(packs[0][0], absent)]
    slabs = [piece] + [lax.ppermute(piece, "pre", x_shift(4 - step)) for step in (1, 2, 3)]

    payloads = attend(6, counts, plane[1:], masks, positions, packs, far, states[1:], last=True)
    payload = attend(6, counts, plane[:1], masks, positions, packs, far, states[:1], last=True)
    parts = payload + [lax.ppermute(payloads[step - 1], BOTH, second_shift(step)) for step in (1, 2, 3)]
    parts = combine(parts)
    received = [parts[0]] + [lax.ppermute(parts[step], BOTH, first_shift(step)) for step in (1, 2, 3)]
    partial = index_partial(slabs, keys, payloads[0])
    parts = [lax.ppermute(partial, "pre", x_shift(step)) for step in (2, 1, 3)]
    partial = log_add(log_add(partial, parts[0]), log_add(parts[1], parts[2]))
    part_out = project(received, value_proj, out_proj, partial)
    return summed_over(summed_over(part_out, first_shift, None), second_shift, queries.shape[:2])


def solution(mesh):
    placed = (
        P(("pre", "tp"), None),
        P(("pre", "tp"), None),
        P(None, "pre", "tp", None),
        P(None, "pre", None, None),
        P(None, "pre", None),
        P("tp", None, None),
        P("tp", None),
        P(None, "pre", None, None),
        P(None, "pre", None),
        P(None, "pre", None),
    )
    return jax.shard_map(
        on_device,
        mesh=mesh,
        in_specs=placed,
        out_specs=(P(None, "pre", None), P(None, "pre")),
        check_vma=False,
    )
```

```python
import jax
import jax.numpy as jnp
from jax import lax
from jax.experimental import pallas as pl
from jax.experimental.pallas import tpu as pltpu
from jax.sharding import PartitionSpec as P

IDX = 128
LAT = 512
KV = 576
BLOCK = 64
PRE = 8
TP = 16
PAIRS = 8
HEADS = 8
ROWS = 1024
PACK = 256
QTILE = 256
PARTS = 4
STAT = 128
QROWS = TP * PAIRS * HEADS
LOWEST = -3.0e38
SOFT_SCALE = 192.0 ** (-0.5)
LOG2E = 1.4426950408889634
SCORE_SCALE = SOFT_SCALE * LOG2E

NT = (((1,), (1,)), ((), ()))


CHEAP = pl.CostEstimate(flops=1000, bytes_accessed=1000, transcendentals=0)


def vmem():
    return pl.BlockSpec(memory_space=pltpu.VMEM)


def smem():
    return pl.BlockSpec(memory_space=pltpu.SMEM)


def table_kernel(rows_ref, owner_ref, count_ref, mask_ref, pos_ref, total_ref):
    me_pre = lax.axis_index("pre")
    me_tp = lax.axis_index("tp")
    number = rows_ref.shape[2]
    before = (
        lax.broadcasted_iota(jnp.int32, (number, number), 0) < lax.broadcasted_iota(jnp.int32, (number, number), 1)
    ).astype(jnp.float32).astype(jnp.bfloat16)
    slot = lax.broadcasted_iota(jnp.int32, (8, number), 0).astype(jnp.float32)
    entry = lax.broadcasted_iota(jnp.int32, (8, BLOCK), 1).astype(jnp.float32)
    high_iota = lax.broadcasted_iota(jnp.int32, (PRE * 8, BLOCK), 0).astype(jnp.float32)
    low_iota = lax.broadcasted_iota(jnp.int32, (128, BLOCK), 0).astype(jnp.float32)
    for pair in range(PAIRS):
        step, local = pair // rows_ref.shape[1], pair % rows_ref.shape[1]
        rows = rows_ref[step, local]
        source = rows >> 10
        relative = ((((source >> 1) - (me_pre >> 1) + 1) & 3) << 1) | ((source ^ me_pre) & 1)
        high = ((relative << 3) | ((rows >> 7) & 7)).astype(jnp.float32).astype(jnp.bfloat16)
        low = (rows & 127).astype(jnp.float32).astype(jnp.bfloat16)
        owned = jnp.where(owner_ref[step, local : local + 1, :] == me_tp, 1.0, 0.0)
        rank = jnp.dot(owned.astype(jnp.bfloat16), before, preferred_element_type=jnp.float32)
        choose = jnp.where(slot == rank, owned, 0.0)
        limit = jnp.sum(choose * count_ref[step, local : local + 1, :].astype(jnp.float32), axis=1, keepdims=True)
        choose = choose.astype(jnp.bfloat16)
        valid = entry < limit
        high = jnp.where(valid, jnp.dot(choose, high, preferred_element_type=jnp.float32), -1.0)
        low = jnp.dot(choose, low, preferred_element_type=jnp.float32)
        chosen = jnp.zeros((PRE * 8, 128), jnp.float32)
        for block in range(number // TP):
            high_one = jnp.where(high_iota == high[block : block + 1, :], 1.0, 0.0).astype(jnp.bfloat16)
            low_one = jnp.where(low_iota == low[block : block + 1, :], 1.0, 0.0).astype(jnp.bfloat16)
            chosen = chosen + lax.dot_general(high_one, low_one, NT, preferred_element_type=jnp.float32)
        for block in range(PRE):
            for part in range(8):
                mask_ref[block, pair : pair + 1, part * 128 : (part + 1) * 128] = chosen[
                    block * 8 + part : block * 8 + part + 1, :
                ]
    union = jnp.concatenate([jnp.max(mask_ref[block], axis=0, keepdims=True) for block in range(PRE)], axis=0)
    before = (
        lax.broadcasted_iota(jnp.int32, (128, 128), 0) < lax.broadcasted_iota(jnp.int32, (128, 128), 1)
    ).astype(jnp.float32).astype(jnp.bfloat16)
    carry = jnp.zeros((PRE, 1), jnp.float32)
    for part in range(8):
        piece = union[:, part * 128 : (part + 1) * 128]
        ahead = jnp.dot(piece.astype(jnp.bfloat16), before, preferred_element_type=jnp.float32) + carry
        pos_ref[:, part * 128 : (part + 1) * 128] = jnp.where(piece > 0.0, ahead, -1.0)
        carry = carry + jnp.sum(piece, axis=1, keepdims=True)
    total_ref[...] = jnp.broadcast_to(carry, (PRE, 128)).astype(jnp.int32)


def make_tables(block_rows, block_owner, block_count):
    return pl.pallas_call(
        table_kernel,
        out_shape=(
            jax.ShapeDtypeStruct((PRE, PAIRS, ROWS), jnp.float32),
            jax.ShapeDtypeStruct((PRE, ROWS), jnp.float32),
            jax.ShapeDtypeStruct((PRE, 128), jnp.int32),
        ),
        in_specs=[vmem()] * 3,
        out_specs=(vmem(), vmem(), vmem()),
        compiler_params=pltpu.CompilerParams(vmem_limit_bytes=8 << 20),
        cost_estimate=CHEAP,
        name="row_tables",
    )(block_rows, block_owner, block_count)


def piece_kernel(query_ref, gate_ref, key_ref, out_ref, key_out_ref):
    pairs = [(step, local) for step in range(query_ref.shape[0]) for local in range(query_ref.shape[1])]
    heads = query_ref.shape[2]
    for pair, (step, local) in enumerate(pairs):
        out_ref[pair * heads : (pair + 1) * heads, :] = query_ref[step, local]
    gates = [gate_ref[step, local : local + 1, :].astype(jnp.float32) for step, local in pairs]
    lines = [jnp.concatenate(gates[2 * line : 2 * line + 2], axis=1) for line in range(4)]
    lines = jnp.concatenate(lines + [jnp.zeros((12, IDX), jnp.float32)], axis=0)
    out_ref[PAIRS * heads :, :] = lines.astype(jnp.bfloat16)
    key_out_ref[...] = key_ref[...].astype(jnp.bfloat16)


def index_piece(index_queries, index_gates, index_keys):
    return pl.pallas_call(
        piece_kernel,
        out_shape=(
            jax.ShapeDtypeStruct((PAIRS * index_queries.shape[2] + 16, IDX), jnp.bfloat16),
            jax.ShapeDtypeStruct(index_keys.shape, jnp.bfloat16),
        ),
        in_specs=[vmem()] * 3,
        out_specs=(vmem(),) * 2,
        compiler_params=pltpu.CompilerParams(vmem_limit_bytes=4 << 20),
        cost_estimate=CHEAP,
        name="index_piece",
    )(index_queries, index_gates, index_keys)


TOKEN = jax.ShapeDtypeStruct((8, 128), jnp.float32)


def token_kernel(*refs):
    refs[-1][...] = jnp.zeros(refs[-1].shape, jnp.float32)


def arrived(values):
    return pl.pallas_call(
        token_kernel,
        out_shape=TOKEN,
        in_specs=[pl.BlockSpec(memory_space=pl.ANY)] * len(values),
        out_specs=vmem(),
        compiler_params=pltpu.CompilerParams(vmem_limit_bytes=2 << 20),
        cost_estimate=CHEAP,
        name="arrived",
    )(*values)


def halves_kernel(forward_ref, backward_ref, top_ref, low_ref):
    top_ref[...] = forward_ref[...]
    low_ref[...] = backward_ref[...]


def halves(forward, backward):
    half = (forward.shape[0] // 2, forward.shape[1])
    out = jax.ShapeDtypeStruct(half, forward.dtype)
    return pl.pallas_call(
        halves_kernel,
        grid=(1,),
        out_shape=(out, out),
        in_specs=[pl.BlockSpec(half, lambda part: (0, 0)), pl.BlockSpec(half, lambda part: (1, 0))],
        out_specs=(pl.BlockSpec(half, lambda part: (0, 0)),) * 2,
        compiler_params=pltpu.CompilerParams(vmem_limit_bytes=8 << 20),
        cost_estimate=CHEAP,
        name="halves",
    )(forward, backward)


def pack_block(number, pieces, mask_row, pos_row, packed_ref, first_lane):
    slot = (lax.broadcasted_iota(jnp.int32, (PACK, ROWS), 0) + number * PACK).astype(jnp.float32)
    pick = jnp.where(slot == pos_row, 1.0, 0.0).astype(jnp.bfloat16)
    depth = KV // len(pieces)
    for order, piece in enumerate(pieces):
        packed = lax.dot_general(piece[...], pick, NT, preferred_element_type=jnp.float32)
        packed_ref[order * depth : (order + 1) * depth, first_lane : first_lane + PACK] = packed.astype(jnp.bfloat16)
    present = lax.dot_general(mask_row.astype(jnp.bfloat16), pick, NT, preferred_element_type=jnp.float32)
    return jnp.where(present > 0.5, 0.0, -jnp.inf)


def pack_kernel(base, parts, unused_ref, mask_ref, pos_ref, *refs):
    packed_ref, absent_ref = refs[-2:]
    for block, number in enumerate(parts):
        pieces, refs = refs[:number], refs[number:]
        row = base + block
        absent_ref[:, block * PACK : (block + 1) * PACK] = pack_block(
            0, pieces, mask_ref[row], pos_ref[row : row + 1, :], packed_ref, block * PACK
        )


def pack(base, token, masks, positions, sources):
    parts = [len(pieces) for pieces in sources]
    rows = sum([list(pieces) for pieces in sources], [])

    def body(*refs):
        pack_kernel(base, parts, *refs)

    return pl.pallas_call(
        body,
        out_shape=(
            jax.ShapeDtypeStruct((KV, len(parts) * PACK), jnp.bfloat16),
            jax.ShapeDtypeStruct((PAIRS, len(parts) * PACK), jnp.float32),
        ),
        in_specs=[pl.BlockSpec(memory_space=pl.ANY)] + [vmem()] * (2 + len(rows)),
        out_specs=(vmem(), vmem()),
        compiler_params=pltpu.CompilerParams(vmem_limit_bytes=16 << 20),
        cost_estimate=CHEAP,
        name="pack_%d" % len(parts),
    )(token, masks, positions, *rows)


def attend_kernel(base, parts, shapes, first, last, count_ref, mask_ref, pos_ref, *refs):
    queries, refs = refs[: shapes[0]], refs[shapes[0] :]
    packs, refs = refs[: 2 * shapes[1]], refs[2 * shapes[1] :]
    sources = []
    for number in parts:
        sources.append(refs[:number])
        refs = refs[number:]
    groups = len(queries)
    if not first:
        former_state, refs = refs[: 2 * groups], refs[2 * groups :]
    if last:
        outs, refs = refs[:groups], refs[groups:]
    state, refs = refs[: 2 * groups], refs[2 * groups :]
    if not last:
        refs[0][...] = jnp.zeros(refs[0].shape, jnp.float32)
        refs = refs[1:]
    packed_ref, rows_ref, sem = refs
    column = lax.broadcasted_iota(jnp.int32, (QTILE, STAT), 1)

    def attention(packed, absent, fresh):
        span = absent.shape[1]
        for group in range(groups):
            stat_ref, acc_ref = state[2 * group], state[2 * group + 1]
            query = queries[group][...]
            scores = [jnp.dot(query, ref[...], preferred_element_type=jnp.float32) for ref in packed]
            scores = scores[0] if len(scores) == 1 else jnp.concatenate(scores, axis=1)
            scores = scores.reshape(QTILE // 64, PAIRS, HEADS, span) * SCORE_SCALE + absent[None, :, None, :]
            scores = scores.reshape(QTILE, span)
            newer = jnp.max(scores, axis=1, keepdims=True)
            if fresh and first:
                newer = jnp.maximum(newer, LOWEST)
            else:
                stats, acc = (former_state[2 * group], former_state[2 * group + 1]) if fresh else (stat_ref, acc_ref)
                former = stats[:, :1]
                newer = jnp.maximum(former, newer)
                decay = jnp.exp2(former - newer)
            weights = jnp.exp2(scores - newer)
            total = jnp.sum(weights, axis=1, keepdims=True)
            weights = weights.astype(jnp.bfloat16)
            added, start = None, 0
            for ref in packed:
                width = ref.shape[1]
                piece = lax.dot_general(
                    weights[:, start : start + width], ref[:LAT, :], NT, preferred_element_type=jnp.float32
                )
                added = piece if added is None else added + piece
                start += width
            if not (fresh and first):
                total = stats[:, STAT // 2 : STAT // 2 + 1] * decay + total
                added = acc[...] * decay + added
            acc_ref[...] = added
            stat_ref[...] = jnp.where(column < STAT // 2, newer, total)

    attention(packs[::2], jnp.concatenate([ref[...] for ref in packs[1::2]], axis=1), True)

    for block in range(len(parts)):
        row = base + block
        rounds = (count_ref[row, 0] + (PACK - 1)) // PACK

        @pl.when(rounds > 1)
        def _(block=block, row=row, rounds=rounds):
            depth = KV // len(sources[block])
            for order, piece in enumerate(sources[block]):
                copy = pltpu.make_async_copy(piece, rows_ref.at[pl.ds(order * depth, depth), :], sem)
                copy.start()
                copy.wait()

            @pl.loop(1, rounds)
            def _(number):
                absent = pack_block(
                    number, [rows_ref], mask_ref[row], pos_ref[row : row + 1, :], packed_ref, 0
                )
                attention([packed_ref], absent, False)

    if last:
        for group in range(groups):
            stat_ref, acc_ref = state[2 * group], state[2 * group + 1]
            write_payload(outs[group], stat_ref[:, :1], stat_ref[:, STAT // 2 : STAT // 2 + 1], acc_ref[...])


def write_payload(out_ref, highest, total, acc):
    lane = lax.broadcasted_iota(jnp.int32, (acc.shape[0], STAT), 1)
    out_ref[:, :LAT] = acc.astype(jnp.bfloat16)
    out_ref[:, LAT:] = (split_three(highest, lane, 0) + split_three(total, lane, 3)).astype(jnp.bfloat16)


def attend(base, counts, queries, masks, positions, packs, sources, states=None, last=False):
    parts = [len(pieces) for pieces in sources]
    first = states is None
    groups = len(queries)
    shapes = (
        jax.ShapeDtypeStruct((QTILE, STAT), jnp.float32),
        jax.ShapeDtypeStruct((QTILE, LAT), jnp.float32),
    ) * groups
    if last:
        out_shape = (jax.ShapeDtypeStruct((QTILE, LAT + STAT), jnp.bfloat16),) * groups
        scratch = [pltpu.VMEM(s.shape, s.dtype) for s in shapes]
    else:
        out_shape = shapes + (TOKEN,)
        scratch = []
    scratch = scratch + [
        pltpu.VMEM((KV, PACK), jnp.bfloat16),
        pltpu.VMEM((KV, ROWS), jnp.bfloat16),
        pltpu.SemaphoreType.DMA(()),
    ]
    packed = sum([list(pair) for pair in packs], [])
    rows = [pltpu.with_memory_space_constraint(piece, pltpu.HBM) for pieces in sources for piece in pieces]
    former = [] if first else [part for state in states for part in state]

    def body(*refs):
        attend_kernel(base, parts, (groups, len(packs)), first, last, *refs)

    in_specs = [smem()] + [vmem()] * (2 + groups + len(packed))
    in_specs = in_specs + [pl.BlockSpec(memory_space=pl.ANY)] * len(rows) + [vmem()] * len(former)
    outs = pl.pallas_call(
        body,
        out_shape=out_shape,
        in_specs=in_specs,
        out_specs=(vmem(),) * len(out_shape),
        scratch_shapes=scratch,
        compiler_params=pltpu.CompilerParams(vmem_limit_bytes=16 << 20),
        cost_estimate=CHEAP,
        name="attend_%d_%d" % (len(parts), groups),
    )(counts, masks, positions, *queries, *packed, *rows, *former)
    if last:
        return list(outs)
    return [tuple(outs[2 * group : 2 * group + 2]) for group in range(groups)], outs[-1]


def combined(refs):
    row = lax.broadcasted_iota(jnp.int32, (STAT, 2 * STAT), 0)
    col = lax.broadcasted_iota(jnp.int32, (STAT, 2 * STAT), 1)
    spread = jnp.where((row // 3) == (col // STAT), 1.0, 0.0).astype(jnp.bfloat16)
    stats = [jnp.dot(ref[:, LAT:], spread, preferred_element_type=jnp.float32) for ref in refs]
    highest = stats[0][:, :STAT]
    for stat in stats[1:]:
        highest = jnp.maximum(highest, stat[:, :STAT])
    total, acc = None, None
    for ref, stat in zip(refs, stats):
        weight = jnp.exp2(stat[:, :STAT] - highest)
        wide = jnp.concatenate([weight] * (LAT // STAT), axis=1) * ref[:, :LAT].astype(jnp.float32)
        total = weight * stat[:, STAT:] if total is None else total + weight * stat[:, STAT:]
        acc = wide if acc is None else acc + wide
    return highest, total, acc


def combine_kernel(*refs):
    highest, total, acc = combined(refs[:4])
    for part, out_ref in enumerate(refs[4:]):
        here = slice(part * PAIRS * HEADS, (part + 1) * PAIRS * HEADS)
        write_payload(out_ref, highest[here, :1], total[here, :1], acc[here, :])


def combine(parts):
    return pl.pallas_call(
        combine_kernel,
        out_shape=(jax.ShapeDtypeStruct((PAIRS * HEADS, LAT + STAT), jnp.bfloat16),) * 4,
        in_specs=[vmem()] * 4,
        out_specs=(vmem(),) * 4,
        compiler_params=pltpu.CompilerParams(vmem_limit_bytes=8 << 20),
        cost_estimate=CHEAP,
        name="combine",
    )(*parts)


def project_kernel(value_ref, weights, partial_ref, *refs):
    out_ref = refs[4]
    highest, total, acc = combined(refs[:4])
    attn = (acc / jnp.concatenate([total] * (LAT // STAT), axis=1)).astype(jnp.bfloat16)
    head_of = lax.broadcasted_iota(jnp.int32, (PAIRS, HEADS, 128), 1)
    pieces = []
    for head in range(HEADS):
        product = jnp.dot(attn, value_ref[head], preferred_element_type=jnp.float32)
        product = jnp.where(head_of == head, product.reshape(PAIRS, HEADS, 128), 0.0)
        pieces.append(jnp.sum(product, axis=1))
    values = jnp.concatenate(pieces, axis=1).astype(jnp.bfloat16)
    width = weights.shape[1]
    result = jnp.dot(values, weights[...], preferred_element_type=jnp.float32)
    out_ref[:, :width] = result.astype(jnp.bfloat16)
    lane = lax.broadcasted_iota(jnp.int32, (PAIRS, STAT), 1)
    group = lax.axis_index("pre")
    mine = jnp.sum(jnp.where(lane == group, partial_ref[...], 0.0), axis=1, keepdims=True)
    out_ref[:, width:] = split_three(mine, lane, 0).astype(jnp.bfloat16)


def project(received, value_proj, out_proj, partial):
    return pl.pallas_call(
        project_kernel,
        out_shape=jax.ShapeDtypeStruct((PAIRS, out_proj.shape[1] + STAT), jnp.bfloat16),
        in_specs=[vmem()] * 7,
        out_specs=vmem(),
        compiler_params=pltpu.CompilerParams(vmem_limit_bytes=16 << 20),
        cost_estimate=CHEAP,
        name="project",
    )(value_proj, pltpu.with_memory_space_constraint(out_proj, pltpu.VMEM), partial, *received)


def index_kernel(slab_ref, first_keys, second_keys, unused_ref, out_ref):
    place = lax.axis_index("pre")
    core = place & 1
    gates = jnp.concatenate([slab_ref[chip * 2 + core, PAIRS * 64 :, :] for chip in range(4)], axis=0)
    gates = jnp.concatenate([gates, jnp.zeros_like(gates)], axis=0).astype(jnp.float32).T
    lane = lax.broadcasted_iota(jnp.int32, (PAIRS, 128), 1)
    result = jnp.zeros((PAIRS, 128), jnp.float32)
    for chip in range(4):
        group = chip * 2 + core
        sums = []
        for keys in (first_keys, second_keys):
            scores = []
            for part in range(4):
                logits = lax.dot_general(
                    slab_ref[group, part * 128 : (part + 1) * 128, :], keys[...], NT, preferred_element_type=jnp.float32
                )
                column = chip * 16 + part
                gated = jnp.maximum(logits, 0.0) * gates[:, column : column + 1]
                scores.append(jnp.sum(gated.reshape(2, 64, ROWS), axis=1))
            scores = jnp.concatenate(scores, axis=0) * IDX ** (-0.5)
            largest = jnp.max(scores, axis=1, keepdims=True)
            sums.append(largest + jnp.log(jnp.sum(jnp.exp(scores - largest), axis=1, keepdims=True)))
        result = jnp.where(lane == group, log_add(sums[0], sums[1]), result)
    out_ref[...] = result


def index_partial(slabs, keys, payload):
    return pl.pallas_call(
        index_kernel,
        out_shape=jax.ShapeDtypeStruct((PAIRS, 128), jnp.float32),
        in_specs=[vmem()] * 3 + [pl.BlockSpec(memory_space=pl.ANY)],
        out_specs=vmem(),
        compiler_params=pltpu.CompilerParams(vmem_limit_bytes=16 << 20),
        cost_estimate=CHEAP,
        name="index_partial",
    )(slabs, *keys, payload)


def log_add(one, two):
    top = jnp.maximum(one, two)
    return top + jnp.log(jnp.exp(one - top) + jnp.exp(two - top))


def split_three(value, lane, start):
    pieces = jnp.zeros(lane.shape, jnp.float32)
    for step in range(3):
        piece = value.astype(jnp.bfloat16).astype(jnp.float32)
        pieces = jnp.where(lane == start + step, piece, pieces)
        value = value - piece
    return pieces


def join_three(pieces, start):
    wide = pieces.astype(jnp.float32)
    return wide[:, start : start + 1] + wide[:, start + 1 : start + 2] + wide[:, start + 2 : start + 3]


def four_sum(refs):
    width = refs[0].shape[1] - STAT
    parts = [ref[:, :width].astype(jnp.float32) for ref in refs]
    logs = [join_three(ref[:, width:], 0) for ref in refs]
    return (parts[0] + parts[1]) + (parts[2] + parts[3]), log_add(log_add(logs[0], logs[1]), log_add(logs[2], logs[3]))


def middle_kernel(own_ref, far_ref, right_ref, left_ref, out_ref):
    summed, logs = four_sum((own_ref, far_ref, right_ref, left_ref))
    width = summed.shape[1]
    out_ref[:, :width] = summed.astype(jnp.bfloat16)
    lane = lax.broadcasted_iota(jnp.int32, (PAIRS, STAT), 1)
    out_ref[:, width:] = split_three(logs, lane, 0).astype(jnp.bfloat16)


def final_kernel(own_ref, far_ref, right_ref, left_ref, out_ref, log_ref):
    summed, logs = four_sum((own_ref, far_ref, right_ref, left_ref))
    steps, local = log_ref.shape
    flat = jnp.broadcast_to(logs, (PAIRS, STAT)).T[:1, :]
    for step in range(steps):
        out_ref[step] = summed[step * local : (step + 1) * local, :].astype(jnp.bfloat16)
        log_ref[step : step + 1, :] = flat[:, step * local : (step + 1) * local]


def summed_over(value, shift, final):
    parts = (value,) + tuple(lax.ppermute(value, BOTH, shift(step)) for step in (2, 1, 3))
    if final:
        out_shape = (
            jax.ShapeDtypeStruct(final + (value.shape[1] - STAT,), jnp.bfloat16),
            jax.ShapeDtypeStruct(final, jnp.float32),
        )
        out_specs = (vmem(), vmem())
    else:
        out_shape = jax.ShapeDtypeStruct(value.shape, jnp.bfloat16)
        out_specs = vmem()
    return pl.pallas_call(
        final_kernel if final else middle_kernel,
        out_shape=out_shape,
        in_specs=[vmem()] * 4,
        out_specs=out_specs,
        compiler_params=pltpu.CompilerParams(vmem_limit_bytes=4 << 20),
        cost_estimate=CHEAP,
        name="sum_last" if final else "sum_first",
    )(*parts)


def prepare_kernel(latent_ref, block_ref):
    block_ref[...] = latent_ref[...].astype(jnp.bfloat16)


def prepare(latent):
    spec = pl.BlockSpec((KV // PARTS, ROWS), lambda part: (part, 0))
    return pl.pallas_call(
        prepare_kernel,
        grid=(PARTS,),
        out_shape=jax.ShapeDtypeStruct(latent.shape, jnp.bfloat16),
        in_specs=[spec],
        out_specs=spec,
        compiler_params=pltpu.CompilerParams(vmem_limit_bytes=8 << 20),
        cost_estimate=CHEAP,
        name="prepare",
    )(pltpu.with_memory_space_constraint(latent, pltpu.HBM))


def x_shift(step):
    return [(x * 2 + c, ((x + step) % 4) * 2 + c) for x in range(4) for c in range(2)]


BOTH = ("pre", "tp")


def plane_shift(step, along_y):
    pairs = []
    for p in range(PRE):
        for z in range(4):
            for y in range(4):
                to_y = along_y == (p % 2 == 0)
                there = z * 4 + (y + step) % 4 if to_y else ((z + step) % 4) * 4 + y
                pairs.append((p * TP + z * 4 + y, p * TP + there))
    return pairs


def first_shift(step):
    return plane_shift(step, True)


def second_shift(step):
    return plane_shift(step, False)


CORE_SWAP = [(i, i ^ 1) for i in range(PRE)]


def on_device(
    latent_rows,
    index_keys,
    queries,
    index_queries,
    index_gates,
    value_proj,
    out_proj,
    block_rows,
    block_owner,
    block_count,
):
    block = prepare(latent_rows.T)
    forward = lax.ppermute(block, "pre", x_shift(1))
    backward = lax.ppermute(block, "pre", x_shift(3))

    own_queries = queries.reshape(PAIRS * HEADS, KV)
    row = jnp.concatenate(
        [own_queries] + [lax.ppermute(own_queries, BOTH, first_shift(4 - step)) for step in (1, 2, 3)], axis=0
    )
    plane = [row] + [lax.ppermute(row, BOTH, second_shift(4 - step)) for step in (1, 2, 3)]

    def swapped(part):
        return lax.ppermute(part, "pre", CORE_SWAP)

    def both(parts):
        return [list(parts), [swapped(part) for part in parts]]

    masks, positions, counts = make_tables(block_rows, block_owner, block_count)
    piece, keys = index_piece(index_queries, index_gates, index_keys)

    slabs = lax.all_gather(piece, "pre")

    token = arrived(plane[1:] + [masks, keys, slabs])
    forward, backward, block, keys, token = lax.optimization_barrier((forward, backward, block, keys, token))
    top, low = halves(forward, backward)
    far = [lax.ppermute(top, "pre", x_shift(1)), lax.ppermute(low, "pre", x_shift(3))]

    own, sides = both([block]), both([forward]) + both([backward])
    packs = [
        pack(base, token, masks, positions, rows) for base, rows in ((0, sides[:2]), (2, own), (4, sides[2:]))
    ]
    keys = [keys, swapped(keys)]
    states, token = attend(0, counts, plane, masks, positions, packs, sides[:2] + own + sides[2:])
    far, token = lax.optimization_barrier((far, token))
    partial = index_partial(slabs, keys, token)
    far = both(far)
    packs = [pack(6, partial, masks, positions, far)]

    payloads = attend(6, counts, plane[1:], masks, positions, packs, far, states[1:], last=True)
    payload = attend(6, counts, plane[:1], masks, positions, packs, far, states[:1], last=True)
    parts = payload + [lax.ppermute(payloads[step - 1], BOTH, second_shift(step)) for step in (1, 2, 3)]
    parts = combine(parts)
    received = [parts[0]] + [lax.ppermute(parts[step], BOTH, first_shift(step)) for step in (1, 2, 3)]
    parts = [lax.ppermute(partial, "pre", x_shift(step)) for step in (2, 1, 3)]
    partial = log_add(log_add(partial, parts[0]), log_add(parts[1], parts[2]))
    part_out = project(received, value_proj, out_proj, partial)
    return summed_over(summed_over(part_out, first_shift, None), second_shift, queries.shape[:2])


def solution(mesh):
    placed = (
        P(("pre", "tp"), None),
        P(("pre", "tp"), None),
        P(None, "pre", "tp", None),
        P(None, "pre", None, None),
        P(None, "pre", None),
        P("tp", None, None),
        P("tp", None),
        P(None, "pre", None, None),
        P(None, "pre", None),
        P(None, "pre", None),
    )
    return jax.shard_map(
        on_device,
        mesh=mesh,
        in_specs=placed,
        out_specs=(P(None, "pre", None), P(None, "pre")),
        check_vma=False,
    )
```

```python
import jax
import jax.numpy as jnp
from jax import lax
from jax.experimental import pallas as pl
from jax.experimental.pallas import tpu as pltpu
from jax.sharding import PartitionSpec as P

IDX = 128
LAT = 512
KV = 576
BLOCK = 64
PRE = 8
TP = 16
PAIRS = 8
HEADS = 8
ROWS = 1024
PACK = 256
MIDDLE = 96
WIDE = KV + MIDDLE
QTILE = 256
STAT = 128
QROWS = TP * PAIRS * HEADS
LOWEST = -3.0e38
SOFT_SCALE = 192.0 ** (-0.5)
LOG2E = 1.4426950408889634
SCORE_SCALE = SOFT_SCALE * LOG2E

NT = (((1,), (1,)), ((), ()))


CHEAP = pl.CostEstimate(flops=1000, bytes_accessed=1000, transcendentals=0)


def vmem():
    return pl.BlockSpec(memory_space=pltpu.VMEM)


def smem():
    return pl.BlockSpec(memory_space=pltpu.SMEM)


def table_kernel(rows_ref, owner_ref, count_ref, mask_ref, pos_ref, total_ref):
    me_pre = lax.axis_index("pre")
    me_tp = lax.axis_index("tp")
    number = rows_ref.shape[2]
    before = (
        lax.broadcasted_iota(jnp.int32, (number, number), 0) < lax.broadcasted_iota(jnp.int32, (number, number), 1)
    ).astype(jnp.float32).astype(jnp.bfloat16)
    slot = lax.broadcasted_iota(jnp.int32, (8, number), 0).astype(jnp.float32)
    entry = lax.broadcasted_iota(jnp.int32, (8, BLOCK), 1).astype(jnp.float32)
    high_iota = lax.broadcasted_iota(jnp.int32, (PRE * 8, BLOCK), 0).astype(jnp.float32)
    low_iota = lax.broadcasted_iota(jnp.int32, (128, BLOCK), 0).astype(jnp.float32)
    for pair in range(PAIRS):
        step, local = pair // rows_ref.shape[1], pair % rows_ref.shape[1]
        rows = rows_ref[step, local]
        source = rows >> 10
        relative = ((((source >> 1) - (me_pre >> 1) + 1) & 3) << 1) | ((source ^ me_pre) & 1)
        high = ((relative << 3) | ((rows >> 7) & 7)).astype(jnp.float32).astype(jnp.bfloat16)
        low = (rows & 127).astype(jnp.float32).astype(jnp.bfloat16)
        owned = jnp.where(owner_ref[step, local : local + 1, :] == me_tp, 1.0, 0.0)
        rank = jnp.dot(owned.astype(jnp.bfloat16), before, preferred_element_type=jnp.float32)
        choose = jnp.where(slot == rank, owned, 0.0)
        limit = jnp.sum(choose * count_ref[step, local : local + 1, :].astype(jnp.float32), axis=1, keepdims=True)
        choose = choose.astype(jnp.bfloat16)
        valid = entry < limit
        high = jnp.where(valid, jnp.dot(choose, high, preferred_element_type=jnp.float32), -1.0)
        low = jnp.dot(choose, low, preferred_element_type=jnp.float32)
        chosen = jnp.zeros((PRE * 8, 128), jnp.float32)
        for block in range(number // TP):
            high_one = jnp.where(high_iota == high[block : block + 1, :], 1.0, 0.0).astype(jnp.bfloat16)
            low_one = jnp.where(low_iota == low[block : block + 1, :], 1.0, 0.0).astype(jnp.bfloat16)
            chosen = chosen + lax.dot_general(high_one, low_one, NT, preferred_element_type=jnp.float32)
        for block in range(PRE):
            for part in range(8):
                mask_ref[block, pair : pair + 1, part * 128 : (part + 1) * 128] = chosen[
                    block * 8 + part : block * 8 + part + 1, :
                ]
    union = jnp.concatenate([jnp.max(mask_ref[block], axis=0, keepdims=True) for block in range(PRE)], axis=0)
    before = (
        lax.broadcasted_iota(jnp.int32, (128, 128), 0) < lax.broadcasted_iota(jnp.int32, (128, 128), 1)
    ).astype(jnp.float32).astype(jnp.bfloat16)
    carry = jnp.zeros((PRE, 1), jnp.float32)
    for part in range(8):
        piece = union[:, part * 128 : (part + 1) * 128]
        ahead = jnp.dot(piece.astype(jnp.bfloat16), before, preferred_element_type=jnp.float32) + carry
        pos_ref[:, part * 128 : (part + 1) * 128] = jnp.where(piece > 0.0, ahead, -1.0)
        carry = carry + jnp.sum(piece, axis=1, keepdims=True)
    total_ref[...] = jnp.broadcast_to(carry, (PRE, 128)).astype(jnp.int32)


def make_tables(block_rows, block_owner, block_count):
    return pl.pallas_call(
        table_kernel,
        out_shape=(
            jax.ShapeDtypeStruct((PRE, PAIRS, ROWS), jnp.float32),
            jax.ShapeDtypeStruct((PRE, ROWS), jnp.float32),
            jax.ShapeDtypeStruct((PRE, 128), jnp.int32),
        ),
        in_specs=[vmem()] * 3,
        out_specs=(vmem(), vmem(), vmem()),
        compiler_params=pltpu.CompilerParams(vmem_limit_bytes=8 << 20),
        cost_estimate=CHEAP,
        name="row_tables",
    )(block_rows, block_owner, block_count)


TOKEN = jax.ShapeDtypeStruct((8, 128), jnp.float32)


def token_kernel(*refs):
    refs[-1][...] = jnp.zeros(refs[-1].shape, jnp.float32)


def arrived(values):
    return pl.pallas_call(
        token_kernel,
        out_shape=TOKEN,
        in_specs=[pl.BlockSpec(memory_space=pl.ANY)] * len(values),
        out_specs=vmem(),
        compiler_params=pltpu.CompilerParams(vmem_limit_bytes=2 << 20),
        cost_estimate=CHEAP,
        name="arrived",
    )(*values)


def halves_kernel(forward_ref, backward_ref, top_ref, low_ref):
    top_ref[...] = forward_ref[...]
    low_ref[...] = backward_ref[...]


def halves(forward, backward):
    half = (forward.shape[0] // 2, forward.shape[1])
    out = jax.ShapeDtypeStruct(half, forward.dtype)
    return pl.pallas_call(
        halves_kernel,
        grid=(1,),
        out_shape=(out, out),
        in_specs=[pl.BlockSpec(half, lambda part: (0, 0)), pl.BlockSpec(half, lambda part: (1, 0))],
        out_specs=(pl.BlockSpec(half, lambda part: (0, 0)),) * 2,
        compiler_params=pltpu.CompilerParams(vmem_limit_bytes=8 << 20),
        cost_estimate=CHEAP,
        name="halves",
    )(forward, backward)


def pack_block(number, pieces, mask_row, pos_row, packed_ref, first_lane):
    slot = (lax.broadcasted_iota(jnp.int32, (PACK, ROWS), 0) + number * PACK).astype(jnp.float32)
    pick = jnp.where(slot == pos_row, 1.0, 0.0).astype(jnp.bfloat16)
    depth = KV // len(pieces)
    for order, piece in enumerate(pieces):
        packed = lax.dot_general(piece, pick, NT, preferred_element_type=jnp.float32)
        packed_ref[order * depth : (order + 1) * depth, first_lane : first_lane + PACK] = packed.astype(jnp.bfloat16)
    present = lax.dot_general(mask_row.astype(jnp.bfloat16), pick, NT, preferred_element_type=jnp.float32)
    return jnp.where(present > 0.5, 0.0, -jnp.inf)


def latent_parts(refs):
    half = KV // 2
    if len(refs) == 1:
        return [refs[0].at[pl.ds(0, half), :], refs[0].at[pl.ds(half + MIDDLE, half), :]]
    return [refs[0].at[pl.ds(0, half), :], refs[1].at[pl.ds(MIDDLE // 2, half), :]]


def pack_kernel(base, parts, unused_ref, mask_ref, pos_ref, *refs):
    packed_ref, absent_ref = refs[-2:]
    for block, number in enumerate(parts):
        pieces, refs = refs[:number], refs[number:]
        row = base + block
        absent_ref[:, block * PACK : (block + 1) * PACK] = pack_block(
            0, [part[...] for part in latent_parts(pieces)], mask_ref[row], pos_ref[row : row + 1, :], packed_ref,
            block * PACK,
        )


def pack(base, token, masks, positions, sources):
    parts = [len(pieces) for pieces in sources]
    rows = sum([list(pieces) for pieces in sources], [])

    def body(*refs):
        pack_kernel(base, parts, *refs)

    return pl.pallas_call(
        body,
        out_shape=(
            jax.ShapeDtypeStruct((KV, len(parts) * PACK), jnp.bfloat16),
            jax.ShapeDtypeStruct((PAIRS, len(parts) * PACK), jnp.float32),
        ),
        in_specs=[pl.BlockSpec(memory_space=pl.ANY)] + [vmem()] * (2 + len(rows)),
        out_specs=(vmem(), vmem()),
        compiler_params=pltpu.CompilerParams(vmem_limit_bytes=16 << 20),
        cost_estimate=CHEAP,
        name="pack_%d" % len(parts),
    )(token, masks, positions, *rows)


def attend_kernel(base, parts, shapes, first, last, count_ref, mask_ref, pos_ref, *refs):
    queries, refs = refs[: shapes[0]], refs[shapes[0] :]
    packs, refs = refs[: 2 * shapes[1]], refs[2 * shapes[1] :]
    sources = []
    for number in parts:
        sources.append(refs[:number])
        refs = refs[number:]
    groups = len(queries)
    if not first:
        former_state, refs = refs[: 2 * groups], refs[2 * groups :]
    if last:
        outs, refs = refs[:groups], refs[groups:]
    state, refs = refs[: 2 * groups], refs[2 * groups :]
    if not last:
        refs[0][...] = jnp.zeros(refs[0].shape, jnp.float32)
        refs = refs[1:]
    packed_ref, rows_ref, sem = refs
    column = lax.broadcasted_iota(jnp.int32, (QTILE, STAT), 1)

    def attention(packed, absent, fresh):
        span = absent.shape[1]
        for group in range(groups):
            stat_ref, acc_ref = state[2 * group], state[2 * group + 1]
            query = queries[group][...]
            scores = [jnp.dot(query, ref[...], preferred_element_type=jnp.float32) for ref in packed]
            scores = scores[0] if len(scores) == 1 else jnp.concatenate(scores, axis=1)
            scores = scores.reshape(QTILE // 64, PAIRS, HEADS, span) * SCORE_SCALE + absent[None, :, None, :]
            scores = scores.reshape(QTILE, span)
            newer = jnp.max(scores, axis=1, keepdims=True)
            if fresh and first:
                newer = jnp.maximum(newer, LOWEST)
            else:
                stats, acc = (former_state[2 * group], former_state[2 * group + 1]) if fresh else (stat_ref, acc_ref)
                former = stats[:, :1]
                newer = jnp.maximum(former, newer)
                decay = jnp.exp2(former - newer)
            weights = jnp.exp2(scores - newer)
            total = jnp.sum(weights, axis=1, keepdims=True)
            weights = weights.astype(jnp.bfloat16)
            added, start = None, 0
            for ref in packed:
                width = ref.shape[1]
                piece = lax.dot_general(
                    weights[:, start : start + width], ref[:LAT, :], NT, preferred_element_type=jnp.float32
                )
                added = piece if added is None else added + piece
                start += width
            if not (fresh and first):
                total = stats[:, STAT // 2 : STAT // 2 + 1] * decay + total
                added = acc[...] * decay + added
            acc_ref[...] = added
            stat_ref[...] = jnp.where(column < STAT // 2, newer, total)

    attention(packs[::2], jnp.concatenate([ref[...] for ref in packs[1::2]], axis=1), True)

    for block in range(len(parts)):
        row = base + block
        rounds = (count_ref[row, 0] + (PACK - 1)) // PACK

        @pl.when(rounds > 1)
        def _(block=block, row=row, rounds=rounds):
            for order, piece in enumerate(latent_parts(sources[block])):
                copy = pltpu.make_async_copy(piece, rows_ref.at[pl.ds(order * (KV // 2), KV // 2), :], sem)
                copy.start()
                copy.wait()

            @pl.loop(1, rounds)
            def _(number):
                absent = pack_block(
                    number, [rows_ref[...]], mask_ref[row], pos_ref[row : row + 1, :], packed_ref, 0
                )
                attention([packed_ref], absent, False)

    if last:
        for group in range(groups):
            stat_ref, acc_ref = state[2 * group], state[2 * group + 1]
            write_payload(outs[group], stat_ref[:, :1], stat_ref[:, STAT // 2 : STAT // 2 + 1], acc_ref[...])


def write_payload(out_ref, highest, total, acc):
    lane = lax.broadcasted_iota(jnp.int32, (acc.shape[0], STAT), 1)
    out_ref[:, :LAT] = acc.astype(jnp.bfloat16)
    out_ref[:, LAT:] = (split_three(highest, lane, 0) + split_three(total, lane, 3)).astype(jnp.bfloat16)


def attend(base, counts, queries, masks, positions, packs, sources, states=None, last=False):
    parts = [len(pieces) for pieces in sources]
    first = states is None
    groups = len(queries)
    shapes = (
        jax.ShapeDtypeStruct((QTILE, STAT), jnp.float32),
        jax.ShapeDtypeStruct((QTILE, LAT), jnp.float32),
    ) * groups
    if last:
        out_shape = (jax.ShapeDtypeStruct((QTILE, LAT + STAT), jnp.bfloat16),) * groups
        scratch = [pltpu.VMEM(s.shape, s.dtype) for s in shapes]
    else:
        out_shape = shapes + (TOKEN,)
        scratch = []
    scratch = scratch + [
        pltpu.VMEM((KV, PACK), jnp.bfloat16),
        pltpu.VMEM((KV, ROWS), jnp.bfloat16),
        pltpu.SemaphoreType.DMA(()),
    ]
    packed = sum([list(pair) for pair in packs], [])
    rows = [pltpu.with_memory_space_constraint(piece, pltpu.HBM) for pieces in sources for piece in pieces]
    former = [] if first else [part for state in states for part in state]

    def body(*refs):
        attend_kernel(base, parts, (groups, len(packs)), first, last, *refs)

    in_specs = [smem()] + [vmem()] * (2 + groups + len(packed))
    in_specs = in_specs + [pl.BlockSpec(memory_space=pl.ANY)] * len(rows) + [vmem()] * len(former)
    outs = pl.pallas_call(
        body,
        out_shape=out_shape,
        in_specs=in_specs,
        out_specs=(vmem(),) * len(out_shape),
        scratch_shapes=scratch,
        compiler_params=pltpu.CompilerParams(vmem_limit_bytes=16 << 20),
        cost_estimate=CHEAP,
        name="attend_%d_%d" % (len(parts), groups),
    )(counts, masks, positions, *queries, *packed, *rows, *former)
    if last:
        return list(outs)
    return [tuple(outs[2 * group : 2 * group + 2]) for group in range(groups)], outs[-1]


def combined(refs):
    row = lax.broadcasted_iota(jnp.int32, (STAT, 2 * STAT), 0)
    col = lax.broadcasted_iota(jnp.int32, (STAT, 2 * STAT), 1)
    spread = jnp.where((row // 3) == (col // STAT), 1.0, 0.0).astype(jnp.bfloat16)
    stats = [jnp.dot(ref[:, LAT:], spread, preferred_element_type=jnp.float32) for ref in refs]
    highest = stats[0][:, :STAT]
    for stat in stats[1:]:
        highest = jnp.maximum(highest, stat[:, :STAT])
    total, acc = None, None
    for ref, stat in zip(refs, stats):
        weight = jnp.exp2(stat[:, :STAT] - highest)
        wide = jnp.concatenate([weight] * (LAT // STAT), axis=1) * ref[:, :LAT].astype(jnp.float32)
        total = weight * stat[:, STAT:] if total is None else total + weight * stat[:, STAT:]
        acc = wide if acc is None else acc + wide
    return highest, total, acc


def combine_kernel(*refs):
    highest, total, acc = combined(refs[:4])
    for part, out_ref in enumerate(refs[4:]):
        here = slice(part * PAIRS * HEADS, (part + 1) * PAIRS * HEADS)
        write_payload(out_ref, highest[here, :1], total[here, :1], acc[here, :])


def combine(parts):
    return pl.pallas_call(
        combine_kernel,
        out_shape=(jax.ShapeDtypeStruct((PAIRS * HEADS, LAT + STAT), jnp.bfloat16),) * 4,
        in_specs=[vmem()] * 4,
        out_specs=(vmem(),) * 4,
        compiler_params=pltpu.CompilerParams(vmem_limit_bytes=8 << 20),
        cost_estimate=CHEAP,
        name="combine",
    )(*parts)


def project_kernel(value_ref, weights, partial_ref, *refs):
    out_ref = refs[4]
    highest, total, acc = combined(refs[:4])
    attn = (acc / jnp.concatenate([total] * (LAT // STAT), axis=1)).astype(jnp.bfloat16)
    head_of = lax.broadcasted_iota(jnp.int32, (PAIRS, HEADS, 128), 1)
    pieces = []
    for head in range(HEADS):
        product = jnp.dot(attn, value_ref[head], preferred_element_type=jnp.float32)
        product = jnp.where(head_of == head, product.reshape(PAIRS, HEADS, 128), 0.0)
        pieces.append(jnp.sum(product, axis=1))
    values = jnp.concatenate(pieces, axis=1).astype(jnp.bfloat16)
    width = weights.shape[1]
    result = jnp.dot(values, weights[...], preferred_element_type=jnp.float32)
    out_ref[:, :width] = result.astype(jnp.bfloat16)
    lane = lax.broadcasted_iota(jnp.int32, (PAIRS, STAT), 1)
    group = lax.axis_index("pre")
    mine = jnp.sum(jnp.where(lane == group, partial_ref[...], 0.0), axis=1, keepdims=True)
    out_ref[:, width:] = split_three(mine, lane, 0).astype(jnp.bfloat16)


def project(received, value_proj, out_proj, partial):
    return pl.pallas_call(
        project_kernel,
        out_shape=jax.ShapeDtypeStruct((PAIRS, out_proj.shape[1] + STAT), jnp.bfloat16),
        in_specs=[vmem()] * 7,
        out_specs=vmem(),
        compiler_params=pltpu.CompilerParams(vmem_limit_bytes=16 << 20),
        cost_estimate=CHEAP,
        name="project",
    )(value_proj, pltpu.with_memory_space_constraint(out_proj, pltpu.VMEM), partial, *received)


def index_kernel(chips, first_keys, second_keys, unused_ref, *refs):
    place = lax.axis_index("pre")
    former_ref, middles, out_ref, slab_ref = refs[0], refs[1:-2], refs[-2], refs[-1]
    lane = lax.broadcasted_iota(jnp.int32, (PAIRS, 128), 1)
    result = former_ref[...]
    for chip in chips:
        uses, middles = middles[: 1 if chip < 2 else 2], middles[1 if chip < 2 else 2 :]
        middle = uses[0][...] if chip < 2 else jnp.concatenate([part[...] for part in uses], axis=0)
        for pair in range(PAIRS):
            slab_ref[pair * 64 : (pair + 1) * 64, :] = middle[:64, pair * IDX : (pair + 1) * IDX]
        gates = middle[64:80, :64].astype(jnp.float32)
        lines = [jnp.concatenate([gates[2 * line : 2 * line + 1], gates[2 * line + 1 : 2 * line + 2]], axis=1) for line in range(4)]
        columns = jnp.concatenate(lines + [jnp.zeros((124, 128), jnp.float32)], axis=0).T
        group = (((place >> 1) + chip) & 3) * 2 + (place & 1)
        sums = []
        for keys in (first_keys, second_keys):
            scores = []
            for part in range(4):
                logits = lax.dot_general(
                    slab_ref[part * 128 : (part + 1) * 128, :], keys[...], NT, preferred_element_type=jnp.float32
                )
                gated = jnp.maximum(logits, 0.0) * columns[:, part : part + 1]
                scores.append(jnp.sum(gated.reshape(2, 64, ROWS), axis=1))
            scores = jnp.concatenate(scores, axis=0) * IDX ** (-0.5)
            largest = jnp.max(scores, axis=1, keepdims=True)
            sums.append(largest + jnp.log(jnp.sum(jnp.exp(scores - largest), axis=1, keepdims=True)))
        result = jnp.where(lane == group, log_add(sums[0], sums[1]), result)
    out_ref[...] = result


def index_partial(chips, keys, token, former, blocks):
    specs, args = [], []
    for parts in blocks:
        if len(parts) == 1:
            specs.append(pl.BlockSpec((MIDDLE, ROWS), lambda part: (3, 0)))
        else:
            specs.append(pl.BlockSpec((MIDDLE // 2, ROWS), lambda part: (6, 0)))
            specs.append(pl.BlockSpec((MIDDLE // 2, ROWS), lambda part: (0, 0)))
        args += list(parts)

    def body(*refs):
        index_kernel(chips, *refs)

    whole = pl.BlockSpec(keys[0].shape, lambda part: (0, 0))
    small = pl.BlockSpec((PAIRS, 128), lambda part: (0, 0))
    return pl.pallas_call(
        body,
        grid=(1,),
        out_shape=jax.ShapeDtypeStruct((PAIRS, 128), jnp.float32),
        in_specs=[whole, whole, pl.BlockSpec(memory_space=pl.ANY), small] + specs,
        out_specs=small,
        scratch_shapes=[pltpu.VMEM((PAIRS * 64, IDX), jnp.bfloat16)],
        compiler_params=pltpu.CompilerParams(vmem_limit_bytes=16 << 20),
        cost_estimate=CHEAP,
        name="index_partial_%d" % len(chips),
    )(*keys, token, former, *args)


def log_add(one, two):
    top = jnp.maximum(one, two)
    return top + jnp.log(jnp.exp(one - top) + jnp.exp(two - top))


def split_three(value, lane, start):
    pieces = jnp.zeros(lane.shape, jnp.float32)
    for step in range(3):
        piece = value.astype(jnp.bfloat16).astype(jnp.float32)
        pieces = jnp.where(lane == start + step, piece, pieces)
        value = value - piece
    return pieces


def join_three(pieces, start):
    wide = pieces.astype(jnp.float32)
    return wide[:, start : start + 1] + wide[:, start + 1 : start + 2] + wide[:, start + 2 : start + 3]


def four_sum(refs):
    width = refs[0].shape[1] - STAT
    parts = [ref[:, :width].astype(jnp.float32) for ref in refs]
    logs = [join_three(ref[:, width:], 0) for ref in refs]
    return (parts[0] + parts[1]) + (parts[2] + parts[3]), log_add(log_add(logs[0], logs[1]), log_add(logs[2], logs[3]))


def middle_kernel(own_ref, far_ref, right_ref, left_ref, out_ref):
    summed, logs = four_sum((own_ref, far_ref, right_ref, left_ref))
    width = summed.shape[1]
    out_ref[:, :width] = summed.astype(jnp.bfloat16)
    lane = lax.broadcasted_iota(jnp.int32, (PAIRS, STAT), 1)
    out_ref[:, width:] = split_three(logs, lane, 0).astype(jnp.bfloat16)


def final_kernel(own_ref, far_ref, right_ref, left_ref, out_ref, log_ref):
    summed, logs = four_sum((own_ref, far_ref, right_ref, left_ref))
    steps, local = log_ref.shape
    flat = jnp.broadcast_to(logs, (PAIRS, STAT)).T[:1, :]
    for step in range(steps):
        out_ref[step] = summed[step * local : (step + 1) * local, :].astype(jnp.bfloat16)
        log_ref[step : step + 1, :] = flat[:, step * local : (step + 1) * local]


def summed_over(value, shift, final):
    parts = (value,) + tuple(lax.ppermute(value, BOTH, shift(step)) for step in (2, 1, 3))
    if final:
        out_shape = (
            jax.ShapeDtypeStruct(final + (value.shape[1] - STAT,), jnp.bfloat16),
            jax.ShapeDtypeStruct(final, jnp.float32),
        )
        out_specs = (vmem(), vmem())
    else:
        out_shape = jax.ShapeDtypeStruct(value.shape, jnp.bfloat16)
        out_specs = vmem()
    return pl.pallas_call(
        final_kernel if final else middle_kernel,
        out_shape=out_shape,
        in_specs=[vmem()] * 4,
        out_specs=out_specs,
        compiler_params=pltpu.CompilerParams(vmem_limit_bytes=4 << 20),
        cost_estimate=CHEAP,
        name="sum_last" if final else "sum_first",
    )(*parts)


def prepare_kernel(latent_ref, query_ref, gate_ref, key_ref, block_ref, key_out_ref):
    part = pl.program_id(0)

    @pl.when(part != 3)
    def _():
        block_ref[...] = latent_ref[...].astype(jnp.bfloat16)

    @pl.when(part == 3)
    def _():
        block_ref[64:, :] = jnp.zeros((MIDDLE - 64, ROWS), jnp.bfloat16)
        gates = []
        for step in range(query_ref.shape[0]):
            for local in range(query_ref.shape[1]):
                pair = step * query_ref.shape[1] + local
                block_ref[:64, pair * IDX : (pair + 1) * IDX] = query_ref[step, local]
                gates.append(gate_ref[step, local : local + 1, :].astype(jnp.float32))
        gates = jnp.concatenate(gates + [jnp.zeros((8, 64), jnp.float32)], axis=0)
        block_ref[64:80, :64] = gates.astype(jnp.bfloat16)
        key_out_ref[...] = key_ref[...].astype(jnp.bfloat16)


def prepare(latent, index_queries, index_gates, index_keys):
    parts = WIDE // MIDDLE
    return pl.pallas_call(
        prepare_kernel,
        grid=(parts,),
        out_shape=(
            jax.ShapeDtypeStruct((WIDE, ROWS), jnp.bfloat16),
            jax.ShapeDtypeStruct(index_keys.shape, jnp.bfloat16),
        ),
        in_specs=[
            pl.BlockSpec((MIDDLE, ROWS), lambda part: (jnp.where(part < 3, part, part - 1), 0)),
            pl.BlockSpec(index_queries.shape, lambda part: (0, 0, 0, 0)),
            pl.BlockSpec(index_gates.shape, lambda part: (0, 0, 0)),
            pl.BlockSpec(index_keys.shape, lambda part: (0, 0)),
        ],
        out_specs=(
            pl.BlockSpec((MIDDLE, ROWS), lambda part: (part, 0)),
            pl.BlockSpec(index_keys.shape, lambda part: (0, 0)),
        ),
        compiler_params=pltpu.CompilerParams(vmem_limit_bytes=8 << 20),
        cost_estimate=CHEAP,
        name="prepare",
    )(
        pltpu.with_memory_space_constraint(latent, pltpu.HBM),
        pltpu.with_memory_space_constraint(index_queries, pltpu.HBM),
        pltpu.with_memory_space_constraint(index_gates, pltpu.HBM),
        pltpu.with_memory_space_constraint(index_keys, pltpu.HBM),
    )


def x_shift(step):
    return [(x * 2 + c, ((x + step) % 4) * 2 + c) for x in range(4) for c in range(2)]


BOTH = ("pre", "tp")


def plane_shift(step, along_y):
    pairs = []
    for p in range(PRE):
        for z in range(4):
            for y in range(4):
                to_y = along_y == (p % 2 == 0)
                there = z * 4 + (y + step) % 4 if to_y else ((z + step) % 4) * 4 + y
                pairs.append((p * TP + z * 4 + y, p * TP + there))
    return pairs


def first_shift(step):
    return plane_shift(step, True)


def second_shift(step):
    return plane_shift(step, False)


CORE_SWAP = [(i, i ^ 1) for i in range(PRE)]


def on_device(
    latent_rows,
    index_keys,
    queries,
    index_queries,
    index_gates,
    value_proj,
    out_proj,
    block_rows,
    block_owner,
    block_count,
):
    block, keys = prepare(latent_rows.T, index_queries, index_gates, index_keys)
    forward = lax.ppermute(block, "pre", x_shift(1))
    backward = lax.ppermute(block, "pre", x_shift(3))

    own_queries = queries.reshape(PAIRS * HEADS, KV)
    row = jnp.concatenate(
        [own_queries] + [lax.ppermute(own_queries, BOTH, first_shift(4 - step)) for step in (1, 2, 3)], axis=0
    )
    plane = [row] + [lax.ppermute(row, BOTH, second_shift(4 - step)) for step in (1, 2, 3)]

    def swapped(part):
        return lax.ppermute(part, "pre", CORE_SWAP)

    def both(parts):
        return [list(parts), [swapped(part) for part in parts]]

    masks, positions, counts = make_tables(block_rows, block_owner, block_count)
    token = arrived(plane[1:] + [masks])
    forward, backward, block, keys, token = lax.optimization_barrier((forward, backward, block, keys, token))
    top, low = halves(forward, backward)
    far = [lax.ppermute(top, "pre", x_shift(1)), lax.ppermute(low, "pre", x_shift(3))]

    own, sides = both([block]), both([forward]) + both([backward])
    keys = [keys, swapped(keys)]
    packs = [
        pack(base, early, masks, positions, rows)
        for base, early, rows in ((0, keys[1], sides[:2]), (2, token, own), (4, token, sides[2:]))
    ]
    states, token = attend(0, counts, plane, masks, positions, packs, sides[:2] + own + sides[2:])
    far, token = lax.optimization_barrier((far, token))
    partial = index_partial((0, 1, -1), keys, token, token, (own[0], sides[2], sides[0]))
    far = both(far)
    packs = [pack(6, partial, masks, positions, far)]

    payloads = attend(6, counts, plane[1:], masks, positions, packs, far, states[1:], last=True)
    payload = attend(6, counts, plane[:1], masks, positions, packs, far, states[:1], last=True)
    parts = payload + [lax.ppermute(payloads[step - 1], BOTH, second_shift(step)) for step in (1, 2, 3)]
    parts = combine(parts)
    received = [parts[0]] + [lax.ppermute(parts[step], BOTH, first_shift(step)) for step in (1, 2, 3)]
    partial = index_partial((2,), keys, payloads[0], partial, (far[0],))
    parts = [lax.ppermute(partial, "pre", x_shift(step)) for step in (2, 1, 3)]
    partial = log_add(log_add(partial, parts[0]), log_add(parts[1], parts[2]))
    part_out = project(received, value_proj, out_proj, partial)
    return summed_over(summed_over(part_out, first_shift, None), second_shift, queries.shape[:2])


def solution(mesh):
    placed = (
        P(("pre", "tp"), None),
        P(("pre", "tp"), None),
        P(None, "pre", "tp", None),
        P(None, "pre", None, None),
        P(None, "pre", None),
        P("tp", None, None),
        P("tp", None),
        P(None, "pre", None, None),
        P(None, "pre", None),
        P(None, "pre", None),
    )
    return jax.shard_map(
        on_device,
        mesh=mesh,
        in_specs=placed,
        out_specs=(P(None, "pre", None), P(None, "pre")),
        check_vma=False,
    )
```

```python
import jax
import jax.numpy as jnp
from jax import lax
from jax.experimental import pallas as pl
from jax.experimental.pallas import tpu as pltpu
from jax.sharding import PartitionSpec as P

IDX = 128
LAT = 512
KV = 576
BLOCK = 64
PRE = 8
TP = 16
PAIRS = 8
HEADS = 8
ROWS = 1024
PACK = 256
MIDDLE = 96
WIDE = KV + MIDDLE
CHUNKS = 6
QTILE = 256
STAT = 128
QROWS = TP * PAIRS * HEADS
LOWEST = -3.0e38
SOFT_SCALE = 192.0 ** (-0.5)
LOG2E = 1.4426950408889634
SCORE_SCALE = SOFT_SCALE * LOG2E

NT = (((1,), (1,)), ((), ()))


CHEAP = pl.CostEstimate(flops=1000, bytes_accessed=1000, transcendentals=0)


def vmem():
    return pl.BlockSpec(memory_space=pltpu.VMEM)


def smem():
    return pl.BlockSpec(memory_space=pltpu.SMEM)


def table_kernel(rows_ref, owner_ref, count_ref, mask_ref, pos_ref, total_ref):
    me_pre = lax.axis_index("pre")
    me_tp = lax.axis_index("tp")
    number = rows_ref.shape[2]
    before = (
        lax.broadcasted_iota(jnp.int32, (number, number), 0) < lax.broadcasted_iota(jnp.int32, (number, number), 1)
    ).astype(jnp.float32).astype(jnp.bfloat16)
    slot = lax.broadcasted_iota(jnp.int32, (8, number), 0).astype(jnp.float32)
    entry = lax.broadcasted_iota(jnp.int32, (8, BLOCK), 1).astype(jnp.float32)
    high_iota = lax.broadcasted_iota(jnp.int32, (PRE * 8, BLOCK), 0).astype(jnp.float32)
    low_iota = lax.broadcasted_iota(jnp.int32, (128, BLOCK), 0).astype(jnp.float32)
    for pair in range(PAIRS):
        step, local = pair // rows_ref.shape[1], pair % rows_ref.shape[1]
        rows = rows_ref[step, local]
        source = rows >> 10
        relative = ((((source >> 1) - (me_pre >> 1) + 1) & 3) << 1) | ((source ^ me_pre) & 1)
        high = ((relative << 3) | ((rows >> 7) & 7)).astype(jnp.float32).astype(jnp.bfloat16)
        low = (rows & 127).astype(jnp.float32).astype(jnp.bfloat16)
        owned = jnp.where(owner_ref[step, local : local + 1, :] == me_tp, 1.0, 0.0)
        rank = jnp.dot(owned.astype(jnp.bfloat16), before, preferred_element_type=jnp.float32)
        choose = jnp.where(slot == rank, owned, 0.0)
        limit = jnp.sum(choose * count_ref[step, local : local + 1, :].astype(jnp.float32), axis=1, keepdims=True)
        choose = choose.astype(jnp.bfloat16)
        valid = entry < limit
        high = jnp.where(valid, jnp.dot(choose, high, preferred_element_type=jnp.float32), -1.0)
        low = jnp.dot(choose, low, preferred_element_type=jnp.float32)
        chosen = jnp.zeros((PRE * 8, 128), jnp.float32)
        for block in range(number // TP):
            high_one = jnp.where(high_iota == high[block : block + 1, :], 1.0, 0.0).astype(jnp.bfloat16)
            low_one = jnp.where(low_iota == low[block : block + 1, :], 1.0, 0.0).astype(jnp.bfloat16)
            chosen = chosen + lax.dot_general(high_one, low_one, NT, preferred_element_type=jnp.float32)
        for block in range(PRE):
            for part in range(8):
                mask_ref[block, pair : pair + 1, part * 128 : (part + 1) * 128] = chosen[
                    block * 8 + part : block * 8 + part + 1, :
                ]
    union = jnp.concatenate([jnp.max(mask_ref[block], axis=0, keepdims=True) for block in range(PRE)], axis=0)
    before = (
        lax.broadcasted_iota(jnp.int32, (128, 128), 0) < lax.broadcasted_iota(jnp.int32, (128, 128), 1)
    ).astype(jnp.float32).astype(jnp.bfloat16)
    carry = jnp.zeros((PRE, 1), jnp.float32)
    for part in range(8):
        piece = union[:, part * 128 : (part + 1) * 128]
        ahead = jnp.dot(piece.astype(jnp.bfloat16), before, preferred_element_type=jnp.float32) + carry
        pos_ref[:, part * 128 : (part + 1) * 128] = jnp.where(piece > 0.0, ahead, -1.0)
        carry = carry + jnp.sum(piece, axis=1, keepdims=True)
    total_ref[...] = jnp.broadcast_to(carry, (PRE, 128)).astype(jnp.int32)


def make_tables(block_rows, block_owner, block_count):
    return pl.pallas_call(
        table_kernel,
        out_shape=(
            jax.ShapeDtypeStruct((PRE, PAIRS, ROWS), jnp.float32),
            jax.ShapeDtypeStruct((PRE, ROWS), jnp.float32),
            jax.ShapeDtypeStruct((PRE, 128), jnp.int32),
        ),
        in_specs=[vmem()] * 3,
        out_specs=(vmem(), vmem(), vmem()),
        compiler_params=pltpu.CompilerParams(vmem_limit_bytes=8 << 20),
        cost_estimate=CHEAP,
        name="row_tables",
    )(block_rows, block_owner, block_count)


TOKEN = jax.ShapeDtypeStruct((8, 128), jnp.float32)


def token_kernel(*refs):
    refs[-1][...] = jnp.zeros(refs[-1].shape, jnp.float32)


def arrived(values):
    return pl.pallas_call(
        token_kernel,
        out_shape=TOKEN,
        in_specs=[pl.BlockSpec(memory_space=pl.ANY)] * len(values),
        out_specs=vmem(),
        compiler_params=pltpu.CompilerParams(vmem_limit_bytes=2 << 20),
        cost_estimate=CHEAP,
        name="arrived",
    )(*values)


def halves_kernel(forward_ref, backward_ref, top_ref, low_ref):
    top_ref[...] = forward_ref[...]
    low_ref[...] = backward_ref[...]


def halves(forward, backward):
    half = (forward.shape[0] // 2, forward.shape[1])
    out = jax.ShapeDtypeStruct(half, forward.dtype)
    return pl.pallas_call(
        halves_kernel,
        grid=(1,),
        out_shape=(out, out),
        in_specs=[pl.BlockSpec(half, lambda part: (0, 0)), pl.BlockSpec(half, lambda part: (1, 0))],
        out_specs=(pl.BlockSpec(half, lambda part: (0, 0)),) * 2,
        compiler_params=pltpu.CompilerParams(vmem_limit_bytes=8 << 20),
        cost_estimate=CHEAP,
        name="halves",
    )(forward, backward)


def pack_block(number, pieces, mask_row, pos_row, packed_ref, first_lane):
    slot = (lax.broadcasted_iota(jnp.int32, (PACK, ROWS), 0) + number * PACK).astype(jnp.float32)
    pick = jnp.where(slot == pos_row, 1.0, 0.0).astype(jnp.bfloat16)
    depth = KV // len(pieces)
    for order, piece in enumerate(pieces):
        packed = lax.dot_general(piece, pick, NT, preferred_element_type=jnp.float32)
        packed_ref[order * depth : (order + 1) * depth, first_lane : first_lane + PACK] = packed.astype(jnp.bfloat16)
    present = lax.dot_general(mask_row.astype(jnp.bfloat16), pick, NT, preferred_element_type=jnp.float32)
    return jnp.where(present > 0.5, 0.0, -jnp.inf)


def latent_parts(refs):
    half = KV // 2
    if len(refs) == 1:
        return [refs[0].at[pl.ds(0, half), :], refs[0].at[pl.ds(half + MIDDLE, half), :]]
    return [refs[0].at[pl.ds(0, half), :], refs[1].at[pl.ds(MIDDLE // 2, half), :]]


def pack_kernel(base, parts, unused_ref, mask_ref, pos_ref, *refs):
    packed_ref, absent_ref = refs[-2:]
    for block, number in enumerate(parts):
        pieces, refs = refs[:number], refs[number:]
        row = base + block
        absent_ref[:, block * PACK : (block + 1) * PACK] = pack_block(
            0, [part[...] for part in latent_parts(pieces)], mask_ref[row], pos_ref[row : row + 1, :], packed_ref,
            block * PACK,
        )


def pack(base, token, masks, positions, sources):
    parts = [len(pieces) for pieces in sources]
    rows = sum([list(pieces) for pieces in sources], [])

    def body(*refs):
        pack_kernel(base, parts, *refs)

    return pl.pallas_call(
        body,
        out_shape=(
            jax.ShapeDtypeStruct((KV, len(parts) * PACK), jnp.bfloat16),
            jax.ShapeDtypeStruct((PAIRS, len(parts) * PACK), jnp.float32),
        ),
        in_specs=[pl.BlockSpec(memory_space=pl.ANY)] + [vmem()] * (2 + len(rows)),
        out_specs=(vmem(), vmem()),
        compiler_params=pltpu.CompilerParams(vmem_limit_bytes=16 << 20),
        cost_estimate=CHEAP,
        name="pack_%d" % len(parts),
    )(token, masks, positions, *rows)


def attend_kernel(base, parts, shapes, first, last, count_ref, mask_ref, pos_ref, *refs):
    queries, refs = refs[: shapes[0]], refs[shapes[0] :]
    packs, refs = refs[: 2 * shapes[1]], refs[2 * shapes[1] :]
    sources = []
    for number in parts:
        sources.append(refs[:number])
        refs = refs[number:]
    groups = len(queries)
    if not first:
        former_state, refs = refs[: 2 * groups], refs[2 * groups :]
    if last:
        outs, refs = refs[:groups], refs[groups:]
    state, refs = refs[: 2 * groups], refs[2 * groups :]
    if not last:
        refs[0][...] = jnp.zeros(refs[0].shape, jnp.float32)
        refs = refs[1:]
    packed_ref, rows_ref, sem = refs
    column = lax.broadcasted_iota(jnp.int32, (QTILE, STAT), 1)

    def attention(packed, absent, fresh):
        span = absent.shape[1]
        for group in range(groups):
            stat_ref, acc_ref = state[2 * group], state[2 * group + 1]
            query = queries[group][...]
            scores = [jnp.dot(query, ref[...], preferred_element_type=jnp.float32) for ref in packed]
            scores = scores[0] if len(scores) == 1 else jnp.concatenate(scores, axis=1)
            scores = scores.reshape(QTILE // 64, PAIRS, HEADS, span) * SCORE_SCALE + absent[None, :, None, :]
            scores = scores.reshape(QTILE, span)
            newer = jnp.max(scores, axis=1, keepdims=True)
            if fresh and first:
                newer = jnp.maximum(newer, LOWEST)
            else:
                stats, acc = (former_state[2 * group], former_state[2 * group + 1]) if fresh else (stat_ref, acc_ref)
                former = stats[:, :1]
                newer = jnp.maximum(former, newer)
                decay = jnp.exp2(former - newer)
            weights = jnp.exp2(scores - newer)
            total = jnp.sum(weights, axis=1, keepdims=True)
            weights = weights.astype(jnp.bfloat16)
            added, start = None, 0
            for ref in packed:
                width = ref.shape[1]
                piece = lax.dot_general(
                    weights[:, start : start + width], ref[:LAT, :], NT, preferred_element_type=jnp.float32
                )
                added = piece if added is None else added + piece
                start += width
            if not (fresh and first):
                total = stats[:, STAT // 2 : STAT // 2 + 1] * decay + total
                added = acc[...] * decay + added
            acc_ref[...] = added
            stat_ref[...] = jnp.where(column < STAT // 2, newer, total)

    attention(packs[::2], jnp.concatenate([ref[...] for ref in packs[1::2]], axis=1), True)

    for block in range(len(parts)):
        row = base + block
        rounds = (count_ref[row, 0] + (PACK - 1)) // PACK

        @pl.when(rounds > 1)
        def _(block=block, row=row, rounds=rounds):
            for order, piece in enumerate(latent_parts(sources[block])):
                copy = pltpu.make_async_copy(piece, rows_ref.at[pl.ds(order * (KV // 2), KV // 2), :], sem)
                copy.start()
                copy.wait()

            @pl.loop(1, rounds)
            def _(number):
                absent = pack_block(
                    number, [rows_ref[...]], mask_ref[row], pos_ref[row : row + 1, :], packed_ref, 0
                )
                attention([packed_ref], absent, False)

    if last:
        for group in range(groups):
            stat_ref, acc_ref = state[2 * group], state[2 * group + 1]
            write_payload(outs[group], stat_ref[:, :1], stat_ref[:, STAT // 2 : STAT // 2 + 1], acc_ref[...])


def write_payload(out_ref, highest, total, acc):
    lane = lax.broadcasted_iota(jnp.int32, (acc.shape[0], STAT), 1)
    out_ref[:, :LAT] = acc.astype(jnp.bfloat16)
    out_ref[:, LAT:] = (split_three(highest, lane, 0) + split_three(total, lane, 3)).astype(jnp.bfloat16)


def attend(base, counts, queries, masks, positions, packs, sources, states=None, last=False):
    parts = [len(pieces) for pieces in sources]
    first = states is None
    groups = len(queries)
    shapes = (
        jax.ShapeDtypeStruct((QTILE, STAT), jnp.float32),
        jax.ShapeDtypeStruct((QTILE, LAT), jnp.float32),
    ) * groups
    if last:
        out_shape = (jax.ShapeDtypeStruct((QTILE, LAT + STAT), jnp.bfloat16),) * groups
        scratch = [pltpu.VMEM(s.shape, s.dtype) for s in shapes]
    else:
        out_shape = shapes + (TOKEN,)
        scratch = []
    scratch = scratch + [
        pltpu.VMEM((KV, PACK), jnp.bfloat16),
        pltpu.VMEM((KV, ROWS), jnp.bfloat16),
        pltpu.SemaphoreType.DMA(()),
    ]
    packed = sum([list(pair) for pair in packs], [])
    rows = [pltpu.with_memory_space_constraint(piece, pltpu.HBM) for pieces in sources for piece in pieces]
    former = [] if first else [part for state in states for part in state]

    def body(*refs):
        attend_kernel(base, parts, (groups, len(packs)), first, last, *refs)

    in_specs = [smem()] + [vmem()] * (2 + groups + len(packed))
    in_specs = in_specs + [pl.BlockSpec(memory_space=pl.ANY)] * len(rows) + [vmem()] * len(former)
    outs = pl.pallas_call(
        body,
        out_shape=out_shape,
        in_specs=in_specs,
        out_specs=(vmem(),) * len(out_shape),
        scratch_shapes=scratch,
        compiler_params=pltpu.CompilerParams(vmem_limit_bytes=16 << 20),
        cost_estimate=CHEAP,
        name="attend_%d_%d" % (len(parts), groups),
    )(counts, masks, positions, *queries, *packed, *rows, *former)
    if last:
        return list(outs)
    return [tuple(outs[2 * group : 2 * group + 2]) for group in range(groups)], outs[-1]


def combined(refs):
    row = lax.broadcasted_iota(jnp.int32, (STAT, 2 * STAT), 0)
    col = lax.broadcasted_iota(jnp.int32, (STAT, 2 * STAT), 1)
    spread = jnp.where((row // 3) == (col // STAT), 1.0, 0.0).astype(jnp.bfloat16)
    stats = [jnp.dot(ref[:, LAT:], spread, preferred_element_type=jnp.float32) for ref in refs]
    highest = stats[0][:, :STAT]
    for stat in stats[1:]:
        highest = jnp.maximum(highest, stat[:, :STAT])
    total, acc = None, None
    for ref, stat in zip(refs, stats):
        weight = jnp.exp2(stat[:, :STAT] - highest)
        wide = jnp.concatenate([weight] * (LAT // STAT), axis=1) * ref[:, :LAT].astype(jnp.float32)
        total = weight * stat[:, STAT:] if total is None else total + weight * stat[:, STAT:]
        acc = wide if acc is None else acc + wide
    return highest, total, acc


def combine_kernel(*refs):
    highest, total, acc = combined(refs[:4])
    for part, out_ref in enumerate(refs[4:]):
        here = slice(part * PAIRS * HEADS, (part + 1) * PAIRS * HEADS)
        write_payload(out_ref, highest[here, :1], total[here, :1], acc[here, :])


def combine(parts):
    return pl.pallas_call(
        combine_kernel,
        out_shape=(jax.ShapeDtypeStruct((PAIRS * HEADS, LAT + STAT), jnp.bfloat16),) * 4,
        in_specs=[vmem()] * 4,
        out_specs=(vmem(),) * 4,
        compiler_params=pltpu.CompilerParams(vmem_limit_bytes=8 << 20),
        cost_estimate=CHEAP,
        name="combine",
    )(*parts)


def project_kernel(value_ref, weights, partial_ref, *refs):
    out_ref = refs[4]
    highest, total, acc = combined(refs[:4])
    attn = (acc / jnp.concatenate([total] * (LAT // STAT), axis=1)).astype(jnp.bfloat16)
    head_of = lax.broadcasted_iota(jnp.int32, (PAIRS, HEADS, 128), 1)
    pieces = []
    for head in range(HEADS):
        product = jnp.dot(attn, value_ref[head], preferred_element_type=jnp.float32)
        product = jnp.where(head_of == head, product.reshape(PAIRS, HEADS, 128), 0.0)
        pieces.append(jnp.sum(product, axis=1))
    values = jnp.concatenate(pieces, axis=1).astype(jnp.bfloat16)
    width = weights.shape[1]
    result = jnp.dot(values, weights[...], preferred_element_type=jnp.float32)
    out_ref[:, :width] = result.astype(jnp.bfloat16)
    lane = lax.broadcasted_iota(jnp.int32, (PAIRS, STAT), 1)
    group = lax.axis_index("pre")
    mine = jnp.sum(jnp.where(lane == group, partial_ref[...], 0.0), axis=1, keepdims=True)
    out_ref[:, width:] = split_three(mine, lane, 0).astype(jnp.bfloat16)


def project(received, value_proj, out_proj, partial):
    return pl.pallas_call(
        project_kernel,
        out_shape=jax.ShapeDtypeStruct((PAIRS, out_proj.shape[1] + STAT), jnp.bfloat16),
        in_specs=[vmem()] * 7,
        out_specs=vmem(),
        compiler_params=pltpu.CompilerParams(vmem_limit_bytes=16 << 20),
        cost_estimate=CHEAP,
        name="project",
    )(value_proj, pltpu.with_memory_space_constraint(out_proj, pltpu.VMEM), partial, *received)


def index_kernel(chips, first_keys, second_keys, unused_ref, *refs):
    place = lax.axis_index("pre")
    former_ref, middles, out_ref, slab_ref = refs[0], refs[1:-2], refs[-2], refs[-1]
    lane = lax.broadcasted_iota(jnp.int32, (PAIRS, 128), 1)
    result = former_ref[...]
    for chip in chips:
        uses, middles = middles[: 1 if chip < 2 else 2], middles[1 if chip < 2 else 2 :]
        middle = uses[0][...] if chip < 2 else jnp.concatenate([part[...] for part in uses], axis=0)
        for pair in range(PAIRS):
            slab_ref[pair * 64 : (pair + 1) * 64, :] = middle[:64, pair * IDX : (pair + 1) * IDX]
        gates = middle[64:80, :64].astype(jnp.float32)
        lines = [jnp.concatenate([gates[2 * line : 2 * line + 1], gates[2 * line + 1 : 2 * line + 2]], axis=1) for line in range(4)]
        columns = jnp.concatenate(lines + [jnp.zeros((124, 128), jnp.float32)], axis=0).T
        group = (((place >> 1) + chip) & 3) * 2 + (place & 1)
        sums = []
        for keys in (first_keys, second_keys):
            scores = []
            for part in range(4):
                logits = lax.dot_general(
                    slab_ref[part * 128 : (part + 1) * 128, :], keys[...], NT, preferred_element_type=jnp.float32
                )
                gated = jnp.maximum(logits, 0.0) * columns[:, part : part + 1]
                scores.append(jnp.sum(gated.reshape(2, 64, ROWS), axis=1))
            scores = jnp.concatenate(scores, axis=0) * IDX ** (-0.5)
            largest = jnp.max(scores, axis=1, keepdims=True)
            sums.append(largest + jnp.log(jnp.sum(jnp.exp(scores - largest), axis=1, keepdims=True)))
        result = jnp.where(lane == group, log_add(sums[0], sums[1]), result)
    out_ref[...] = result


def index_partial(chips, keys, token, former, blocks):
    specs, args = [], []
    for parts in blocks:
        if len(parts) == 1:
            specs.append(pl.BlockSpec((MIDDLE, ROWS), lambda part: (3, 0)))
        else:
            specs.append(pl.BlockSpec((MIDDLE // 2, ROWS), lambda part: (6, 0)))
            specs.append(pl.BlockSpec((MIDDLE // 2, ROWS), lambda part: (0, 0)))
        args += list(parts)

    def body(*refs):
        index_kernel(chips, *refs)

    whole = pl.BlockSpec(keys[0].shape, lambda part: (0, 0))
    small = pl.BlockSpec((PAIRS, 128), lambda part: (0, 0))
    return pl.pallas_call(
        body,
        grid=(1,),
        out_shape=jax.ShapeDtypeStruct((PAIRS, 128), jnp.float32),
        in_specs=[whole, whole, pl.BlockSpec(memory_space=pl.ANY), small] + specs,
        out_specs=small,
        scratch_shapes=[pltpu.VMEM((PAIRS * 64, IDX), jnp.bfloat16)],
        compiler_params=pltpu.CompilerParams(vmem_limit_bytes=16 << 20),
        cost_estimate=CHEAP,
        name="index_partial_%d" % len(chips),
    )(*keys, token, former, *args)


def log_add(one, two):
    top = jnp.maximum(one, two)
    return top + jnp.log(jnp.exp(one - top) + jnp.exp(two - top))


def split_three(value, lane, start):
    pieces = jnp.zeros(lane.shape, jnp.float32)
    for step in range(3):
        piece = value.astype(jnp.bfloat16).astype(jnp.float32)
        pieces = jnp.where(lane == start + step, piece, pieces)
        value = value - piece
    return pieces


def join_three(pieces, start):
    wide = pieces.astype(jnp.float32)
    return wide[:, start : start + 1] + wide[:, start + 1 : start + 2] + wide[:, start + 2 : start + 3]


def four_sum(refs):
    width = refs[0].shape[1] - STAT
    parts = [ref[:, :width].astype(jnp.float32) for ref in refs]
    logs = [join_three(ref[:, width:], 0) for ref in refs]
    return (parts[0] + parts[1]) + (parts[2] + parts[3]), log_add(log_add(logs[0], logs[1]), log_add(logs[2], logs[3]))


def middle_kernel(own_ref, far_ref, right_ref, left_ref, out_ref):
    summed, logs = four_sum((own_ref, far_ref, right_ref, left_ref))
    width = summed.shape[1]
    out_ref[:, :width] = summed.astype(jnp.bfloat16)
    lane = lax.broadcasted_iota(jnp.int32, (PAIRS, STAT), 1)
    out_ref[:, width:] = split_three(logs, lane, 0).astype(jnp.bfloat16)


def final_kernel(own_ref, far_ref, right_ref, left_ref, out_ref, log_ref):
    summed, logs = four_sum((own_ref, far_ref, right_ref, left_ref))
    steps, local = log_ref.shape
    flat = jnp.broadcast_to(logs, (PAIRS, STAT)).T[:1, :]
    for step in range(steps):
        out_ref[step] = summed[step * local : (step + 1) * local, :].astype(jnp.bfloat16)
        log_ref[step : step + 1, :] = flat[:, step * local : (step + 1) * local]


def summed_over(value, shift, final):
    parts = (value,) + tuple(lax.ppermute(value, BOTH, shift(step)) for step in (2, 1, 3))
    if final:
        out_shape = (
            jax.ShapeDtypeStruct(final + (value.shape[1] - STAT,), jnp.bfloat16),
            jax.ShapeDtypeStruct(final, jnp.float32),
        )
        out_specs = (vmem(), vmem())
    else:
        out_shape = jax.ShapeDtypeStruct(value.shape, jnp.bfloat16)
        out_specs = vmem()
    return pl.pallas_call(
        final_kernel if final else middle_kernel,
        out_shape=out_shape,
        in_specs=[vmem()] * 4,
        out_specs=out_specs,
        compiler_params=pltpu.CompilerParams(vmem_limit_bytes=4 << 20),
        cost_estimate=CHEAP,
        name="sum_last" if final else "sum_first",
    )(*parts)


def prepare_kernel(latent_ref, query_ref, gate_ref, key_ref, block_ref, key_out_ref, latent, queries, gates, keys, sems):
    depth = KV // CHUNKS
    copies = [
        pltpu.make_async_copy(
            latent_ref.at[pl.ds(part * depth, depth)], latent.at[pl.ds(part * depth, depth)], sems.at[part]
        )
        for part in range(CHUNKS)
    ]
    others = [
        pltpu.make_async_copy(query_ref, queries, sems.at[CHUNKS]),
        pltpu.make_async_copy(gate_ref, gates, sems.at[CHUNKS + 1]),
        pltpu.make_async_copy(key_ref, keys, sems.at[CHUNKS + 2]),
    ]
    for copy in copies + others:
        copy.start()
    for part, copy in enumerate(copies):
        copy.wait()
        start = part * depth + (MIDDLE if part >= CHUNKS // 2 else 0)
        block_ref[start : start + depth, :] = latent[part * depth : (part + 1) * depth, :].astype(jnp.bfloat16)
    for copy in others:
        copy.wait()
    first = KV // 2
    block_ref[first + 64 : first + MIDDLE, :] = jnp.zeros((MIDDLE - 64, ROWS), jnp.bfloat16)
    lines = []
    for step in range(query_ref.shape[0]):
        for local in range(query_ref.shape[1]):
            pair = step * query_ref.shape[1] + local
            block_ref[first : first + 64, pair * IDX : (pair + 1) * IDX] = queries[step, local]
            lines.append(gates[step, local : local + 1, :].astype(jnp.float32))
    lines = jnp.concatenate(lines + [jnp.zeros((8, 64), jnp.float32)], axis=0)
    block_ref[first + 64 : first + 80, :64] = lines.astype(jnp.bfloat16)
    key_out_ref[...] = keys[...].astype(jnp.bfloat16)


def prepare(latent, index_queries, index_gates, index_keys):
    args = (latent, index_queries, index_gates, index_keys)
    return pl.pallas_call(
        prepare_kernel,
        out_shape=(
            jax.ShapeDtypeStruct((WIDE, ROWS), jnp.bfloat16),
            jax.ShapeDtypeStruct(index_keys.shape, jnp.bfloat16),
        ),
        in_specs=[pl.BlockSpec(memory_space=pl.ANY)] * 4,
        out_specs=(vmem(), vmem()),
        scratch_shapes=[pltpu.VMEM(arg.shape, arg.dtype) for arg in args] + [pltpu.SemaphoreType.DMA((CHUNKS + 3,))],
        compiler_params=pltpu.CompilerParams(vmem_limit_bytes=12 << 20),
        cost_estimate=CHEAP,
        name="prepare",
    )(*[pltpu.with_memory_space_constraint(arg, pltpu.HBM) for arg in args])


def x_shift(step):
    return [(x * 2 + c, ((x + step) % 4) * 2 + c) for x in range(4) for c in range(2)]


BOTH = ("pre", "tp")


def plane_shift(step, along_y):
    pairs = []
    for p in range(PRE):
        for z in range(4):
            for y in range(4):
                to_y = along_y == (p % 2 == 0)
                there = z * 4 + (y + step) % 4 if to_y else ((z + step) % 4) * 4 + y
                pairs.append((p * TP + z * 4 + y, p * TP + there))
    return pairs


def first_shift(step):
    return plane_shift(step, True)


def second_shift(step):
    return plane_shift(step, False)


CORE_SWAP = [(i, i ^ 1) for i in range(PRE)]


def on_device(
    latent_rows,
    index_keys,
    queries,
    index_queries,
    index_gates,
    value_proj,
    out_proj,
    block_rows,
    block_owner,
    block_count,
):
    block, keys = prepare(latent_rows.T, index_queries, index_gates, index_keys)
    forward = lax.ppermute(block, "pre", x_shift(1))
    backward = lax.ppermute(block, "pre", x_shift(3))

    own_queries = queries.reshape(PAIRS * HEADS, KV)
    row = jnp.concatenate(
        [own_queries] + [lax.ppermute(own_queries, BOTH, first_shift(4 - step)) for step in (1, 2, 3)], axis=0
    )
    plane = [row] + [lax.ppermute(row, BOTH, second_shift(4 - step)) for step in (1, 2, 3)]

    def swapped(part):
        return lax.ppermute(part, "pre", CORE_SWAP)

    def both(parts):
        return [list(parts), [swapped(part) for part in parts]]

    masks, positions, counts = make_tables(block_rows, block_owner, block_count)
    token = arrived(plane[1:] + [masks])
    forward, backward, block, keys, token = lax.optimization_barrier((forward, backward, block, keys, token))
    top, low = halves(forward, backward)
    far = [lax.ppermute(top, "pre", x_shift(1)), lax.ppermute(low, "pre", x_shift(3))]

    own, sides = both([block]), both([forward]) + both([backward])
    keys = [keys, swapped(keys)]
    packs = [
        pack(base, early, masks, positions, rows)
        for base, early, rows in ((0, keys[1], sides[:2]), (2, token, own), (4, token, sides[2:]))
    ]
    states, token = attend(0, counts, plane, masks, positions, packs, sides[:2] + own + sides[2:])
    partial = index_partial((0, 1, -1), keys, token, token, (own[0], sides[2], sides[0]))
    far, partial = lax.optimization_barrier((far, partial))
    far = both(far)
    packs = [pack(6, partial, masks, positions, far)]

    payloads = [None] * 4
    parts = [None] * 4
    for step in (2, 1, 3, 0):
        one = slice(step, step + 1)
        payloads[step] = attend(6, counts, plane[one], masks, positions, packs, far, states[one], last=True)[0]
        parts[step] = lax.ppermute(payloads[step], BOTH, second_shift(step)) if step else payloads[0]
    parts = combine(parts)
    received = [parts[0]] + [lax.ppermute(parts[step], BOTH, first_shift(step)) for step in (2, 1, 3)]
    partial = index_partial((2,), keys, payloads[3], partial, (far[0],))
    parts = [lax.ppermute(partial, "pre", x_shift(step)) for step in (2, 1, 3)]
    partial = log_add(log_add(partial, parts[0]), log_add(parts[1], parts[2]))
    part_out = project(received, value_proj, out_proj, partial)
    return summed_over(summed_over(part_out, first_shift, None), second_shift, queries.shape[:2])


def solution(mesh):
    placed = (
        P(("pre", "tp"), None),
        P(("pre", "tp"), None),
        P(None, "pre", "tp", None),
        P(None, "pre", None, None),
        P(None, "pre", None),
        P("tp", None, None),
        P("tp", None),
        P(None, "pre", None, None),
        P(None, "pre", None),
        P(None, "pre", None),
    )
    return jax.shard_map(
        on_device,
        mesh=mesh,
        in_specs=placed,
        out_specs=(P(None, "pre", None), P(None, "pre")),
        check_vma=False,
    )
```

```python
import jax
import jax.numpy as jnp
from jax import lax
from jax.experimental import pallas as pl
from jax.experimental.pallas import tpu as pltpu
from jax.sharding import PartitionSpec as P

IDX = 128
LAT = 512
KV = 576
BLOCK = 64
PRE = 8
TP = 16
PAIRS = 8
HEADS = 8
ROWS = 1024
PACK = 256
MIDDLE = 96
WIDE = KV + MIDDLE
CHUNKS = 6
QTILE = 256
STAT = 128
QROWS = TP * PAIRS * HEADS
LOWEST = -3.0e38
SOFT_SCALE = 192.0 ** (-0.5)
LOG2E = 1.4426950408889634
SCORE_SCALE = SOFT_SCALE * LOG2E

NT = (((1,), (1,)), ((), ()))


CHEAP = pl.CostEstimate(flops=1000, bytes_accessed=1000, transcendentals=0)


def vmem():
    return pl.BlockSpec(memory_space=pltpu.VMEM)


def smem():
    return pl.BlockSpec(memory_space=pltpu.SMEM)


def table_kernel(rows_ref, owner_ref, count_ref, mask_ref, pos_ref, total_ref):
    me_pre = lax.axis_index("pre")
    me_tp = lax.axis_index("tp")
    number = rows_ref.shape[2]
    before = (
        lax.broadcasted_iota(jnp.int32, (number, number), 0) < lax.broadcasted_iota(jnp.int32, (number, number), 1)
    ).astype(jnp.float32).astype(jnp.bfloat16)
    slot = lax.broadcasted_iota(jnp.int32, (8, number), 0).astype(jnp.float32)
    entry = lax.broadcasted_iota(jnp.int32, (8, BLOCK), 1).astype(jnp.float32)
    high_iota = lax.broadcasted_iota(jnp.int32, (PRE * 8, BLOCK), 0).astype(jnp.float32)
    low_iota = lax.broadcasted_iota(jnp.int32, (128, BLOCK), 0).astype(jnp.float32)
    for pair in range(PAIRS):
        step, local = pair // rows_ref.shape[1], pair % rows_ref.shape[1]
        rows = rows_ref[step, local]
        source = rows >> 10
        relative = ((((source >> 1) - (me_pre >> 1) + 1) & 3) << 1) | ((source ^ me_pre) & 1)
        high = ((relative << 3) | ((rows >> 7) & 7)).astype(jnp.float32).astype(jnp.bfloat16)
        low = (rows & 127).astype(jnp.float32).astype(jnp.bfloat16)
        owned = jnp.where(owner_ref[step, local : local + 1, :] == me_tp, 1.0, 0.0)
        rank = jnp.dot(owned.astype(jnp.bfloat16), before, preferred_element_type=jnp.float32)
        choose = jnp.where(slot == rank, owned, 0.0)
        limit = jnp.sum(choose * count_ref[step, local : local + 1, :].astype(jnp.float32), axis=1, keepdims=True)
        choose = choose.astype(jnp.bfloat16)
        valid = entry < limit
        high = jnp.where(valid, jnp.dot(choose, high, preferred_element_type=jnp.float32), -1.0)
        low = jnp.dot(choose, low, preferred_element_type=jnp.float32)
        chosen = jnp.zeros((PRE * 8, 128), jnp.float32)
        for block in range(number // TP):
            high_one = jnp.where(high_iota == high[block : block + 1, :], 1.0, 0.0).astype(jnp.bfloat16)
            low_one = jnp.where(low_iota == low[block : block + 1, :], 1.0, 0.0).astype(jnp.bfloat16)
            chosen = chosen + lax.dot_general(high_one, low_one, NT, preferred_element_type=jnp.float32)
        for block in range(PRE):
            for part in range(8):
                mask_ref[block, pair : pair + 1, part * 128 : (part + 1) * 128] = chosen[
                    block * 8 + part : block * 8 + part + 1, :
                ]
    union = jnp.concatenate([jnp.max(mask_ref[block], axis=0, keepdims=True) for block in range(PRE)], axis=0)
    before = (
        lax.broadcasted_iota(jnp.int32, (128, 128), 0) < lax.broadcasted_iota(jnp.int32, (128, 128), 1)
    ).astype(jnp.float32).astype(jnp.bfloat16)
    carry = jnp.zeros((PRE, 1), jnp.float32)
    for part in range(8):
        piece = union[:, part * 128 : (part + 1) * 128]
        ahead = jnp.dot(piece.astype(jnp.bfloat16), before, preferred_element_type=jnp.float32) + carry
        pos_ref[:, part * 128 : (part + 1) * 128] = jnp.where(piece > 0.0, ahead, -1.0)
        carry = carry + jnp.sum(piece, axis=1, keepdims=True)
    total_ref[...] = jnp.broadcast_to(carry, (PRE, 128)).astype(jnp.int32)


def make_tables(block_rows, block_owner, block_count):
    return pl.pallas_call(
        table_kernel,
        out_shape=(
            jax.ShapeDtypeStruct((PRE, PAIRS, ROWS), jnp.float32),
            jax.ShapeDtypeStruct((PRE, ROWS), jnp.float32),
            jax.ShapeDtypeStruct((PRE, 128), jnp.int32),
        ),
        in_specs=[vmem()] * 3,
        out_specs=(vmem(), vmem(), vmem()),
        compiler_params=pltpu.CompilerParams(vmem_limit_bytes=8 << 20),
        cost_estimate=CHEAP,
        name="row_tables",
    )(block_rows, block_owner, block_count)


TOKEN = jax.ShapeDtypeStruct((8, 128), jnp.float32)


def token_kernel(*refs):
    refs[-1][...] = jnp.zeros(refs[-1].shape, jnp.float32)


def arrived(values):
    return pl.pallas_call(
        token_kernel,
        out_shape=TOKEN,
        in_specs=[pl.BlockSpec(memory_space=pl.ANY)] * len(values),
        out_specs=vmem(),
        compiler_params=pltpu.CompilerParams(vmem_limit_bytes=2 << 20),
        cost_estimate=CHEAP,
        name="arrived",
    )(*values)


def halves_kernel(forward_ref, backward_ref, *refs):
    top_ref, low_ref = refs[-2:]
    top_ref[...] = forward_ref[...]
    low_ref[...] = backward_ref[...]


def halves(forward, backward, earlier):
    half = (forward.shape[0] // 2, forward.shape[1])
    out = jax.ShapeDtypeStruct(half, forward.dtype)
    return pl.pallas_call(
        halves_kernel,
        grid=(1,),
        out_shape=(out, out),
        in_specs=[pl.BlockSpec(half, lambda part: (0, 0)), pl.BlockSpec(half, lambda part: (1, 0))]
        + [pl.BlockSpec(memory_space=pl.ANY)] * len(earlier),
        out_specs=(pl.BlockSpec(half, lambda part: (0, 0)),) * 2,
        compiler_params=pltpu.CompilerParams(vmem_limit_bytes=8 << 20),
        cost_estimate=CHEAP,
        name="halves",
    )(forward, backward, *earlier)


def pack_block(number, pieces, mask_row, pos_row, packed_ref, first_lane):
    slot = (lax.broadcasted_iota(jnp.int32, (PACK, ROWS), 0) + number * PACK).astype(jnp.float32)
    pick = jnp.where(slot == pos_row, 1.0, 0.0).astype(jnp.bfloat16)
    depth = KV // len(pieces)
    for order, piece in enumerate(pieces):
        packed = lax.dot_general(piece, pick, NT, preferred_element_type=jnp.float32)
        packed_ref[order * depth : (order + 1) * depth, first_lane : first_lane + PACK] = packed.astype(jnp.bfloat16)
    present = lax.dot_general(mask_row.astype(jnp.bfloat16), pick, NT, preferred_element_type=jnp.float32)
    return jnp.where(present > 0.5, 0.0, -jnp.inf)


def latent_parts(refs):
    half = KV // 2
    if len(refs) == 1:
        return [refs[0].at[pl.ds(0, half), :], refs[0].at[pl.ds(half + MIDDLE, half), :]]
    return [refs[0].at[pl.ds(0, half), :], refs[1].at[pl.ds(MIDDLE // 2, half), :]]


def pack_kernel(base, parts, unused_ref, mask_ref, pos_ref, *refs):
    packed_ref, absent_ref = refs[-2:]
    for block, number in enumerate(parts):
        pieces, refs = refs[:number], refs[number:]
        row = base + block
        absent_ref[:, block * PACK : (block + 1) * PACK] = pack_block(
            0, [part[...] for part in latent_parts(pieces)], mask_ref[row], pos_ref[row : row + 1, :], packed_ref,
            block * PACK,
        )


def pack(base, token, masks, positions, sources):
    parts = [len(pieces) for pieces in sources]
    rows = sum([list(pieces) for pieces in sources], [])

    def body(*refs):
        pack_kernel(base, parts, *refs)

    return pl.pallas_call(
        body,
        out_shape=(
            jax.ShapeDtypeStruct((KV, len(parts) * PACK), jnp.bfloat16),
            jax.ShapeDtypeStruct((PAIRS, len(parts) * PACK), jnp.float32),
        ),
        in_specs=[pl.BlockSpec(memory_space=pl.ANY)] + [vmem()] * (2 + len(rows)),
        out_specs=(vmem(), vmem()),
        compiler_params=pltpu.CompilerParams(vmem_limit_bytes=16 << 20),
        cost_estimate=CHEAP,
        name="pack_%d" % len(parts),
    )(token, masks, positions, *rows)


def attend_kernel(base, parts, shapes, first, last, count_ref, mask_ref, pos_ref, *refs):
    queries, refs = refs[: shapes[0]], refs[shapes[0] :]
    packs, refs = refs[: 2 * shapes[1]], refs[2 * shapes[1] :]
    sources = []
    for number in parts:
        sources.append(refs[:number])
        refs = refs[number:]
    groups = len(queries)
    if not first:
        former_state, refs = refs[: 2 * groups], refs[2 * groups :]
    if last:
        outs, refs = refs[:groups], refs[groups:]
    state, refs = refs[: 2 * groups], refs[2 * groups :]
    if not last:
        refs[0][...] = jnp.zeros(refs[0].shape, jnp.float32)
        refs = refs[1:]
    packed_ref, rows_ref, sem = refs
    column = lax.broadcasted_iota(jnp.int32, (QTILE, STAT), 1)

    def attention(packed, absent, fresh):
        span = absent.shape[1]
        for group in range(groups):
            stat_ref, acc_ref = state[2 * group], state[2 * group + 1]
            query = queries[group][...]
            scores = [jnp.dot(query, ref[...], preferred_element_type=jnp.float32) for ref in packed]
            scores = scores[0] if len(scores) == 1 else jnp.concatenate(scores, axis=1)
            scores = scores.reshape(QTILE // 64, PAIRS, HEADS, span) * SCORE_SCALE + absent[None, :, None, :]
            scores = scores.reshape(QTILE, span)
            newer = jnp.max(scores, axis=1, keepdims=True)
            if fresh and first:
                newer = jnp.maximum(newer, LOWEST)
            else:
                stats, acc = (former_state[2 * group], former_state[2 * group + 1]) if fresh else (stat_ref, acc_ref)
                former = stats[:, :1]
                newer = jnp.maximum(former, newer)
                decay = jnp.exp2(former - newer)
            weights = jnp.exp2(scores - newer)
            total = jnp.sum(weights, axis=1, keepdims=True)
            weights = weights.astype(jnp.bfloat16)
            added, start = None, 0
            for ref in packed:
                width = ref.shape[1]
                piece = lax.dot_general(
                    weights[:, start : start + width], ref[:LAT, :], NT, preferred_element_type=jnp.float32
                )
                added = piece if added is None else added + piece
                start += width
            if not (fresh and first):
                total = stats[:, STAT // 2 : STAT // 2 + 1] * decay + total
                added = acc[...] * decay + added
            acc_ref[...] = added
            stat_ref[...] = jnp.where(column < STAT // 2, newer, total)

    attention(packs[::2], jnp.concatenate([ref[...] for ref in packs[1::2]], axis=1), True)

    for block in range(len(parts)):
        row = base + block
        rounds = (count_ref[row, 0] + (PACK - 1)) // PACK

        @pl.when(rounds > 1)
        def _(block=block, row=row, rounds=rounds):
            for order, piece in enumerate(latent_parts(sources[block])):
                copy = pltpu.make_async_copy(piece, rows_ref.at[pl.ds(order * (KV // 2), KV // 2), :], sem)
                copy.start()
                copy.wait()

            @pl.loop(1, rounds)
            def _(number):
                absent = pack_block(
                    number, [rows_ref[...]], mask_ref[row], pos_ref[row : row + 1, :], packed_ref, 0
                )
                attention([packed_ref], absent, False)

    if last:
        for group in range(groups):
            stat_ref, acc_ref = state[2 * group], state[2 * group + 1]
            write_payload(outs[group], stat_ref[:, :1], stat_ref[:, STAT // 2 : STAT // 2 + 1], acc_ref[...])


def write_payload(out_ref, highest, total, acc):
    lane = lax.broadcasted_iota(jnp.int32, (acc.shape[0], STAT), 1)
    out_ref[:, :LAT] = acc.astype(jnp.bfloat16)
    out_ref[:, LAT:] = (split_three(highest, lane, 0) + split_three(total, lane, 3)).astype(jnp.bfloat16)


def attend(base, counts, queries, masks, positions, packs, sources, states=None, last=False):
    parts = [len(pieces) for pieces in sources]
    first = states is None
    groups = len(queries)
    shapes = (
        jax.ShapeDtypeStruct((QTILE, STAT), jnp.float32),
        jax.ShapeDtypeStruct((QTILE, LAT), jnp.float32),
    ) * groups
    if last:
        out_shape = (jax.ShapeDtypeStruct((QTILE, LAT + STAT), jnp.bfloat16),) * groups
        scratch = [pltpu.VMEM(s.shape, s.dtype) for s in shapes]
    else:
        out_shape = shapes + (TOKEN,)
        scratch = []
    scratch = scratch + [
        pltpu.VMEM((KV, PACK), jnp.bfloat16),
        pltpu.VMEM((KV, ROWS), jnp.bfloat16),
        pltpu.SemaphoreType.DMA(()),
    ]
    packed = sum([list(pair) for pair in packs], [])
    rows = [pltpu.with_memory_space_constraint(piece, pltpu.HBM) for pieces in sources for piece in pieces]
    former = [] if first else [part for state in states for part in state]

    def body(*refs):
        attend_kernel(base, parts, (groups, len(packs)), first, last, *refs)

    in_specs = [smem()] + [vmem()] * (2 + groups + len(packed))
    in_specs = in_specs + [pl.BlockSpec(memory_space=pl.ANY)] * len(rows) + [vmem()] * len(former)
    outs = pl.pallas_call(
        body,
        out_shape=out_shape,
        in_specs=in_specs,
        out_specs=(vmem(),) * len(out_shape),
        scratch_shapes=scratch,
        compiler_params=pltpu.CompilerParams(vmem_limit_bytes=16 << 20),
        cost_estimate=CHEAP,
        name="attend_%d_%d" % (len(parts), groups),
    )(counts, masks, positions, *queries, *packed, *rows, *former)
    if last:
        return list(outs)
    return [tuple(outs[2 * group : 2 * group + 2]) for group in range(groups)], outs[-1]


def combined(refs):
    row = lax.broadcasted_iota(jnp.int32, (STAT, 2 * STAT), 0)
    col = lax.broadcasted_iota(jnp.int32, (STAT, 2 * STAT), 1)
    spread = jnp.where((row // 3) == (col // STAT), 1.0, 0.0).astype(jnp.bfloat16)
    stats = [jnp.dot(ref[:, LAT:], spread, preferred_element_type=jnp.float32) for ref in refs]
    highest = stats[0][:, :STAT]
    for stat in stats[1:]:
        highest = jnp.maximum(highest, stat[:, :STAT])
    total, acc = None, None
    for ref, stat in zip(refs, stats):
        weight = jnp.exp2(stat[:, :STAT] - highest)
        wide = jnp.concatenate([weight] * (LAT // STAT), axis=1) * ref[:, :LAT].astype(jnp.float32)
        total = weight * stat[:, STAT:] if total is None else total + weight * stat[:, STAT:]
        acc = wide if acc is None else acc + wide
    return highest, total, acc


def combine_kernel(*refs):
    highest, total, acc = combined(refs[:4])
    for part, out_ref in enumerate(refs[4:]):
        here = slice(part * PAIRS * HEADS, (part + 1) * PAIRS * HEADS)
        write_payload(out_ref, highest[here, :1], total[here, :1], acc[here, :])


def combine(parts):
    return pl.pallas_call(
        combine_kernel,
        out_shape=(jax.ShapeDtypeStruct((PAIRS * HEADS, LAT + STAT), jnp.bfloat16),) * 4,
        in_specs=[vmem()] * 4,
        out_specs=(vmem(),) * 4,
        compiler_params=pltpu.CompilerParams(vmem_limit_bytes=8 << 20),
        cost_estimate=CHEAP,
        name="combine",
    )(*parts)


def project_kernel(value_ref, weights, *refs):
    sums, received, out_ref = refs[:4], refs[4:8], refs[8]
    highest, total, acc = combined(received)
    attn = (acc / jnp.concatenate([total] * (LAT // STAT), axis=1)).astype(jnp.bfloat16)
    head_of = lax.broadcasted_iota(jnp.int32, (PAIRS, HEADS, 128), 1)
    pieces = []
    for head in range(HEADS):
        product = jnp.dot(attn, value_ref[head], preferred_element_type=jnp.float32)
        product = jnp.where(head_of == head, product.reshape(PAIRS, HEADS, 128), 0.0)
        pieces.append(jnp.sum(product, axis=1))
    values = jnp.concatenate(pieces, axis=1).astype(jnp.bfloat16)
    width = weights.shape[1]
    result = jnp.dot(values, weights[...], preferred_element_type=jnp.float32)
    out_ref[:, :width] = result.astype(jnp.bfloat16)
    lane = lax.broadcasted_iota(jnp.int32, (PAIRS, STAT), 1)
    group = lax.axis_index("pre")
    mine = [jnp.sum(jnp.where(lane == group, ref[...], 0.0), axis=1, keepdims=True) for ref in sums]
    mine = log_add(log_add(mine[0], mine[3]), log_add(mine[1], mine[2]))
    out_ref[:, width:] = split_three(mine, lane, 0).astype(jnp.bfloat16)


def project(received, value_proj, out_proj, sums):
    return pl.pallas_call(
        project_kernel,
        out_shape=jax.ShapeDtypeStruct((PAIRS, out_proj.shape[1] + STAT), jnp.bfloat16),
        in_specs=[vmem()] * (2 + len(sums) + len(received)),
        out_specs=vmem(),
        compiler_params=pltpu.CompilerParams(vmem_limit_bytes=16 << 20),
        cost_estimate=CHEAP,
        name="project",
    )(value_proj, pltpu.with_memory_space_constraint(out_proj, pltpu.VMEM), *sums, *received)


def index_kernel(chips, first_keys, second_keys, unused_ref, *refs):
    place = lax.axis_index("pre")
    former_ref, middles, out_ref, slab_ref = refs[0], refs[1:-2], refs[-2], refs[-1]
    lane = lax.broadcasted_iota(jnp.int32, (PAIRS, 128), 1)
    result = former_ref[...]
    for chip in chips:
        uses, middles = middles[: 1 if chip < 2 else 2], middles[1 if chip < 2 else 2 :]
        middle = uses[0][...] if chip < 2 else jnp.concatenate([part[...] for part in uses], axis=0)
        for pair in range(PAIRS):
            slab_ref[pair * 64 : (pair + 1) * 64, :] = middle[:64, pair * IDX : (pair + 1) * IDX]
        gates = middle[64:80, :64].astype(jnp.float32)
        lines = [jnp.concatenate([gates[2 * line : 2 * line + 1], gates[2 * line + 1 : 2 * line + 2]], axis=1) for line in range(4)]
        columns = jnp.concatenate(lines + [jnp.zeros((124, 128), jnp.float32)], axis=0).T
        group = (((place >> 1) + chip) & 3) * 2 + (place & 1)
        sums = []
        for keys in (first_keys, second_keys):
            scores = []
            for part in range(4):
                logits = lax.dot_general(
                    slab_ref[part * 128 : (part + 1) * 128, :], keys[...], NT, preferred_element_type=jnp.float32
                )
                gated = jnp.maximum(logits, 0.0) * columns[:, part : part + 1]
                scores.append(jnp.sum(gated.reshape(2, 64, ROWS), axis=1))
            scores = jnp.concatenate(scores, axis=0) * IDX ** (-0.5)
            largest = jnp.max(scores, axis=1, keepdims=True)
            sums.append(largest + jnp.log(jnp.sum(jnp.exp(scores - largest), axis=1, keepdims=True)))
        result = jnp.where(lane == group, log_add(sums[0], sums[1]), result)
    out_ref[...] = result


def index_partial(chips, keys, token, former, blocks):
    specs, args = [], []
    for parts in blocks:
        if len(parts) == 1:
            specs.append(pl.BlockSpec((MIDDLE, ROWS), lambda part: (3, 0)))
        else:
            specs.append(pl.BlockSpec((MIDDLE // 2, ROWS), lambda part: (6, 0)))
            specs.append(pl.BlockSpec((MIDDLE // 2, ROWS), lambda part: (0, 0)))
        args += list(parts)

    def body(*refs):
        index_kernel(chips, *refs)

    whole = pl.BlockSpec(keys[0].shape, lambda part: (0, 0))
    small = pl.BlockSpec((PAIRS, 128), lambda part: (0, 0))
    return pl.pallas_call(
        body,
        grid=(1,),
        out_shape=jax.ShapeDtypeStruct((PAIRS, 128), jnp.float32),
        in_specs=[whole, whole, pl.BlockSpec(memory_space=pl.ANY), small] + specs,
        out_specs=small,
        scratch_shapes=[pltpu.VMEM((PAIRS * 64, IDX), jnp.bfloat16)],
        compiler_params=pltpu.CompilerParams(vmem_limit_bytes=16 << 20),
        cost_estimate=CHEAP,
        name="index_partial_%d" % len(chips),
    )(*keys, token, former, *args)


def log_add(one, two):
    top = jnp.maximum(one, two)
    return top + jnp.log(jnp.exp(one - top) + jnp.exp(two - top))


def split_three(value, lane, start):
    pieces = jnp.zeros(lane.shape, jnp.float32)
    for step in range(3):
        piece = value.astype(jnp.bfloat16).astype(jnp.float32)
        pieces = jnp.where(lane == start + step, piece, pieces)
        value = value - piece
    return pieces


def join_three(pieces, start):
    wide = pieces.astype(jnp.float32)
    return wide[:, start : start + 1] + wide[:, start + 1 : start + 2] + wide[:, start + 2 : start + 3]


def four_sum(refs):
    width = refs[0].shape[1] - STAT
    parts = [ref[:, :width].astype(jnp.float32) for ref in refs]
    logs = [join_three(ref[:, width:], 0) for ref in refs]
    return (parts[0] + parts[1]) + (parts[2] + parts[3]), log_add(log_add(logs[0], logs[1]), log_add(logs[2], logs[3]))


def middle_kernel(own_ref, far_ref, right_ref, left_ref, out_ref):
    summed, logs = four_sum((own_ref, far_ref, right_ref, left_ref))
    width = summed.shape[1]
    out_ref[:, :width] = summed.astype(jnp.bfloat16)
    lane = lax.broadcasted_iota(jnp.int32, (PAIRS, STAT), 1)
    out_ref[:, width:] = split_three(logs, lane, 0).astype(jnp.bfloat16)


def final_kernel(own_ref, far_ref, right_ref, left_ref, out_ref, log_ref):
    summed, logs = four_sum((own_ref, far_ref, right_ref, left_ref))
    steps, local = log_ref.shape
    flat = jnp.broadcast_to(logs, (PAIRS, STAT)).T[:1, :]
    for step in range(steps):
        out_ref[step] = summed[step * local : (step + 1) * local, :].astype(jnp.bfloat16)
        log_ref[step : step + 1, :] = flat[:, step * local : (step + 1) * local]


def summed_over(value, shift, final):
    parts = (value,) + tuple(lax.ppermute(value, BOTH, shift(step)) for step in (2, 1, 3))
    if final:
        out_shape = (
            jax.ShapeDtypeStruct(final + (value.shape[1] - STAT,), jnp.bfloat16),
            jax.ShapeDtypeStruct(final, jnp.float32),
        )
        out_specs = (vmem(), vmem())
    else:
        out_shape = jax.ShapeDtypeStruct(value.shape, jnp.bfloat16)
        out_specs = vmem()
    return pl.pallas_call(
        final_kernel if final else middle_kernel,
        out_shape=out_shape,
        in_specs=[vmem()] * 4,
        out_specs=out_specs,
        compiler_params=pltpu.CompilerParams(vmem_limit_bytes=4 << 20),
        cost_estimate=CHEAP,
        name="sum_last" if final else "sum_first",
    )(*parts)


def prepare_kernel(latent_ref, query_ref, gate_ref, key_ref, block_ref, key_out_ref, latent, queries, gates, keys, sems):
    depth = KV // CHUNKS
    copies = [
        pltpu.make_async_copy(
            latent_ref.at[pl.ds(part * depth, depth)], latent.at[pl.ds(part * depth, depth)], sems.at[part]
        )
        for part in range(CHUNKS)
    ]
    others = [
        pltpu.make_async_copy(query_ref, queries, sems.at[CHUNKS]),
        pltpu.make_async_copy(gate_ref, gates, sems.at[CHUNKS + 1]),
        pltpu.make_async_copy(key_ref, keys, sems.at[CHUNKS + 2]),
    ]
    for copy in copies + others:
        copy.start()
    for part, copy in enumerate(copies):
        copy.wait()
        start = part * depth + (MIDDLE if part >= CHUNKS // 2 else 0)
        block_ref[start : start + depth, :] = latent[part * depth : (part + 1) * depth, :].astype(jnp.bfloat16)
    for copy in others:
        copy.wait()
    first = KV // 2
    block_ref[first + 64 : first + MIDDLE, :] = jnp.zeros((MIDDLE - 64, ROWS), jnp.bfloat16)
    lines = []
    for step in range(query_ref.shape[0]):
        for local in range(query_ref.shape[1]):
            pair = step * query_ref.shape[1] + local
            block_ref[first : first + 64, pair * IDX : (pair + 1) * IDX] = queries[step, local]
            lines.append(gates[step, local : local + 1, :].astype(jnp.float32))
    lines = jnp.concatenate(lines + [jnp.zeros((8, 64), jnp.float32)], axis=0)
    block_ref[first + 64 : first + 80, :64] = lines.astype(jnp.bfloat16)
    key_out_ref[...] = keys[...].astype(jnp.bfloat16)


def prepare(latent, index_queries, index_gates, index_keys):
    args = (latent, index_queries, index_gates, index_keys)
    return pl.pallas_call(
        prepare_kernel,
        out_shape=(
            jax.ShapeDtypeStruct((WIDE, ROWS), jnp.bfloat16),
            jax.ShapeDtypeStruct(index_keys.shape, jnp.bfloat16),
        ),
        in_specs=[pl.BlockSpec(memory_space=pl.ANY)] * 4,
        out_specs=(vmem(), vmem()),
        scratch_shapes=[pltpu.VMEM(arg.shape, arg.dtype) for arg in args] + [pltpu.SemaphoreType.DMA((CHUNKS + 3,))],
        compiler_params=pltpu.CompilerParams(vmem_limit_bytes=12 << 20),
        cost_estimate=CHEAP,
        name="prepare",
    )(*[pltpu.with_memory_space_constraint(arg, pltpu.HBM) for arg in args])


def x_shift(step):
    return [(x * 2 + c, ((x + step) % 4) * 2 + c) for x in range(4) for c in range(2)]


BOTH = ("pre", "tp")


def plane_shift(step, along_y):
    pairs = []
    for p in range(PRE):
        for z in range(4):
            for y in range(4):
                to_y = along_y == (p % 2 == 0)
                there = z * 4 + (y + step) % 4 if to_y else ((z + step) % 4) * 4 + y
                pairs.append((p * TP + z * 4 + y, p * TP + there))
    return pairs


def first_shift(step):
    return plane_shift(step, True)


def second_shift(step):
    return plane_shift(step, False)


CORE_SWAP = [(i, i ^ 1) for i in range(PRE)]


def on_device(
    latent_rows,
    index_keys,
    queries,
    index_queries,
    index_gates,
    value_proj,
    out_proj,
    block_rows,
    block_owner,
    block_count,
):
    block, keys = prepare(latent_rows.T, index_queries, index_gates, index_keys)
    forward = lax.ppermute(block, "pre", x_shift(1))
    backward = lax.ppermute(block, "pre", x_shift(3))

    own_queries = queries.reshape(PAIRS * HEADS, KV)
    row = jnp.concatenate(
        [own_queries] + [lax.ppermute(own_queries, BOTH, first_shift(4 - step)) for step in (1, 2, 3)], axis=0
    )
    def swapped(part):
        return lax.ppermute(part, "pre", CORE_SWAP)

    def both(parts):
        return [list(parts), [swapped(part) for part in parts]]

    masks, positions, counts = make_tables(block_rows, block_owner, block_count)
    own = both([block])
    own_pack = pack(2, masks, masks, positions, own)

    token = arrived([row, own_pack[0], keys])
    forward, backward, keys, token = lax.optimization_barrier((forward, backward, keys, token))
    sides = both([forward]) + both([backward])
    keys = [keys, swapped(keys)]
    top, low = halves(forward, backward, [sides[1][0], sides[3][0], keys[1]])
    top, low, row = lax.optimization_barrier((top, low, row))
    far = [lax.ppermute(top, "pre", x_shift(1)), lax.ppermute(low, "pre", x_shift(3))]
    plane = [row] + [lax.ppermute(row, BOTH, second_shift(4 - step)) for step in (1, 2, 3)]

    side_packs = [
        pack(base, early, masks, positions, rows) for base, early, rows in ((0, keys[1], sides[:2]), (4, token, sides[2:]))
    ]
    packs = [side_packs[0], own_pack, side_packs[1]]
    partial = index_partial((0, 1, -1), keys, side_packs[1][0], token, (own[0], sides[2], sides[0]))
    sums = [partial, lax.ppermute(partial, "pre", x_shift(1)), lax.ppermute(partial, "pre", x_shift(3))]
    far, sums, token = lax.optimization_barrier((far, sums, arrived(plane[1:])))
    partial = sums[0]
    far = both(far)
    packs.append(pack(6, token, masks, positions, far))

    rows = sides[:2] + own + sides[2:] + far
    payloads = [None] * 4
    parts = [None] * 4
    for step in (1, 3, 2, 0):
        payloads[step] = attend(0, counts, plane[step : step + 1], masks, positions, packs, rows, last=True)[0]
        parts[step] = lax.ppermute(payloads[step], BOTH, second_shift(step)) if step else payloads[0]
    parts = combine(parts)
    received = [parts[0]] + [lax.ppermute(parts[step], BOTH, first_shift(step)) for step in (2, 1, 3)]
    partial = index_partial((2,), keys, payloads[3], token, (far[0],))
    sums.append(lax.ppermute(partial, "pre", x_shift(2)))
    part_out = project(received, value_proj, out_proj, sums)
    return summed_over(summed_over(part_out, first_shift, None), second_shift, queries.shape[:2])


def solution(mesh):
    placed = (
        P(("pre", "tp"), None),
        P(("pre", "tp"), None),
        P(None, "pre", "tp", None),
        P(None, "pre", None, None),
        P(None, "pre", None),
        P("tp", None, None),
        P("tp", None),
        P(None, "pre", None, None),
        P(None, "pre", None),
        P(None, "pre", None),
    )
    return jax.shard_map(
        on_device,
        mesh=mesh,
        in_specs=placed,
        out_specs=(P(None, "pre", None), P(None, "pre")),
        check_vma=False,
    )
```

```python
import jax
import jax.numpy as jnp
from jax import lax
from jax.experimental import pallas as pl
from jax.experimental.pallas import tpu as pltpu
from jax.sharding import PartitionSpec as P

IDX = 128
LAT = 512
KV = 576
BLOCK = 64
PRE = 8
TP = 16
PAIRS = 8
HEADS = 8
ROWS = 1024
PACK = 256
MIDDLE = 96
WIDE = KV + MIDDLE
CHUNKS = 6
QTILE = 256
STAT = 128
QROWS = TP * PAIRS * HEADS
LOWEST = -3.0e38
SOFT_SCALE = 192.0 ** (-0.5)
LOG2E = 1.4426950408889634
SCORE_SCALE = SOFT_SCALE * LOG2E

NT = (((1,), (1,)), ((), ()))


CHEAP = pl.CostEstimate(flops=1000, bytes_accessed=1000, transcendentals=0)


def vmem():
    return pl.BlockSpec(memory_space=pltpu.VMEM)


def smem():
    return pl.BlockSpec(memory_space=pltpu.SMEM)


def table_kernel(rows_ref, owner_ref, count_ref, mask_ref, pos_ref, total_ref):
    me_pre = lax.axis_index("pre")
    me_tp = lax.axis_index("tp")
    number = rows_ref.shape[2]
    before = (
        lax.broadcasted_iota(jnp.int32, (number, number), 0) < lax.broadcasted_iota(jnp.int32, (number, number), 1)
    ).astype(jnp.float32).astype(jnp.bfloat16)
    slot = lax.broadcasted_iota(jnp.int32, (8, number), 0).astype(jnp.float32)
    entry = lax.broadcasted_iota(jnp.int32, (8, BLOCK), 1).astype(jnp.float32)
    high_iota = lax.broadcasted_iota(jnp.int32, (PRE * 8, BLOCK), 0).astype(jnp.float32)
    low_iota = lax.broadcasted_iota(jnp.int32, (128, BLOCK), 0).astype(jnp.float32)
    for pair in range(PAIRS):
        step, local = pair // rows_ref.shape[1], pair % rows_ref.shape[1]
        rows = rows_ref[step, local]
        source = rows >> 10
        relative = ((((source >> 1) - (me_pre >> 1) + 1) & 3) << 1) | ((source ^ me_pre) & 1)
        high = ((relative << 3) | ((rows >> 7) & 7)).astype(jnp.float32).astype(jnp.bfloat16)
        low = (rows & 127).astype(jnp.float32).astype(jnp.bfloat16)
        owned = jnp.where(owner_ref[step, local : local + 1, :] == me_tp, 1.0, 0.0)
        rank = jnp.dot(owned.astype(jnp.bfloat16), before, preferred_element_type=jnp.float32)
        choose = jnp.where(slot == rank, owned, 0.0)
        limit = jnp.sum(choose * count_ref[step, local : local + 1, :].astype(jnp.float32), axis=1, keepdims=True)
        choose = choose.astype(jnp.bfloat16)
        valid = entry < limit
        high = jnp.where(valid, jnp.dot(choose, high, preferred_element_type=jnp.float32), -1.0)
        low = jnp.dot(choose, low, preferred_element_type=jnp.float32)
        chosen = jnp.zeros((PRE * 8, 128), jnp.float32)
        for block in range(number // TP):
            high_one = jnp.where(high_iota == high[block : block + 1, :], 1.0, 0.0).astype(jnp.bfloat16)
            low_one = jnp.where(low_iota == low[block : block + 1, :], 1.0, 0.0).astype(jnp.bfloat16)
            chosen = chosen + lax.dot_general(high_one, low_one, NT, preferred_element_type=jnp.float32)
        for block in range(PRE):
            for part in range(8):
                mask_ref[block, pair : pair + 1, part * 128 : (part + 1) * 128] = chosen[
                    block * 8 + part : block * 8 + part + 1, :
                ]
    union = jnp.concatenate([jnp.max(mask_ref[block], axis=0, keepdims=True) for block in range(PRE)], axis=0)
    before = (
        lax.broadcasted_iota(jnp.int32, (128, 128), 0) < lax.broadcasted_iota(jnp.int32, (128, 128), 1)
    ).astype(jnp.float32).astype(jnp.bfloat16)
    carry = jnp.zeros((PRE, 1), jnp.float32)
    for part in range(8):
        piece = union[:, part * 128 : (part + 1) * 128]
        ahead = jnp.dot(piece.astype(jnp.bfloat16), before, preferred_element_type=jnp.float32) + carry
        pos_ref[:, part * 128 : (part + 1) * 128] = jnp.where(piece > 0.0, ahead, -1.0)
        carry = carry + jnp.sum(piece, axis=1, keepdims=True)
    total_ref[...] = jnp.broadcast_to(carry, (PRE, 128)).astype(jnp.int32)


def make_tables(block_rows, block_owner, block_count):
    return pl.pallas_call(
        table_kernel,
        out_shape=(
            jax.ShapeDtypeStruct((PRE, PAIRS, ROWS), jnp.float32),
            jax.ShapeDtypeStruct((PRE, ROWS), jnp.float32),
            jax.ShapeDtypeStruct((PRE, 128), jnp.int32),
        ),
        in_specs=[vmem()] * 3,
        out_specs=(vmem(), vmem(), vmem()),
        compiler_params=pltpu.CompilerParams(vmem_limit_bytes=8 << 20),
        cost_estimate=CHEAP,
        name="row_tables",
    )(block_rows, block_owner, block_count)


TOKEN = jax.ShapeDtypeStruct((8, 128), jnp.float32)


def token_kernel(*refs):
    refs[-1][...] = jnp.zeros(refs[-1].shape, jnp.float32)


def arrived(values):
    return pl.pallas_call(
        token_kernel,
        out_shape=TOKEN,
        in_specs=[pl.BlockSpec(memory_space=pl.ANY)] * len(values),
        out_specs=vmem(),
        compiler_params=pltpu.CompilerParams(vmem_limit_bytes=2 << 20),
        cost_estimate=CHEAP,
        name="arrived",
    )(*values)


def halves_kernel(forward_ref, backward_ref, top_ref, low_ref):
    top_ref[...] = forward_ref[...]
    low_ref[...] = backward_ref[...]


def halves(forward, backward):
    half = (forward.shape[0] // 2, forward.shape[1])
    out = jax.ShapeDtypeStruct(half, forward.dtype)
    return pl.pallas_call(
        halves_kernel,
        grid=(1,),
        out_shape=(out, out),
        in_specs=[pl.BlockSpec(half, lambda part: (0, 0)), pl.BlockSpec(half, lambda part: (1, 0))],
        out_specs=(pl.BlockSpec(half, lambda part: (0, 0)),) * 2,
        compiler_params=pltpu.CompilerParams(vmem_limit_bytes=8 << 20),
        cost_estimate=CHEAP,
        name="halves",
    )(forward, backward)


def pack_block(number, pieces, mask_row, pos_row, packed_ref, first_lane):
    slot = (lax.broadcasted_iota(jnp.int32, (PACK, ROWS), 0) + number * PACK).astype(jnp.float32)
    pick = jnp.where(slot == pos_row, 1.0, 0.0).astype(jnp.bfloat16)
    depth = KV // len(pieces)
    for order, piece in enumerate(pieces):
        packed = lax.dot_general(piece, pick, NT, preferred_element_type=jnp.float32)
        packed_ref[order * depth : (order + 1) * depth, first_lane : first_lane + PACK] = packed.astype(jnp.bfloat16)
    present = lax.dot_general(mask_row.astype(jnp.bfloat16), pick, NT, preferred_element_type=jnp.float32)
    return jnp.where(present > 0.5, 0.0, -jnp.inf)


def latent_parts(refs):
    half = KV // 2
    if len(refs) == 1:
        return [refs[0].at[pl.ds(0, half), :], refs[0].at[pl.ds(half + MIDDLE, half), :]]
    return [refs[0].at[pl.ds(0, half), :], refs[1].at[pl.ds(MIDDLE // 2, half), :]]


def pack_kernel(base, parts, unused_ref, mask_ref, pos_ref, *refs):
    packed_ref, absent_ref = refs[-2:]
    for block, number in enumerate(parts):
        pieces, refs = refs[:number], refs[number:]
        row = base + block
        absent_ref[:, block * PACK : (block + 1) * PACK] = pack_block(
            0, [part[...] for part in latent_parts(pieces)], mask_ref[row], pos_ref[row : row + 1, :], packed_ref,
            block * PACK,
        )


def pack(base, token, masks, positions, sources):
    parts = [len(pieces) for pieces in sources]
    rows = sum([list(pieces) for pieces in sources], [])

    def body(*refs):
        pack_kernel(base, parts, *refs)

    return pl.pallas_call(
        body,
        out_shape=(
            jax.ShapeDtypeStruct((KV, len(parts) * PACK), jnp.bfloat16),
            jax.ShapeDtypeStruct((PAIRS, len(parts) * PACK), jnp.float32),
        ),
        in_specs=[pl.BlockSpec(memory_space=pl.ANY)] + [vmem()] * (2 + len(rows)),
        out_specs=(vmem(), vmem()),
        compiler_params=pltpu.CompilerParams(vmem_limit_bytes=16 << 20),
        cost_estimate=CHEAP,
        name="pack_%d" % len(parts),
    )(token, masks, positions, *rows)


def attend_kernel(base, parts, shapes, first, last, count_ref, mask_ref, pos_ref, *refs):
    queries, refs = refs[: shapes[0]], refs[shapes[0] :]
    packs, refs = refs[: 2 * shapes[1]], refs[2 * shapes[1] :]
    sources = []
    for number in parts:
        sources.append(refs[:number])
        refs = refs[number:]
    groups = len(queries)
    if not first:
        former_state, refs = refs[: 2 * groups], refs[2 * groups :]
    if last:
        outs, refs = refs[:groups], refs[groups:]
    state, refs = refs[: 2 * groups], refs[2 * groups :]
    if not last:
        refs[0][...] = jnp.zeros(refs[0].shape, jnp.float32)
        refs = refs[1:]
    packed_ref, rows_ref, sem = refs
    column = lax.broadcasted_iota(jnp.int32, (QTILE, STAT), 1)

    def attention(packed, absent, fresh):
        span = absent.shape[1]
        for group in range(groups):
            stat_ref, acc_ref = state[2 * group], state[2 * group + 1]
            query = queries[group][...]
            scores = [jnp.dot(query, ref[...], preferred_element_type=jnp.float32) for ref in packed]
            scores = scores[0] if len(scores) == 1 else jnp.concatenate(scores, axis=1)
            scores = scores.reshape(QTILE // 64, PAIRS, HEADS, span) * SCORE_SCALE + absent[None, :, None, :]
            scores = scores.reshape(QTILE, span)
            newer = jnp.max(scores, axis=1, keepdims=True)
            if fresh and first:
                newer = jnp.maximum(newer, LOWEST)
            else:
                stats, acc = (former_state[2 * group], former_state[2 * group + 1]) if fresh else (stat_ref, acc_ref)
                former = stats[:, :1]
                newer = jnp.maximum(former, newer)
                decay = jnp.exp2(former - newer)
            weights = jnp.exp2(scores - newer)
            total = jnp.sum(weights, axis=1, keepdims=True)
            weights = weights.astype(jnp.bfloat16)
            added, start = None, 0
            for ref in packed:
                width = ref.shape[1]
                piece = lax.dot_general(
                    weights[:, start : start + width], ref[:LAT, :], NT, preferred_element_type=jnp.float32
                )
                added = piece if added is None else added + piece
                start += width
            if not (fresh and first):
                total = stats[:, STAT // 2 : STAT // 2 + 1] * decay + total
                added = acc[...] * decay + added
            acc_ref[...] = added
            stat_ref[...] = jnp.where(column < STAT // 2, newer, total)

    attention(packs[::2], jnp.concatenate([ref[...] for ref in packs[1::2]], axis=1), True)

    for block in range(len(parts)):
        row = base + block
        rounds = (count_ref[row, 0] + (PACK - 1)) // PACK

        @pl.when(rounds > 1)
        def _(block=block, row=row, rounds=rounds):
            for order, piece in enumerate(latent_parts(sources[block])):
                copy = pltpu.make_async_copy(piece, rows_ref.at[pl.ds(order * (KV // 2), KV // 2), :], sem)
                copy.start()
                copy.wait()

            @pl.loop(1, rounds)
            def _(number):
                absent = pack_block(
                    number, [rows_ref[...]], mask_ref[row], pos_ref[row : row + 1, :], packed_ref, 0
                )
                attention([packed_ref], absent, False)

    if last:
        for group in range(groups):
            stat_ref, acc_ref = state[2 * group], state[2 * group + 1]
            write_payload(outs[group], stat_ref[:, :1], stat_ref[:, STAT // 2 : STAT // 2 + 1], acc_ref[...])


def write_payload(out_ref, highest, total, acc):
    lane = lax.broadcasted_iota(jnp.int32, (acc.shape[0], STAT), 1)
    out_ref[:, :LAT] = acc.astype(jnp.bfloat16)
    out_ref[:, LAT:] = (split_three(highest, lane, 0) + split_three(total, lane, 3)).astype(jnp.bfloat16)


def attend(base, counts, queries, masks, positions, packs, sources, states=None, last=False):
    parts = [len(pieces) for pieces in sources]
    first = states is None
    groups = len(queries)
    shapes = (
        jax.ShapeDtypeStruct((QTILE, STAT), jnp.float32),
        jax.ShapeDtypeStruct((QTILE, LAT), jnp.float32),
    ) * groups
    if last:
        out_shape = (jax.ShapeDtypeStruct((QTILE, LAT + STAT), jnp.bfloat16),) * groups
        scratch = [pltpu.VMEM(s.shape, s.dtype) for s in shapes]
    else:
        out_shape = shapes + (TOKEN,)
        scratch = []
    scratch = scratch + [
        pltpu.VMEM((KV, PACK), jnp.bfloat16),
        pltpu.VMEM((KV, ROWS), jnp.bfloat16),
        pltpu.SemaphoreType.DMA(()),
    ]
    packed = sum([list(pair) for pair in packs], [])
    rows = [pltpu.with_memory_space_constraint(piece, pltpu.HBM) for pieces in sources for piece in pieces]
    former = [] if first else [part for state in states for part in state]

    def body(*refs):
        attend_kernel(base, parts, (groups, len(packs)), first, last, *refs)

    in_specs = [smem()] + [vmem()] * (2 + groups + len(packed))
    in_specs = in_specs + [pl.BlockSpec(memory_space=pl.ANY)] * len(rows) + [vmem()] * len(former)
    outs = pl.pallas_call(
        body,
        out_shape=out_shape,
        in_specs=in_specs,
        out_specs=(vmem(),) * len(out_shape),
        scratch_shapes=scratch,
        compiler_params=pltpu.CompilerParams(vmem_limit_bytes=16 << 20),
        cost_estimate=CHEAP,
        name="attend_%d_%d" % (len(parts), groups),
    )(counts, masks, positions, *queries, *packed, *rows, *former)
    if last:
        return list(outs)
    return [tuple(outs[2 * group : 2 * group + 2]) for group in range(groups)], outs[-1]


def combined(refs):
    row = lax.broadcasted_iota(jnp.int32, (STAT, 2 * STAT), 0)
    col = lax.broadcasted_iota(jnp.int32, (STAT, 2 * STAT), 1)
    spread = jnp.where((row // 3) == (col // STAT), 1.0, 0.0).astype(jnp.bfloat16)
    stats = [jnp.dot(ref[:, LAT:], spread, preferred_element_type=jnp.float32) for ref in refs]
    highest = stats[0][:, :STAT]
    for stat in stats[1:]:
        highest = jnp.maximum(highest, stat[:, :STAT])
    total, acc = None, None
    for ref, stat in zip(refs, stats):
        weight = jnp.exp2(stat[:, :STAT] - highest)
        wide = jnp.concatenate([weight] * (LAT // STAT), axis=1) * ref[:, :LAT].astype(jnp.float32)
        total = weight * stat[:, STAT:] if total is None else total + weight * stat[:, STAT:]
        acc = wide if acc is None else acc + wide
    return highest, total, acc


def combine_kernel(*refs):
    highest, total, acc = combined(refs[:4])
    for part, out_ref in enumerate(refs[4:]):
        here = slice(part * PAIRS * HEADS, (part + 1) * PAIRS * HEADS)
        write_payload(out_ref, highest[here, :1], total[here, :1], acc[here, :])


def combine(parts):
    return pl.pallas_call(
        combine_kernel,
        out_shape=(jax.ShapeDtypeStruct((PAIRS * HEADS, LAT + STAT), jnp.bfloat16),) * 4,
        in_specs=[vmem()] * 4,
        out_specs=(vmem(),) * 4,
        compiler_params=pltpu.CompilerParams(vmem_limit_bytes=8 << 20),
        cost_estimate=CHEAP,
        name="combine",
    )(*parts)


def project_kernel(value_ref, weights, *refs):
    sums, received, out_ref = refs[:4], refs[4:8], refs[8]
    highest, total, acc = combined(received)
    attn = (acc / jnp.concatenate([total] * (LAT // STAT), axis=1)).astype(jnp.bfloat16)
    head_of = lax.broadcasted_iota(jnp.int32, (PAIRS, HEADS, 128), 1)
    pieces = []
    for head in range(HEADS):
        product = jnp.dot(attn, value_ref[head], preferred_element_type=jnp.float32)
        product = jnp.where(head_of == head, product.reshape(PAIRS, HEADS, 128), 0.0)
        pieces.append(jnp.sum(product, axis=1))
    values = jnp.concatenate(pieces, axis=1).astype(jnp.bfloat16)
    width = weights.shape[1]
    result = jnp.dot(values, weights[...], preferred_element_type=jnp.float32)
    out_ref[:, :width] = result.astype(jnp.bfloat16)
    lane = lax.broadcasted_iota(jnp.int32, (PAIRS, STAT), 1)
    group = lax.axis_index("pre")
    mine = [jnp.sum(jnp.where(lane == group, ref[...], 0.0), axis=1, keepdims=True) for ref in sums]
    mine = log_add(log_add(mine[0], mine[3]), log_add(mine[1], mine[2]))
    out_ref[:, width:] = split_three(mine, lane, 0).astype(jnp.bfloat16)


def project(received, value_proj, out_proj, sums):
    return pl.pallas_call(
        project_kernel,
        out_shape=jax.ShapeDtypeStruct((PAIRS, out_proj.shape[1] + STAT), jnp.bfloat16),
        in_specs=[vmem()] * (2 + len(sums) + len(received)),
        out_specs=vmem(),
        compiler_params=pltpu.CompilerParams(vmem_limit_bytes=16 << 20),
        cost_estimate=CHEAP,
        name="project",
    )(value_proj, pltpu.with_memory_space_constraint(out_proj, pltpu.VMEM), *sums, *received)


def index_kernel(chips, first_keys, second_keys, unused_ref, *refs):
    place = lax.axis_index("pre")
    former_ref, middles, out_ref, slab_ref = refs[0], refs[1:-2], refs[-2], refs[-1]
    lane = lax.broadcasted_iota(jnp.int32, (PAIRS, 128), 1)
    result = former_ref[...]
    for chip in chips:
        uses, middles = middles[: 1 if chip < 2 else 2], middles[1 if chip < 2 else 2 :]
        middle = uses[0][...] if chip < 2 else jnp.concatenate([part[...] for part in uses], axis=0)
        for pair in range(PAIRS):
            slab_ref[pair * 64 : (pair + 1) * 64, :] = middle[:64, pair * IDX : (pair + 1) * IDX]
        gates = middle[64:80, :64].astype(jnp.float32)
        lines = [jnp.concatenate([gates[2 * line : 2 * line + 1], gates[2 * line + 1 : 2 * line + 2]], axis=1) for line in range(4)]
        columns = jnp.concatenate(lines + [jnp.zeros((124, 128), jnp.float32)], axis=0).T
        group = (((place >> 1) + chip) & 3) * 2 + (place & 1)
        sums = []
        for keys in (first_keys, second_keys):
            scores = []
            for part in range(4):
                logits = lax.dot_general(
                    slab_ref[part * 128 : (part + 1) * 128, :], keys[...], NT, preferred_element_type=jnp.float32
                )
                gated = jnp.maximum(logits, 0.0) * columns[:, part : part + 1]
                scores.append(jnp.sum(gated.reshape(2, 64, ROWS), axis=1))
            scores = jnp.concatenate(scores, axis=0) * IDX ** (-0.5)
            largest = jnp.max(scores, axis=1, keepdims=True)
            sums.append(largest + jnp.log(jnp.sum(jnp.exp(scores - largest), axis=1, keepdims=True)))
        result = jnp.where(lane == group, log_add(sums[0], sums[1]), result)
    out_ref[...] = result


def index_partial(chips, keys, token, former, blocks):
    specs, args = [], []
    for parts in blocks:
        if len(parts) == 1:
            specs.append(pl.BlockSpec((MIDDLE, ROWS), lambda part: (3, 0)))
        else:
            specs.append(pl.BlockSpec((MIDDLE // 2, ROWS), lambda part: (6, 0)))
            specs.append(pl.BlockSpec((MIDDLE // 2, ROWS), lambda part: (0, 0)))
        args += list(parts)

    def body(*refs):
        index_kernel(chips, *refs)

    whole = pl.BlockSpec(keys[0].shape, lambda part: (0, 0))
    small = pl.BlockSpec((PAIRS, 128), lambda part: (0, 0))
    return pl.pallas_call(
        body,
        grid=(1,),
        out_shape=jax.ShapeDtypeStruct((PAIRS, 128), jnp.float32),
        in_specs=[whole, whole, pl.BlockSpec(memory_space=pl.ANY), small] + specs,
        out_specs=small,
        scratch_shapes=[pltpu.VMEM((PAIRS * 64, IDX), jnp.bfloat16)],
        compiler_params=pltpu.CompilerParams(vmem_limit_bytes=16 << 20),
        cost_estimate=CHEAP,
        name="index_partial_%d" % len(chips),
    )(*keys, token, former, *args)


def log_add(one, two):
    top = jnp.maximum(one, two)
    return top + jnp.log(jnp.exp(one - top) + jnp.exp(two - top))


def split_three(value, lane, start):
    pieces = jnp.zeros(lane.shape, jnp.float32)
    for step in range(3):
        piece = value.astype(jnp.bfloat16).astype(jnp.float32)
        pieces = jnp.where(lane == start + step, piece, pieces)
        value = value - piece
    return pieces


def join_three(pieces, start):
    wide = pieces.astype(jnp.float32)
    return wide[:, start : start + 1] + wide[:, start + 1 : start + 2] + wide[:, start + 2 : start + 3]


def four_sum(refs):
    width = refs[0].shape[1] - STAT
    parts = [ref[:, :width].astype(jnp.float32) for ref in refs]
    logs = [join_three(ref[:, width:], 0) for ref in refs]
    return (parts[0] + parts[1]) + (parts[2] + parts[3]), log_add(log_add(logs[0], logs[1]), log_add(logs[2], logs[3]))


def middle_kernel(own_ref, far_ref, right_ref, left_ref, out_ref):
    summed, logs = four_sum((own_ref, far_ref, right_ref, left_ref))
    width = summed.shape[1]
    out_ref[:, :width] = summed.astype(jnp.bfloat16)
    lane = lax.broadcasted_iota(jnp.int32, (PAIRS, STAT), 1)
    out_ref[:, width:] = split_three(logs, lane, 0).astype(jnp.bfloat16)


def final_kernel(own_ref, far_ref, right_ref, left_ref, out_ref, log_ref):
    summed, logs = four_sum((own_ref, far_ref, right_ref, left_ref))
    steps, local = log_ref.shape
    flat = jnp.broadcast_to(logs, (PAIRS, STAT)).T[:1, :]
    for step in range(steps):
        out_ref[step] = summed[step * local : (step + 1) * local, :].astype(jnp.bfloat16)
        log_ref[step : step + 1, :] = flat[:, step * local : (step + 1) * local]


def summed_over(value, shift, final):
    parts = (value,) + tuple(lax.ppermute(value, BOTH, shift(step)) for step in (2, 1, 3))
    if final:
        out_shape = (
            jax.ShapeDtypeStruct(final + (value.shape[1] - STAT,), jnp.bfloat16),
            jax.ShapeDtypeStruct(final, jnp.float32),
        )
        out_specs = (vmem(), vmem())
    else:
        out_shape = jax.ShapeDtypeStruct(value.shape, jnp.bfloat16)
        out_specs = vmem()
    return pl.pallas_call(
        final_kernel if final else middle_kernel,
        out_shape=out_shape,
        in_specs=[vmem()] * 4,
        out_specs=out_specs,
        compiler_params=pltpu.CompilerParams(vmem_limit_bytes=4 << 20),
        cost_estimate=CHEAP,
        name="sum_last" if final else "sum_first",
    )(*parts)


def prepare_kernel(latent_ref, query_ref, gate_ref, key_ref, block_ref, key_out_ref, latent, queries, gates, keys, sems):
    depth = KV // CHUNKS
    copies = [
        pltpu.make_async_copy(
            latent_ref.at[pl.ds(part * depth, depth)], latent.at[pl.ds(part * depth, depth)], sems.at[part]
        )
        for part in range(CHUNKS)
    ]
    others = [
        pltpu.make_async_copy(query_ref, queries, sems.at[CHUNKS]),
        pltpu.make_async_copy(gate_ref, gates, sems.at[CHUNKS + 1]),
        pltpu.make_async_copy(key_ref, keys, sems.at[CHUNKS + 2]),
    ]
    for copy in copies + others:
        copy.start()
    for part, copy in enumerate(copies):
        copy.wait()
        start = part * depth + (MIDDLE if part >= CHUNKS // 2 else 0)
        block_ref[start : start + depth, :] = latent[part * depth : (part + 1) * depth, :].astype(jnp.bfloat16)
    for copy in others:
        copy.wait()
    first = KV // 2
    block_ref[first + 64 : first + MIDDLE, :] = jnp.zeros((MIDDLE - 64, ROWS), jnp.bfloat16)
    lines = []
    for step in range(query_ref.shape[0]):
        for local in range(query_ref.shape[1]):
            pair = step * query_ref.shape[1] + local
            block_ref[first : first + 64, pair * IDX : (pair + 1) * IDX] = queries[step, local]
            lines.append(gates[step, local : local + 1, :].astype(jnp.float32))
    lines = jnp.concatenate(lines + [jnp.zeros((8, 64), jnp.float32)], axis=0)
    block_ref[first + 64 : first + 80, :64] = lines.astype(jnp.bfloat16)
    key_out_ref[...] = keys[...].astype(jnp.bfloat16)


def prepare(latent, index_queries, index_gates, index_keys):
    args = (latent, index_queries, index_gates, index_keys)
    return pl.pallas_call(
        prepare_kernel,
        out_shape=(
            jax.ShapeDtypeStruct((WIDE, ROWS), jnp.bfloat16),
            jax.ShapeDtypeStruct(index_keys.shape, jnp.bfloat16),
        ),
        in_specs=[pl.BlockSpec(memory_space=pl.ANY)] * 4,
        out_specs=(vmem(), vmem()),
        scratch_shapes=[pltpu.VMEM(arg.shape, arg.dtype) for arg in args] + [pltpu.SemaphoreType.DMA((CHUNKS + 3,))],
        compiler_params=pltpu.CompilerParams(vmem_limit_bytes=12 << 20),
        cost_estimate=CHEAP,
        name="prepare",
    )(*[pltpu.with_memory_space_constraint(arg, pltpu.HBM) for arg in args])


def x_shift(step):
    return [(x * 2 + c, ((x + step) % 4) * 2 + c) for x in range(4) for c in range(2)]


BOTH = ("pre", "tp")


def plane_shift(step, along_y):
    pairs = []
    for p in range(PRE):
        for z in range(4):
            for y in range(4):
                to_y = along_y == (p % 2 == 0)
                there = z * 4 + (y + step) % 4 if to_y else ((z + step) % 4) * 4 + y
                pairs.append((p * TP + z * 4 + y, p * TP + there))
    return pairs


def first_shift(step):
    return plane_shift(step, True)


def second_shift(step):
    return plane_shift(step, False)


CORE_SWAP = [(i, i ^ 1) for i in range(PRE)]


def on_device(
    latent_rows,
    index_keys,
    queries,
    index_queries,
    index_gates,
    value_proj,
    out_proj,
    block_rows,
    block_owner,
    block_count,
):
    block, keys = prepare(latent_rows.T, index_queries, index_gates, index_keys)
    forward = lax.ppermute(block, "pre", x_shift(1))
    backward = lax.ppermute(block, "pre", x_shift(3))

    own_queries = queries.reshape(PAIRS * HEADS, KV)
    row = jnp.concatenate(
        [own_queries] + [lax.ppermute(own_queries, BOTH, first_shift(4 - step)) for step in (1, 2, 3)], axis=0
    )
    plane = [row] + [lax.ppermute(row, BOTH, second_shift(4 - step)) for step in (1, 2, 3)]

    def swapped(part):
        return lax.ppermute(part, "pre", CORE_SWAP)

    def both(parts):
        return [list(parts), [swapped(part) for part in parts]]

    masks, positions, counts = make_tables(block_rows, block_owner, block_count)
    token = arrived(plane[1:] + [masks])
    forward, backward, token = lax.optimization_barrier((forward, backward, token))
    top, low = halves(forward, backward)
    top, low, block, keys = lax.optimization_barrier((top, low, block, keys))
    far = [lax.ppermute(top, "pre", x_shift(1)), lax.ppermute(low, "pre", x_shift(3))]

    own, sides = both([block]), both([forward]) + both([backward])
    keys = [keys, swapped(keys)]
    packs = [
        pack(base, early, masks, positions, rows)
        for base, early, rows in ((0, keys[1], sides[:2]), (2, token, own), (4, token, sides[2:]))
    ]
    states, token = attend(0, counts, plane, masks, positions, packs, sides[:2] + own + sides[2:])
    partial = index_partial((0, 1, -1), keys, token, token, (own[0], sides[2], sides[0]))
    sums = [partial, lax.ppermute(partial, "pre", x_shift(1)), lax.ppermute(partial, "pre", x_shift(3))]
    far, sums = lax.optimization_barrier((far, sums))
    partial = sums[0]
    far = both(far)
    packs = [pack(6, partial, masks, positions, far)]

    payloads = attend(6, counts, plane[1:], masks, positions, packs, far, states[1:], last=True)
    parts = attend(6, counts, plane[:1], masks, positions, packs, far, states[:1], last=True)
    parts += [lax.ppermute(payloads[step - 1], BOTH, second_shift(step)) for step in (2, 1, 3)]
    parts = combine(parts)
    received = [parts[0]] + [lax.ppermute(parts[step], BOTH, first_shift(step)) for step in (2, 1, 3)]
    partial = index_partial((2,), keys, parts[0], token, (far[0],))
    sums.append(lax.ppermute(partial, "pre", x_shift(2)))
    part_out = project(received, value_proj, out_proj, sums)
    return summed_over(summed_over(part_out, first_shift, None), second_shift, queries.shape[:2])


def solution(mesh):
    placed = (
        P(("pre", "tp"), None),
        P(("pre", "tp"), None),
        P(None, "pre", "tp", None),
        P(None, "pre", None, None),
        P(None, "pre", None),
        P("tp", None, None),
        P("tp", None),
        P(None, "pre", None, None),
        P(None, "pre", None),
        P(None, "pre", None),
    )
    return jax.shard_map(
        on_device,
        mesh=mesh,
        in_specs=placed,
        out_specs=(P(None, "pre", None), P(None, "pre")),
        check_vma=False,
    )
```

```python
import jax
import jax.numpy as jnp
from jax import lax
from jax.experimental import pallas as pl
from jax.experimental.pallas import tpu as pltpu
from jax.sharding import PartitionSpec as P

IDX = 128
LAT = 512
KV = 576
BLOCK = 64
PRE = 8
TP = 16
PAIRS = 8
HEADS = 8
ROWS = 1024
PACK = 256
MIDDLE = 96
WIDE = KV + MIDDLE
CHUNKS = 6
QTILE = 256
STAT = 128
QROWS = TP * PAIRS * HEADS
LOWEST = -3.0e38
SOFT_SCALE = 192.0 ** (-0.5)
LOG2E = 1.4426950408889634
SCORE_SCALE = SOFT_SCALE * LOG2E

NT = (((1,), (1,)), ((), ()))


CHEAP = pl.CostEstimate(flops=1000, bytes_accessed=1000, transcendentals=0)


def vmem():
    return pl.BlockSpec(memory_space=pltpu.VMEM)


def smem():
    return pl.BlockSpec(memory_space=pltpu.SMEM)


def table_kernel(rows_ref, owner_ref, count_ref, mask_ref, pos_ref, total_ref):
    me_pre = lax.axis_index("pre")
    me_tp = lax.axis_index("tp")
    number = rows_ref.shape[2]
    before = (
        lax.broadcasted_iota(jnp.int32, (number, number), 0) < lax.broadcasted_iota(jnp.int32, (number, number), 1)
    ).astype(jnp.float32).astype(jnp.bfloat16)
    slot = lax.broadcasted_iota(jnp.int32, (8, number), 0).astype(jnp.float32)
    entry = lax.broadcasted_iota(jnp.int32, (8, BLOCK), 1).astype(jnp.float32)
    high_iota = lax.broadcasted_iota(jnp.int32, (PRE * 8, BLOCK), 0).astype(jnp.float32)
    low_iota = lax.broadcasted_iota(jnp.int32, (128, BLOCK), 0).astype(jnp.float32)
    for pair in range(PAIRS):
        step, local = pair // rows_ref.shape[1], pair % rows_ref.shape[1]
        rows = rows_ref[step, local]
        source = rows >> 10
        relative = ((((source >> 1) - (me_pre >> 1) + 1) & 3) << 1) | ((source ^ me_pre) & 1)
        high = ((relative << 3) | ((rows >> 7) & 7)).astype(jnp.float32).astype(jnp.bfloat16)
        low = (rows & 127).astype(jnp.float32).astype(jnp.bfloat16)
        owned = jnp.where(owner_ref[step, local : local + 1, :] == me_tp, 1.0, 0.0)
        rank = jnp.dot(owned.astype(jnp.bfloat16), before, preferred_element_type=jnp.float32)
        choose = jnp.where(slot == rank, owned, 0.0)
        limit = jnp.sum(choose * count_ref[step, local : local + 1, :].astype(jnp.float32), axis=1, keepdims=True)
        choose = choose.astype(jnp.bfloat16)
        valid = entry < limit
        high = jnp.where(valid, jnp.dot(choose, high, preferred_element_type=jnp.float32), -1.0)
        low = jnp.dot(choose, low, preferred_element_type=jnp.float32)
        chosen = jnp.zeros((PRE * 8, 128), jnp.float32)
        for block in range(number // TP):
            high_one = jnp.where(high_iota == high[block : block + 1, :], 1.0, 0.0).astype(jnp.bfloat16)
            low_one = jnp.where(low_iota == low[block : block + 1, :], 1.0, 0.0).astype(jnp.bfloat16)
            chosen = chosen + lax.dot_general(high_one, low_one, NT, preferred_element_type=jnp.float32)
        for block in range(PRE):
            for part in range(8):
                mask_ref[block, pair : pair + 1, part * 128 : (part + 1) * 128] = chosen[
                    block * 8 + part : block * 8 + part + 1, :
                ]
    union = jnp.concatenate([jnp.max(mask_ref[block], axis=0, keepdims=True) for block in range(PRE)], axis=0)
    before = (
        lax.broadcasted_iota(jnp.int32, (128, 128), 0) < lax.broadcasted_iota(jnp.int32, (128, 128), 1)
    ).astype(jnp.float32).astype(jnp.bfloat16)
    carry = jnp.zeros((PRE, 1), jnp.float32)
    for part in range(8):
        piece = union[:, part * 128 : (part + 1) * 128]
        ahead = jnp.dot(piece.astype(jnp.bfloat16), before, preferred_element_type=jnp.float32) + carry
        pos_ref[:, part * 128 : (part + 1) * 128] = jnp.where(piece > 0.0, ahead, -1.0)
        carry = carry + jnp.sum(piece, axis=1, keepdims=True)
    total_ref[...] = jnp.broadcast_to(carry, (PRE, 128)).astype(jnp.int32)


def make_tables(block_rows, block_owner, block_count):
    return pl.pallas_call(
        table_kernel,
        out_shape=(
            jax.ShapeDtypeStruct((PRE, PAIRS, ROWS), jnp.float32),
            jax.ShapeDtypeStruct((PRE, ROWS), jnp.float32),
            jax.ShapeDtypeStruct((PRE, 128), jnp.int32),
        ),
        in_specs=[vmem()] * 3,
        out_specs=(vmem(), vmem(), vmem()),
        compiler_params=pltpu.CompilerParams(vmem_limit_bytes=8 << 20),
        cost_estimate=CHEAP,
        name="row_tables",
    )(block_rows, block_owner, block_count)


def cut_kernel(*refs):
    number = len(refs) // 3
    half = KV // 2
    for block in range(number):
        refs[number + 2 * block][...] = refs[block][:half, :]
        refs[number + 2 * block + 1][...] = refs[block][half + MIDDLE :, :]


def cut(blocks):
    out = jax.ShapeDtypeStruct((KV // 2, ROWS), jnp.bfloat16)
    return pl.pallas_call(
        cut_kernel,
        out_shape=(out,) * (2 * len(blocks)),
        in_specs=[vmem()] * len(blocks),
        out_specs=(vmem(),) * (2 * len(blocks)),
        compiler_params=pltpu.CompilerParams(vmem_limit_bytes=16 << 20),
        cost_estimate=CHEAP,
        name="cut",
    )(*blocks)


TOKEN = jax.ShapeDtypeStruct((8, 128), jnp.float32)


def token_kernel(*refs):
    refs[-1][...] = jnp.zeros(refs[-1].shape, jnp.float32)


def arrived(values):
    return pl.pallas_call(
        token_kernel,
        out_shape=TOKEN,
        in_specs=[pl.BlockSpec(memory_space=pl.ANY)] * len(values),
        out_specs=vmem(),
        compiler_params=pltpu.CompilerParams(vmem_limit_bytes=2 << 20),
        cost_estimate=CHEAP,
        name="arrived",
    )(*values)


def halves_kernel(forward_ref, backward_ref, top_ref, low_ref):
    top_ref[...] = forward_ref[...]
    low_ref[...] = backward_ref[...]


def halves(forward, backward):
    half = (forward.shape[0] // 2, forward.shape[1])
    out = jax.ShapeDtypeStruct(half, forward.dtype)
    return pl.pallas_call(
        halves_kernel,
        grid=(1,),
        out_shape=(out, out),
        in_specs=[pl.BlockSpec(half, lambda part: (0, 0)), pl.BlockSpec(half, lambda part: (1, 0))],
        out_specs=(pl.BlockSpec(half, lambda part: (0, 0)),) * 2,
        compiler_params=pltpu.CompilerParams(vmem_limit_bytes=8 << 20),
        cost_estimate=CHEAP,
        name="halves",
    )(forward, backward)


def pack_block(number, pieces, mask_row, pos_row, packed_ref, first_lane):
    slot = (lax.broadcasted_iota(jnp.int32, (PACK, ROWS), 0) + number * PACK).astype(jnp.float32)
    pick = jnp.where(slot == pos_row, 1.0, 0.0).astype(jnp.bfloat16)
    depth = KV // len(pieces)
    for order, piece in enumerate(pieces):
        packed = lax.dot_general(piece, pick, NT, preferred_element_type=jnp.float32)
        packed_ref[order * depth : (order + 1) * depth, first_lane : first_lane + PACK] = packed.astype(jnp.bfloat16)
    present = lax.dot_general(mask_row.astype(jnp.bfloat16), pick, NT, preferred_element_type=jnp.float32)
    return jnp.where(present > 0.5, 0.0, -jnp.inf)


def latent_parts(refs):
    half = KV // 2
    if refs[0].shape[0] == half:
        return list(refs)
    if len(refs) == 1:
        return [refs[0].at[pl.ds(0, half), :], refs[0].at[pl.ds(half + MIDDLE, half), :]]
    return [refs[0].at[pl.ds(0, half), :], refs[1].at[pl.ds(MIDDLE // 2, half), :]]


def pack_kernel(base, parts, unused_ref, mask_ref, pos_ref, *refs):
    packed_ref, absent_ref = refs[-2:]
    for block, number in enumerate(parts):
        pieces, refs = refs[:number], refs[number:]
        row = base + block
        absent_ref[:, block * PACK : (block + 1) * PACK] = pack_block(
            0, [part[...] for part in latent_parts(pieces)], mask_ref[row], pos_ref[row : row + 1, :], packed_ref,
            block * PACK,
        )


def pack(base, token, masks, positions, sources):
    parts = [len(pieces) for pieces in sources]
    rows = sum([list(pieces) for pieces in sources], [])

    def body(*refs):
        pack_kernel(base, parts, *refs)

    return pl.pallas_call(
        body,
        out_shape=(
            jax.ShapeDtypeStruct((KV, len(parts) * PACK), jnp.bfloat16),
            jax.ShapeDtypeStruct((PAIRS, len(parts) * PACK), jnp.float32),
        ),
        in_specs=[pl.BlockSpec(memory_space=pl.ANY)] + [vmem()] * (2 + len(rows)),
        out_specs=(vmem(), vmem()),
        compiler_params=pltpu.CompilerParams(vmem_limit_bytes=16 << 20),
        cost_estimate=CHEAP,
        name="pack_%d" % len(parts),
    )(token, masks, positions, *rows)


def attend_kernel(base, parts, shapes, first, last, count_ref, mask_ref, pos_ref, *refs):
    queries, refs = refs[: shapes[0]], refs[shapes[0] :]
    packs, refs = refs[: 2 * shapes[1]], refs[2 * shapes[1] :]
    sources = []
    for number in parts:
        sources.append(refs[:number])
        refs = refs[number:]
    groups = len(queries)
    if not first:
        former_state, refs = refs[: 2 * groups], refs[2 * groups :]
    if last:
        outs, refs = refs[:groups], refs[groups:]
    state, refs = refs[: 2 * groups], refs[2 * groups :]
    if not last:
        refs[0][...] = jnp.zeros(refs[0].shape, jnp.float32)
        refs = refs[1:]
    packed_ref, rows_ref, sem = refs
    column = lax.broadcasted_iota(jnp.int32, (QTILE, STAT), 1)

    def attention(packed, absent, fresh):
        span = absent.shape[1]
        for group in range(groups):
            stat_ref, acc_ref = state[2 * group], state[2 * group + 1]
            query = queries[group][...]
            scores = [jnp.dot(query, ref[...], preferred_element_type=jnp.float32) for ref in packed]
            scores = scores[0] if len(scores) == 1 else jnp.concatenate(scores, axis=1)
            scores = scores.reshape(QTILE // 64, PAIRS, HEADS, span) * SCORE_SCALE + absent[None, :, None, :]
            scores = scores.reshape(QTILE, span)
            newer = jnp.max(scores, axis=1, keepdims=True)
            if fresh and first:
                newer = jnp.maximum(newer, LOWEST)
            else:
                stats, acc = (former_state[2 * group], former_state[2 * group + 1]) if fresh else (stat_ref, acc_ref)
                former = stats[:, :1]
                newer = jnp.maximum(former, newer)
                decay = jnp.exp2(former - newer)
            weights = jnp.exp2(scores - newer)
            total = jnp.sum(weights, axis=1, keepdims=True)
            weights = weights.astype(jnp.bfloat16)
            added, start = None, 0
            for ref in packed:
                width = ref.shape[1]
                piece = lax.dot_general(
                    weights[:, start : start + width], ref[:LAT, :], NT, preferred_element_type=jnp.float32
                )
                added = piece if added is None else added + piece
                start += width
            if not (fresh and first):
                total = stats[:, STAT // 2 : STAT // 2 + 1] * decay + total
                added = acc[...] * decay + added
            acc_ref[...] = added
            stat_ref[...] = jnp.where(column < STAT // 2, newer, total)

    attention(packs[::2], jnp.concatenate([ref[...] for ref in packs[1::2]], axis=1), True)

    for block in range(len(parts)):
        row = base + block
        rounds = (count_ref[row, 0] + (PACK - 1)) // PACK

        @pl.when(rounds > 1)
        def _(block=block, row=row, rounds=rounds):
            for order, piece in enumerate(latent_parts(sources[block])):
                copy = pltpu.make_async_copy(piece, rows_ref.at[pl.ds(order * (KV // 2), KV // 2), :], sem)
                copy.start()
                copy.wait()

            @pl.loop(1, rounds)
            def _(number):
                absent = pack_block(
                    number, [rows_ref[...]], mask_ref[row], pos_ref[row : row + 1, :], packed_ref, 0
                )
                attention([packed_ref], absent, False)

    if last:
        for group in range(groups):
            stat_ref, acc_ref = state[2 * group], state[2 * group + 1]
            write_payload(outs[group], stat_ref[:, :1], stat_ref[:, STAT // 2 : STAT // 2 + 1], acc_ref[...])


def write_payload(out_ref, highest, total, acc):
    lane = lax.broadcasted_iota(jnp.int32, (acc.shape[0], STAT), 1)
    out_ref[:, :LAT] = acc.astype(jnp.bfloat16)
    out_ref[:, LAT:] = (split_three(highest, lane, 0) + split_three(total, lane, 3)).astype(jnp.bfloat16)


def attend(base, counts, queries, masks, positions, packs, sources, states=None, last=False):
    parts = [len(pieces) for pieces in sources]
    first = states is None
    groups = len(queries)
    shapes = (
        jax.ShapeDtypeStruct((QTILE, STAT), jnp.float32),
        jax.ShapeDtypeStruct((QTILE, LAT), jnp.float32),
    ) * groups
    if last:
        out_shape = (jax.ShapeDtypeStruct((QTILE, LAT + STAT), jnp.bfloat16),) * groups
        scratch = [pltpu.VMEM(s.shape, s.dtype) for s in shapes]
    else:
        out_shape = shapes + (TOKEN,)
        scratch = []
    scratch = scratch + [
        pltpu.VMEM((KV, PACK), jnp.bfloat16),
        pltpu.VMEM((KV, ROWS), jnp.bfloat16),
        pltpu.SemaphoreType.DMA(()),
    ]
    packed = sum([list(pair) for pair in packs], [])
    rows = [pltpu.with_memory_space_constraint(piece, pltpu.HBM) for pieces in sources for piece in pieces]
    former = [] if first else [part for state in states for part in state]

    def body(*refs):
        attend_kernel(base, parts, (groups, len(packs)), first, last, *refs)

    in_specs = [smem()] + [vmem()] * (2 + groups + len(packed))
    in_specs = in_specs + [pl.BlockSpec(memory_space=pl.ANY)] * len(rows) + [vmem()] * len(former)
    outs = pl.pallas_call(
        body,
        out_shape=out_shape,
        in_specs=in_specs,
        out_specs=(vmem(),) * len(out_shape),
        scratch_shapes=scratch,
        compiler_params=pltpu.CompilerParams(vmem_limit_bytes=16 << 20),
        cost_estimate=CHEAP,
        name="attend_%d_%d" % (len(parts), groups),
    )(counts, masks, positions, *queries, *packed, *rows, *former)
    if last:
        return list(outs)
    return [tuple(outs[2 * group : 2 * group + 2]) for group in range(groups)], outs[-1]


def combined(refs):
    row = lax.broadcasted_iota(jnp.int32, (STAT, 2 * STAT), 0)
    col = lax.broadcasted_iota(jnp.int32, (STAT, 2 * STAT), 1)
    spread = jnp.where((row // 3) == (col // STAT), 1.0, 0.0).astype(jnp.bfloat16)
    stats = [jnp.dot(ref[:, LAT:], spread, preferred_element_type=jnp.float32) for ref in refs]
    highest = stats[0][:, :STAT]
    for stat in stats[1:]:
        highest = jnp.maximum(highest, stat[:, :STAT])
    total, acc = None, None
    for ref, stat in zip(refs, stats):
        weight = jnp.exp2(stat[:, :STAT] - highest)
        wide = jnp.concatenate([weight] * (LAT // STAT), axis=1) * ref[:, :LAT].astype(jnp.float32)
        total = weight * stat[:, STAT:] if total is None else total + weight * stat[:, STAT:]
        acc = wide if acc is None else acc + wide
    return highest, total, acc


def combine_kernel(*refs):
    highest, total, acc = combined(refs[:4])
    for part, out_ref in enumerate(refs[4:]):
        here = slice(part * PAIRS * HEADS, (part + 1) * PAIRS * HEADS)
        write_payload(out_ref, highest[here, :1], total[here, :1], acc[here, :])


def combine(parts):
    return pl.pallas_call(
        combine_kernel,
        out_shape=(jax.ShapeDtypeStruct((PAIRS * HEADS, LAT + STAT), jnp.bfloat16),) * 4,
        in_specs=[vmem()] * 4,
        out_specs=(vmem(),) * 4,
        compiler_params=pltpu.CompilerParams(vmem_limit_bytes=8 << 20),
        cost_estimate=CHEAP,
        name="combine",
    )(*parts)


def project_kernel(value_ref, weights, partial_ref, *refs):
    out_ref = refs[4]
    highest, total, acc = combined(refs[:4])
    attn = (acc / jnp.concatenate([total] * (LAT // STAT), axis=1)).astype(jnp.bfloat16)
    head_of = lax.broadcasted_iota(jnp.int32, (PAIRS, HEADS, 128), 1)
    pieces = []
    for head in range(HEADS):
        product = jnp.dot(attn, value_ref[head], preferred_element_type=jnp.float32)
        product = jnp.where(head_of == head, product.reshape(PAIRS, HEADS, 128), 0.0)
        pieces.append(jnp.sum(product, axis=1))
    values = jnp.concatenate(pieces, axis=1).astype(jnp.bfloat16)
    width = weights.shape[1]
    result = jnp.dot(values, weights[...], preferred_element_type=jnp.float32)
    out_ref[:, :width] = result.astype(jnp.bfloat16)
    lane = lax.broadcasted_iota(jnp.int32, (PAIRS, STAT), 1)
    group = lax.axis_index("pre")
    mine = jnp.sum(jnp.where(lane == group, partial_ref[...], 0.0), axis=1, keepdims=True)
    out_ref[:, width:] = split_three(mine, lane, 0).astype(jnp.bfloat16)


def project(received, value_proj, out_proj, partial):
    return pl.pallas_call(
        project_kernel,
        out_shape=jax.ShapeDtypeStruct((PAIRS, out_proj.shape[1] + STAT), jnp.bfloat16),
        in_specs=[vmem()] * 7,
        out_specs=vmem(),
        compiler_params=pltpu.CompilerParams(vmem_limit_bytes=16 << 20),
        cost_estimate=CHEAP,
        name="project",
    )(value_proj, pltpu.with_memory_space_constraint(out_proj, pltpu.VMEM), partial, *received)


def index_kernel(chips, first_keys, second_keys, unused_ref, *refs):
    place = lax.axis_index("pre")
    former_ref, middles, out_ref, slab_ref = refs[0], refs[1:-2], refs[-2], refs[-1]
    lane = lax.broadcasted_iota(jnp.int32, (PAIRS, 128), 1)
    result = former_ref[...]
    for chip in chips:
        uses, middles = middles[: 1 if chip < 2 else 2], middles[1 if chip < 2 else 2 :]
        middle = uses[0][...] if chip < 2 else jnp.concatenate([part[...] for part in uses], axis=0)
        for pair in range(PAIRS):
            slab_ref[pair * 64 : (pair + 1) * 64, :] = middle[:64, pair * IDX : (pair + 1) * IDX]
        gates = middle[64:80, :64].astype(jnp.float32)
        lines = [jnp.concatenate([gates[2 * line : 2 * line + 1], gates[2 * line + 1 : 2 * line + 2]], axis=1) for line in range(4)]
        columns = jnp.concatenate(lines + [jnp.zeros((124, 128), jnp.float32)], axis=0).T
        group = (((place >> 1) + chip) & 3) * 2 + (place & 1)
        sums = []
        for keys in (first_keys, second_keys):
            scores = []
            for part in range(4):
                logits = lax.dot_general(
                    slab_ref[part * 128 : (part + 1) * 128, :], keys[...], NT, preferred_element_type=jnp.float32
                )
                gated = jnp.maximum(logits, 0.0) * columns[:, part : part + 1]
                scores.append(jnp.sum(gated.reshape(2, 64, ROWS), axis=1))
            scores = jnp.concatenate(scores, axis=0) * IDX ** (-0.5)
            largest = jnp.max(scores, axis=1, keepdims=True)
            sums.append(largest + jnp.log(jnp.sum(jnp.exp(scores - largest), axis=1, keepdims=True)))
        result = jnp.where(lane == group, log_add(sums[0], sums[1]), result)
    out_ref[...] = result


def index_partial(chips, keys, token, former, blocks):
    specs, args = [], []
    for parts in blocks:
        if len(parts) == 1:
            specs.append(pl.BlockSpec((MIDDLE, ROWS), lambda part: (3, 0)))
        else:
            specs.append(pl.BlockSpec((MIDDLE // 2, ROWS), lambda part: (6, 0)))
            specs.append(pl.BlockSpec((MIDDLE // 2, ROWS), lambda part: (0, 0)))
        args += list(parts)

    def body(*refs):
        index_kernel(chips, *refs)

    whole = pl.BlockSpec(keys[0].shape, lambda part: (0, 0))
    small = pl.BlockSpec((PAIRS, 128), lambda part: (0, 0))
    return pl.pallas_call(
        body,
        grid=(1,),
        out_shape=jax.ShapeDtypeStruct((PAIRS, 128), jnp.float32),
        in_specs=[whole, whole, pl.BlockSpec(memory_space=pl.ANY), small] + specs,
        out_specs=small,
        scratch_shapes=[pltpu.VMEM((PAIRS * 64, IDX), jnp.bfloat16)],
        compiler_params=pltpu.CompilerParams(vmem_limit_bytes=16 << 20),
        cost_estimate=CHEAP,
        name="index_partial_%d" % len(chips),
    )(*keys, token, former, *args)


def log_add(one, two):
    top = jnp.maximum(one, two)
    return top + jnp.log(jnp.exp(one - top) + jnp.exp(two - top))


def split_three(value, lane, start):
    pieces = jnp.zeros(lane.shape, jnp.float32)
    for step in range(3):
        piece = value.astype(jnp.bfloat16).astype(jnp.float32)
        pieces = jnp.where(lane == start + step, piece, pieces)
        value = value - piece
    return pieces


def join_three(pieces, start):
    wide = pieces.astype(jnp.float32)
    return wide[:, start : start + 1] + wide[:, start + 1 : start + 2] + wide[:, start + 2 : start + 3]


def four_sum(refs):
    width = refs[0].shape[1] - STAT
    parts = [ref[:, :width].astype(jnp.float32) for ref in refs]
    logs = [join_three(ref[:, width:], 0) for ref in refs]
    return (parts[0] + parts[1]) + (parts[2] + parts[3]), log_add(log_add(logs[0], logs[1]), log_add(logs[2], logs[3]))


def middle_kernel(own_ref, far_ref, right_ref, left_ref, out_ref):
    summed, logs = four_sum((own_ref, far_ref, right_ref, left_ref))
    width = summed.shape[1]
    out_ref[:, :width] = summed.astype(jnp.bfloat16)
    lane = lax.broadcasted_iota(jnp.int32, (PAIRS, STAT), 1)
    out_ref[:, width:] = split_three(logs, lane, 0).astype(jnp.bfloat16)


def final_kernel(own_ref, far_ref, right_ref, left_ref, out_ref, log_ref):
    summed, logs = four_sum((own_ref, far_ref, right_ref, left_ref))
    steps, local = log_ref.shape
    flat = jnp.broadcast_to(logs, (PAIRS, STAT)).T[:1, :]
    for step in range(steps):
        out_ref[step] = summed[step * local : (step + 1) * local, :].astype(jnp.bfloat16)
        log_ref[step : step + 1, :] = flat[:, step * local : (step + 1) * local]


def summed_over(value, shift, final):
    parts = (value,) + tuple(lax.ppermute(value, BOTH, shift(step)) for step in (2, 1, 3))
    if final:
        out_shape = (
            jax.ShapeDtypeStruct(final + (value.shape[1] - STAT,), jnp.bfloat16),
            jax.ShapeDtypeStruct(final, jnp.float32),
        )
        out_specs = (vmem(), vmem())
    else:
        out_shape = jax.ShapeDtypeStruct(value.shape, jnp.bfloat16)
        out_specs = vmem()
    return pl.pallas_call(
        final_kernel if final else middle_kernel,
        out_shape=out_shape,
        in_specs=[vmem()] * 4,
        out_specs=out_specs,
        compiler_params=pltpu.CompilerParams(vmem_limit_bytes=4 << 20),
        cost_estimate=CHEAP,
        name="sum_last" if final else "sum_first",
    )(*parts)


def prepare_kernel(latent_ref, query_ref, gate_ref, key_ref, block_ref, key_out_ref, latent, queries, gates, keys, sems):
    depth = KV // CHUNKS
    copies = [
        pltpu.make_async_copy(
            latent_ref.at[pl.ds(part * depth, depth)], latent.at[pl.ds(part * depth, depth)], sems.at[part]
        )
        for part in range(CHUNKS)
    ]
    others = [
        pltpu.make_async_copy(query_ref, queries, sems.at[CHUNKS]),
        pltpu.make_async_copy(gate_ref, gates, sems.at[CHUNKS + 1]),
        pltpu.make_async_copy(key_ref, keys, sems.at[CHUNKS + 2]),
    ]
    for copy in copies + others:
        copy.start()
    for part, copy in enumerate(copies):
        copy.wait()
        start = part * depth + (MIDDLE if part >= CHUNKS // 2 else 0)
        block_ref[start : start + depth, :] = latent[part * depth : (part + 1) * depth, :].astype(jnp.bfloat16)
    for copy in others:
        copy.wait()
    first = KV // 2
    block_ref[first + 64 : first + MIDDLE, :] = jnp.zeros((MIDDLE - 64, ROWS), jnp.bfloat16)
    lines = []
    for step in range(query_ref.shape[0]):
        for local in range(query_ref.shape[1]):
            pair = step * query_ref.shape[1] + local
            block_ref[first : first + 64, pair * IDX : (pair + 1) * IDX] = queries[step, local]
            lines.append(gates[step, local : local + 1, :].astype(jnp.float32))
    lines = jnp.concatenate(lines + [jnp.zeros((8, 64), jnp.float32)], axis=0)
    block_ref[first + 64 : first + 80, :64] = lines.astype(jnp.bfloat16)
    key_out_ref[...] = keys[...].astype(jnp.bfloat16)


def prepare(latent, index_queries, index_gates, index_keys):
    args = (latent, index_queries, index_gates, index_keys)
    return pl.pallas_call(
        prepare_kernel,
        out_shape=(
            jax.ShapeDtypeStruct((WIDE, ROWS), jnp.bfloat16),
            jax.ShapeDtypeStruct(index_keys.shape, jnp.bfloat16),
        ),
        in_specs=[pl.BlockSpec(memory_space=pl.ANY)] * 4,
        out_specs=(vmem(), vmem()),
        scratch_shapes=[pltpu.VMEM(arg.shape, arg.dtype) for arg in args] + [pltpu.SemaphoreType.DMA((CHUNKS + 3,))],
        compiler_params=pltpu.CompilerParams(vmem_limit_bytes=12 << 20),
        cost_estimate=CHEAP,
        name="prepare",
    )(*[pltpu.with_memory_space_constraint(arg, pltpu.HBM) for arg in args])


def x_shift(step):
    return [(x * 2 + c, ((x + step) % 4) * 2 + c) for x in range(4) for c in range(2)]


BOTH = ("pre", "tp")


def plane_shift(step, along_y):
    pairs = []
    for p in range(PRE):
        for z in range(4):
            for y in range(4):
                to_y = along_y == (p % 2 == 0)
                there = z * 4 + (y + step) % 4 if to_y else ((z + step) % 4) * 4 + y
                pairs.append((p * TP + z * 4 + y, p * TP + there))
    return pairs


def first_shift(step):
    return plane_shift(step, True)


def second_shift(step):
    return plane_shift(step, False)


CORE_SWAP = [(i, i ^ 1) for i in range(PRE)]


def on_device(
    latent_rows,
    index_keys,
    queries,
    index_queries,
    index_gates,
    value_proj,
    out_proj,
    block_rows,
    block_owner,
    block_count,
):
    block, keys = prepare(latent_rows.T, index_queries, index_gates, index_keys)
    forward = lax.ppermute(block, "pre", x_shift(1))
    backward = lax.ppermute(block, "pre", x_shift(3))

    own_queries = queries.reshape(PAIRS * HEADS, KV)
    row = jnp.concatenate(
        [own_queries] + [lax.ppermute(own_queries, BOTH, first_shift(4 - step)) for step in (1, 2, 3)], axis=0
    )
    plane = [row] + [lax.ppermute(row, BOTH, second_shift(4 - step)) for step in (1, 2, 3)]

    def swapped(part):
        return lax.ppermute(part, "pre", CORE_SWAP)

    def both(parts):
        return [list(parts), [swapped(part) for part in parts]]

    masks, positions, counts = make_tables(block_rows, block_owner, block_count)
    token = arrived(plane[1:] + [masks])
    forward, backward, block, keys, token = lax.optimization_barrier((forward, backward, block, keys, token))
    top, low = halves(forward, backward)

    far = [lax.ppermute(top, "pre", x_shift(1)), lax.ppermute(low, "pre", x_shift(3))]
    sides = both([forward]) + both([backward])
    keys = [keys, swapped(keys)]
    packs = [
        pack(base, early, masks, positions, rows) for base, early, rows in ((0, keys[1], sides[:2]), (4, token, sides[2:]))
    ]
    mine, absent = lax.optimization_barrier((cut([block]), packs[1][1]))
    packs[1] = (packs[1][0], absent)
    own = [[block], [swapped(part) for part in mine]]
    packs.append(pack(2, token, masks, positions, own))
    packs = [packs[0], packs[2], packs[1]]
    states, token = attend(0, counts, plane, masks, positions, packs, sides[:2] + own + sides[2:])
    partial = index_partial((0, 1, -1), keys, token, token, (own[0], sides[2], sides[0]))
    far, partial = lax.optimization_barrier((far, partial))
    far = both(far)
    packs = [pack(6, partial, masks, positions, far)]

    payloads = [None] * 4
    parts = [None] * 4
    for step in (2, 1, 3, 0):
        one = slice(step, step + 1)
        payloads[step] = attend(6, counts, plane[one], masks, positions, packs, far, states[one], last=True)[0]
        parts[step] = lax.ppermute(payloads[step], BOTH, second_shift(step)) if step else payloads[0]
    parts = combine(parts)
    received = [parts[0]] + [lax.ppermute(parts[step], BOTH, first_shift(step)) for step in (2, 1, 3)]
    partial = index_partial((2,), keys, payloads[3], partial, (far[0],))
    parts = [lax.ppermute(partial, "pre", x_shift(step)) for step in (2, 1, 3)]
    partial = log_add(log_add(partial, parts[0]), log_add(parts[1], parts[2]))
    part_out = project(received, value_proj, out_proj, partial)
    return summed_over(summed_over(part_out, first_shift, None), second_shift, queries.shape[:2])


def solution(mesh):
    placed = (
        P(("pre", "tp"), None),
        P(("pre", "tp"), None),
        P(None, "pre", "tp", None),
        P(None, "pre", None, None),
        P(None, "pre", None),
        P("tp", None, None),
        P("tp", None),
        P(None, "pre", None, None),
        P(None, "pre", None),
        P(None, "pre", None),
    )
    return jax.shard_map(
        on_device,
        mesh=mesh,
        in_specs=placed,
        out_specs=(P(None, "pre", None), P(None, "pre")),
        check_vma=False,
    )
```

```python
import jax
import jax.numpy as jnp
from jax import lax
from jax.experimental import pallas as pl
from jax.experimental.pallas import tpu as pltpu
from jax.sharding import PartitionSpec as P

IDX = 128
LAT = 512
KV = 576
BLOCK = 64
PRE = 8
TP = 16
PAIRS = 8
HEADS = 8
ROWS = 1024
PACK = 256
MIDDLE = 80
TOP = KV // 2 + 48
WIDE = KV + MIDDLE
CHUNKS = 6
QTILE = 256
STAT = 128
QROWS = TP * PAIRS * HEADS
LOWEST = -3.0e38
SOFT_SCALE = 192.0 ** (-0.5)
LOG2E = 1.4426950408889634
SCORE_SCALE = SOFT_SCALE * LOG2E

NT = (((1,), (1,)), ((), ()))


CHEAP = pl.CostEstimate(flops=1000, bytes_accessed=1000, transcendentals=0)


def vmem():
    return pl.BlockSpec(memory_space=pltpu.VMEM)


def smem():
    return pl.BlockSpec(memory_space=pltpu.SMEM)


def table_kernel(rows_ref, owner_ref, count_ref, mask_ref, pos_ref, total_ref):
    me_pre = lax.axis_index("pre")
    me_tp = lax.axis_index("tp")
    number = rows_ref.shape[2]
    before = (
        lax.broadcasted_iota(jnp.int32, (number, number), 0) < lax.broadcasted_iota(jnp.int32, (number, number), 1)
    ).astype(jnp.float32).astype(jnp.bfloat16)
    slot = lax.broadcasted_iota(jnp.int32, (8, number), 0).astype(jnp.float32)
    entry = lax.broadcasted_iota(jnp.int32, (8, BLOCK), 1).astype(jnp.float32)
    high_iota = lax.broadcasted_iota(jnp.int32, (PRE * 8, BLOCK), 0).astype(jnp.float32)
    low_iota = lax.broadcasted_iota(jnp.int32, (128, BLOCK), 0).astype(jnp.float32)
    for pair in range(PAIRS):
        step, local = pair // rows_ref.shape[1], pair % rows_ref.shape[1]
        rows = rows_ref[step, local]
        source = rows >> 10
        relative = ((((source >> 1) - (me_pre >> 1) + 1) & 3) << 1) | ((source ^ me_pre) & 1)
        high = ((relative << 3) | ((rows >> 7) & 7)).astype(jnp.float32).astype(jnp.bfloat16)
        low = (rows & 127).astype(jnp.float32).astype(jnp.bfloat16)
        owned = jnp.where(owner_ref[step, local : local + 1, :] == me_tp, 1.0, 0.0)
        rank = jnp.dot(owned.astype(jnp.bfloat16), before, preferred_element_type=jnp.float32)
        choose = jnp.where(slot == rank, owned, 0.0)
        limit = jnp.sum(choose * count_ref[step, local : local + 1, :].astype(jnp.float32), axis=1, keepdims=True)
        choose = choose.astype(jnp.bfloat16)
        valid = entry < limit
        high = jnp.where(valid, jnp.dot(choose, high, preferred_element_type=jnp.float32), -1.0)
        low = jnp.dot(choose, low, preferred_element_type=jnp.float32)
        chosen = jnp.zeros((PRE * 8, 128), jnp.float32)
        for block in range(number // TP):
            high_one = jnp.where(high_iota == high[block : block + 1, :], 1.0, 0.0).astype(jnp.bfloat16)
            low_one = jnp.where(low_iota == low[block : block + 1, :], 1.0, 0.0).astype(jnp.bfloat16)
            chosen = chosen + lax.dot_general(high_one, low_one, NT, preferred_element_type=jnp.float32)
        for block in range(PRE):
            for part in range(8):
                mask_ref[block, pair : pair + 1, part * 128 : (part + 1) * 128] = chosen[
                    block * 8 + part : block * 8 + part + 1, :
                ]
    union = jnp.concatenate([jnp.max(mask_ref[block], axis=0, keepdims=True) for block in range(PRE)], axis=0)
    before = (
        lax.broadcasted_iota(jnp.int32, (128, 128), 0) < lax.broadcasted_iota(jnp.int32, (128, 128), 1)
    ).astype(jnp.float32).astype(jnp.bfloat16)
    carry = jnp.zeros((PRE, 1), jnp.float32)
    for part in range(8):
        piece = union[:, part * 128 : (part + 1) * 128]
        ahead = jnp.dot(piece.astype(jnp.bfloat16), before, preferred_element_type=jnp.float32) + carry
        pos_ref[:, part * 128 : (part + 1) * 128] = jnp.where(piece > 0.0, ahead, -1.0)
        carry = carry + jnp.sum(piece, axis=1, keepdims=True)
    total_ref[...] = jnp.broadcast_to(carry, (PRE, 128)).astype(jnp.int32)


def make_tables(block_rows, block_owner, block_count):
    return pl.pallas_call(
        table_kernel,
        out_shape=(
            jax.ShapeDtypeStruct((PRE, PAIRS, ROWS), jnp.float32),
            jax.ShapeDtypeStruct((PRE, ROWS), jnp.float32),
            jax.ShapeDtypeStruct((PRE, 128), jnp.int32),
        ),
        in_specs=[vmem()] * 3,
        out_specs=(vmem(), vmem(), vmem()),
        compiler_params=pltpu.CompilerParams(vmem_limit_bytes=8 << 20),
        cost_estimate=CHEAP,
        name="row_tables",
    )(block_rows, block_owner, block_count)


TOKEN = jax.ShapeDtypeStruct((8, 128), jnp.float32)


def token_kernel(*refs):
    refs[-1][...] = jnp.zeros(refs[-1].shape, jnp.float32)


def arrived(values):
    return pl.pallas_call(
        token_kernel,
        out_shape=TOKEN,
        in_specs=[pl.BlockSpec(memory_space=pl.ANY)] * len(values),
        out_specs=vmem(),
        compiler_params=pltpu.CompilerParams(vmem_limit_bytes=2 << 20),
        cost_estimate=CHEAP,
        name="arrived",
    )(*values)


def halves_kernel(forward_ref, backward_ref, top_ref, low_ref):
    top_ref[...] = forward_ref[:TOP, :]
    low_ref[...] = backward_ref[TOP:, :]


def halves(forward, backward):
    return pl.pallas_call(
        halves_kernel,
        out_shape=(
            jax.ShapeDtypeStruct((TOP, ROWS), forward.dtype),
            jax.ShapeDtypeStruct((WIDE - TOP, ROWS), forward.dtype),
        ),
        in_specs=[vmem()] * 2,
        out_specs=(vmem(),) * 2,
        compiler_params=pltpu.CompilerParams(vmem_limit_bytes=8 << 20),
        cost_estimate=CHEAP,
        name="halves",
    )(forward, backward)


def pack_block(number, pieces, mask_row, pos_row, packed_ref, first_lane):
    slot = (lax.broadcasted_iota(jnp.int32, (PACK, ROWS), 0) + number * PACK).astype(jnp.float32)
    pick = jnp.where(slot == pos_row, 1.0, 0.0).astype(jnp.bfloat16)
    depth = KV // len(pieces)
    for order, piece in enumerate(pieces):
        packed = lax.dot_general(piece, pick, NT, preferred_element_type=jnp.float32)
        packed_ref[order * depth : (order + 1) * depth, first_lane : first_lane + PACK] = packed.astype(jnp.bfloat16)
    present = lax.dot_general(mask_row.astype(jnp.bfloat16), pick, NT, preferred_element_type=jnp.float32)
    return jnp.where(present > 0.5, 0.0, -jnp.inf)


def latent_parts(refs):
    half = KV // 2
    if len(refs) == 1:
        return [refs[0].at[pl.ds(0, half), :], refs[0].at[pl.ds(half + MIDDLE, half), :]]
    return [refs[0].at[pl.ds(0, half), :], refs[1].at[pl.ds(KV // 2 + MIDDLE - TOP, half), :]]


def pack_kernel(base, parts, unused_ref, mask_ref, pos_ref, *refs):
    packed_ref, absent_ref = refs[-2:]
    for block, number in enumerate(parts):
        pieces, refs = refs[:number], refs[number:]
        row = base + block
        absent_ref[:, block * PACK : (block + 1) * PACK] = pack_block(
            0, [part[...] for part in latent_parts(pieces)], mask_ref[row], pos_ref[row : row + 1, :], packed_ref,
            block * PACK,
        )


def pack(base, token, masks, positions, sources):
    parts = [len(pieces) for pieces in sources]
    rows = sum([list(pieces) for pieces in sources], [])

    def body(*refs):
        pack_kernel(base, parts, *refs)

    return pl.pallas_call(
        body,
        out_shape=(
            jax.ShapeDtypeStruct((KV, len(parts) * PACK), jnp.bfloat16),
            jax.ShapeDtypeStruct((PAIRS, len(parts) * PACK), jnp.float32),
        ),
        in_specs=[pl.BlockSpec(memory_space=pl.ANY)] + [vmem()] * (2 + len(rows)),
        out_specs=(vmem(), vmem()),
        compiler_params=pltpu.CompilerParams(vmem_limit_bytes=16 << 20),
        cost_estimate=CHEAP,
        name="pack_%d" % len(parts),
    )(token, masks, positions, *rows)


def attend_kernel(base, parts, shapes, first, last, count_ref, mask_ref, pos_ref, *refs):
    queries, refs = refs[: shapes[0]], refs[shapes[0] :]
    packs, refs = refs[: 2 * shapes[1]], refs[2 * shapes[1] :]
    sources = []
    for number in parts:
        sources.append(refs[:number])
        refs = refs[number:]
    groups = len(queries)
    if not first:
        former_state, refs = refs[: 2 * groups], refs[2 * groups :]
    if last:
        outs, refs = refs[:groups], refs[groups:]
    state, refs = refs[: 2 * groups], refs[2 * groups :]
    if not last:
        refs[0][...] = jnp.zeros(refs[0].shape, jnp.float32)
        refs = refs[1:]
    packed_ref, rows_ref, sem = refs
    column = lax.broadcasted_iota(jnp.int32, (QTILE, STAT), 1)

    def attention(packed, absent, fresh):
        span = absent.shape[1]
        for group in range(groups):
            stat_ref, acc_ref = state[2 * group], state[2 * group + 1]
            query = queries[group][...]
            scores = [jnp.dot(query, ref[...], preferred_element_type=jnp.float32) for ref in packed]
            scores = scores[0] if len(scores) == 1 else jnp.concatenate(scores, axis=1)
            scores = scores.reshape(QTILE // 64, PAIRS, HEADS, span) * SCORE_SCALE + absent[None, :, None, :]
            scores = scores.reshape(QTILE, span)
            newer = jnp.max(scores, axis=1, keepdims=True)
            if fresh and first:
                newer = jnp.maximum(newer, LOWEST)
            else:
                stats, acc = (former_state[2 * group], former_state[2 * group + 1]) if fresh else (stat_ref, acc_ref)
                former = stats[:, :1]
                newer = jnp.maximum(former, newer)
                decay = jnp.exp2(former - newer)
            weights = jnp.exp2(scores - newer)
            total = jnp.sum(weights, axis=1, keepdims=True)
            weights = weights.astype(jnp.bfloat16)
            added, start = None, 0
            for ref in packed:
                width = ref.shape[1]
                piece = lax.dot_general(
                    weights[:, start : start + width], ref[:LAT, :], NT, preferred_element_type=jnp.float32
                )
                added = piece if added is None else added + piece
                start += width
            if not (fresh and first):
                total = stats[:, STAT // 2 : STAT // 2 + 1] * decay + total
                added = acc[...] * decay + added
            acc_ref[...] = added
            stat_ref[...] = jnp.where(column < STAT // 2, newer, total)

    attention(packs[::2], jnp.concatenate([ref[...] for ref in packs[1::2]], axis=1), True)

    for block in range(len(parts)):
        row = base + block
        rounds = (count_ref[row, 0] + (PACK - 1)) // PACK

        @pl.when(rounds > 1)
        def _(block=block, row=row, rounds=rounds):
            for order, piece in enumerate(latent_parts(sources[block])):
                copy = pltpu.make_async_copy(piece, rows_ref.at[pl.ds(order * (KV // 2), KV // 2), :], sem)
                copy.start()
                copy.wait()

            @pl.loop(1, rounds)
            def _(number):
                absent = pack_block(
                    number, [rows_ref[...]], mask_ref[row], pos_ref[row : row + 1, :], packed_ref, 0
                )
                attention([packed_ref], absent, False)

    if last:
        for group in range(groups):
            stat_ref, acc_ref = state[2 * group], state[2 * group + 1]
            write_payload(outs[group], stat_ref[:, :1], stat_ref[:, STAT // 2 : STAT // 2 + 1], acc_ref[...])


def write_payload(out_ref, highest, total, acc):
    lane = lax.broadcasted_iota(jnp.int32, (acc.shape[0], STAT), 1)
    out_ref[:, :LAT] = acc.astype(jnp.bfloat16)
    out_ref[:, LAT:] = (split_three(highest, lane, 0) + split_three(total, lane, 3)).astype(jnp.bfloat16)


def attend(base, counts, queries, masks, positions, packs, sources, states=None, last=False):
    parts = [len(pieces) for pieces in sources]
    first = states is None
    groups = len(queries)
    shapes = (
        jax.ShapeDtypeStruct((QTILE, STAT), jnp.float32),
        jax.ShapeDtypeStruct((QTILE, LAT), jnp.float32),
    ) * groups
    if last:
        out_shape = (jax.ShapeDtypeStruct((QTILE, LAT + STAT), jnp.bfloat16),) * groups
        scratch = [pltpu.VMEM(s.shape, s.dtype) for s in shapes]
    else:
        out_shape = shapes + (TOKEN,)
        scratch = []
    scratch = scratch + [
        pltpu.VMEM((KV, PACK), jnp.bfloat16),
        pltpu.VMEM((KV, ROWS), jnp.bfloat16),
        pltpu.SemaphoreType.DMA(()),
    ]
    packed = sum([list(pair) for pair in packs], [])
    rows = [pltpu.with_memory_space_constraint(piece, pltpu.HBM) for pieces in sources for piece in pieces]
    former = [] if first else [part for state in states for part in state]

    def body(*refs):
        attend_kernel(base, parts, (groups, len(packs)), first, last, *refs)

    in_specs = [smem()] + [vmem()] * (2 + groups + len(packed))
    in_specs = in_specs + [pl.BlockSpec(memory_space=pl.ANY)] * len(rows) + [vmem()] * len(former)
    outs = pl.pallas_call(
        body,
        out_shape=out_shape,
        in_specs=in_specs,
        out_specs=(vmem(),) * len(out_shape),
        scratch_shapes=scratch,
        compiler_params=pltpu.CompilerParams(vmem_limit_bytes=16 << 20),
        cost_estimate=CHEAP,
        name="attend_%d_%d" % (len(parts), groups),
    )(counts, masks, positions, *queries, *packed, *rows, *former)
    if last:
        return list(outs)
    return [tuple(outs[2 * group : 2 * group + 2]) for group in range(groups)], outs[-1]


def combined(refs):
    row = lax.broadcasted_iota(jnp.int32, (STAT, 2 * STAT), 0)
    col = lax.broadcasted_iota(jnp.int32, (STAT, 2 * STAT), 1)
    spread = jnp.where((row // 3) == (col // STAT), 1.0, 0.0).astype(jnp.bfloat16)
    stats = [jnp.dot(ref[:, LAT:], spread, preferred_element_type=jnp.float32) for ref in refs]
    highest = stats[0][:, :STAT]
    for stat in stats[1:]:
        highest = jnp.maximum(highest, stat[:, :STAT])
    total, acc = None, None
    for ref, stat in zip(refs, stats):
        weight = jnp.exp2(stat[:, :STAT] - highest)
        wide = jnp.concatenate([weight] * (LAT // STAT), axis=1) * ref[:, :LAT].astype(jnp.float32)
        total = weight * stat[:, STAT:] if total is None else total + weight * stat[:, STAT:]
        acc = wide if acc is None else acc + wide
    return highest, total, acc


def combine_kernel(*refs):
    highest, total, acc = combined(refs[:4])
    for part, out_ref in enumerate(refs[4:]):
        here = slice(part * PAIRS * HEADS, (part + 1) * PAIRS * HEADS)
        write_payload(out_ref, highest[here, :1], total[here, :1], acc[here, :])


def combine(parts):
    return pl.pallas_call(
        combine_kernel,
        out_shape=(jax.ShapeDtypeStruct((PAIRS * HEADS, LAT + STAT), jnp.bfloat16),) * 4,
        in_specs=[vmem()] * 4,
        out_specs=(vmem(),) * 4,
        compiler_params=pltpu.CompilerParams(vmem_limit_bytes=8 << 20),
        cost_estimate=CHEAP,
        name="combine",
    )(*parts)


def project_kernel(value_ref, weights, partial_ref, *refs):
    out_ref = refs[4]
    highest, total, acc = combined(refs[:4])
    attn = (acc / jnp.concatenate([total] * (LAT // STAT), axis=1)).astype(jnp.bfloat16)
    head_of = lax.broadcasted_iota(jnp.int32, (PAIRS, HEADS, 128), 1)
    pieces = []
    for head in range(HEADS):
        product = jnp.dot(attn, value_ref[head], preferred_element_type=jnp.float32)
        product = jnp.where(head_of == head, product.reshape(PAIRS, HEADS, 128), 0.0)
        pieces.append(jnp.sum(product, axis=1))
    values = jnp.concatenate(pieces, axis=1).astype(jnp.bfloat16)
    width = weights.shape[1]
    result = jnp.dot(values, weights[...], preferred_element_type=jnp.float32)
    out_ref[:, :width] = result.astype(jnp.bfloat16)
    lane = lax.broadcasted_iota(jnp.int32, (PAIRS, STAT), 1)
    group = lax.axis_index("pre")
    mine = jnp.sum(jnp.where(lane == group, partial_ref[...], 0.0), axis=1, keepdims=True)
    out_ref[:, width:] = split_three(mine, lane, 0).astype(jnp.bfloat16)


def project(received, value_proj, out_proj, partial):
    return pl.pallas_call(
        project_kernel,
        out_shape=jax.ShapeDtypeStruct((PAIRS, out_proj.shape[1] + STAT), jnp.bfloat16),
        in_specs=[vmem()] * 7,
        out_specs=vmem(),
        compiler_params=pltpu.CompilerParams(vmem_limit_bytes=16 << 20),
        cost_estimate=CHEAP,
        name="project",
    )(value_proj, pltpu.with_memory_space_constraint(out_proj, pltpu.VMEM), partial, *received)


def index_kernel(chips, first_keys, second_keys, unused_ref, *refs):
    place = lax.axis_index("pre")
    former_ref, middles, out_ref, slab_ref = refs[0], refs[1:-2], refs[-2], refs[-1]
    lane = lax.broadcasted_iota(jnp.int32, (PAIRS, 128), 1)
    result = former_ref[...]
    for chip in chips:
        uses, middles = middles[: 1 if chip < 2 else 2], middles[1 if chip < 2 else 2 :]
        first, last = KV // 2, KV // 2 + MIDDLE
        if chip < 2:
            middle = uses[0][first:last, :]
        else:
            middle = jnp.concatenate([uses[0][first:TOP, :], uses[1][: last - TOP, :]], axis=0)
        for pair in range(PAIRS):
            slab_ref[pair * 64 : (pair + 1) * 64, :] = middle[:64, pair * IDX : (pair + 1) * IDX]
        gates = middle[64:80, :64].astype(jnp.float32)
        lines = [jnp.concatenate([gates[2 * line : 2 * line + 1], gates[2 * line + 1 : 2 * line + 2]], axis=1) for line in range(4)]
        columns = jnp.concatenate(lines + [jnp.zeros((124, 128), jnp.float32)], axis=0).T
        group = (((place >> 1) + chip) & 3) * 2 + (place & 1)
        sums = []
        for keys in (first_keys, second_keys):
            scores = []
            for part in range(4):
                logits = lax.dot_general(
                    slab_ref[part * 128 : (part + 1) * 128, :], keys[...], NT, preferred_element_type=jnp.float32
                )
                gated = jnp.maximum(logits, 0.0) * columns[:, part : part + 1]
                scores.append(jnp.sum(gated.reshape(2, 64, ROWS), axis=1))
            scores = jnp.concatenate(scores, axis=0) * IDX ** (-0.5)
            largest = jnp.max(scores, axis=1, keepdims=True)
            sums.append(largest + jnp.log(jnp.sum(jnp.exp(scores - largest), axis=1, keepdims=True)))
        result = jnp.where(lane == group, log_add(sums[0], sums[1]), result)
    out_ref[...] = result


def index_partial(chips, keys, token, former, blocks):
    args = [part for parts in blocks for part in parts]

    def body(*refs):
        index_kernel(chips, *refs)

    return pl.pallas_call(
        body,
        out_shape=jax.ShapeDtypeStruct((PAIRS, 128), jnp.float32),
        in_specs=[vmem()] * 2 + [pl.BlockSpec(memory_space=pl.ANY)] + [vmem()] * (1 + len(args)),
        out_specs=vmem(),
        scratch_shapes=[pltpu.VMEM((PAIRS * 64, IDX), jnp.bfloat16)],
        compiler_params=pltpu.CompilerParams(vmem_limit_bytes=16 << 20),
        cost_estimate=CHEAP,
        name="index_partial_%d" % len(chips),
    )(*keys, token, former, *args)


def log_add(one, two):
    top = jnp.maximum(one, two)
    return top + jnp.log(jnp.exp(one - top) + jnp.exp(two - top))


def split_three(value, lane, start):
    pieces = jnp.zeros(lane.shape, jnp.float32)
    for step in range(3):
        piece = value.astype(jnp.bfloat16).astype(jnp.float32)
        pieces = jnp.where(lane == start + step, piece, pieces)
        value = value - piece
    return pieces


def join_three(pieces, start):
    wide = pieces.astype(jnp.float32)
    return wide[:, start : start + 1] + wide[:, start + 1 : start + 2] + wide[:, start + 2 : start + 3]


def four_sum(refs):
    width = refs[0].shape[1] - STAT
    parts = [ref[:, :width].astype(jnp.float32) for ref in refs]
    logs = [join_three(ref[:, width:], 0) for ref in refs]
    return (parts[0] + parts[1]) + (parts[2] + parts[3]), log_add(log_add(logs[0], logs[1]), log_add(logs[2], logs[3]))


def middle_kernel(own_ref, far_ref, right_ref, left_ref, out_ref):
    summed, logs = four_sum((own_ref, far_ref, right_ref, left_ref))
    width = summed.shape[1]
    out_ref[:, :width] = summed.astype(jnp.bfloat16)
    lane = lax.broadcasted_iota(jnp.int32, (PAIRS, STAT), 1)
    out_ref[:, width:] = split_three(logs, lane, 0).astype(jnp.bfloat16)


def final_kernel(own_ref, far_ref, right_ref, left_ref, out_ref, log_ref):
    summed, logs = four_sum((own_ref, far_ref, right_ref, left_ref))
    steps, local = log_ref.shape
    flat = jnp.broadcast_to(logs, (PAIRS, STAT)).T[:1, :]
    for step in range(steps):
        out_ref[step] = summed[step * local : (step + 1) * local, :].astype(jnp.bfloat16)
        log_ref[step : step + 1, :] = flat[:, step * local : (step + 1) * local]


def summed_over(value, shift, final):
    parts = (value,) + tuple(lax.ppermute(value, BOTH, shift(step)) for step in (2, 1, 3))
    if final:
        out_shape = (
            jax.ShapeDtypeStruct(final + (value.shape[1] - STAT,), jnp.bfloat16),
            jax.ShapeDtypeStruct(final, jnp.float32),
        )
        out_specs = (vmem(), vmem())
    else:
        out_shape = jax.ShapeDtypeStruct(value.shape, jnp.bfloat16)
        out_specs = vmem()
    return pl.pallas_call(
        final_kernel if final else middle_kernel,
        out_shape=out_shape,
        in_specs=[vmem()] * 4,
        out_specs=out_specs,
        compiler_params=pltpu.CompilerParams(vmem_limit_bytes=4 << 20),
        cost_estimate=CHEAP,
        name="sum_last" if final else "sum_first",
    )(*parts)


def prepare_kernel(latent_ref, query_ref, gate_ref, key_ref, block_ref, key_out_ref, latent, queries, gates, keys, sems):
    depth = KV // CHUNKS
    copies = [
        pltpu.make_async_copy(
            latent_ref.at[pl.ds(part * depth, depth)], latent.at[pl.ds(part * depth, depth)], sems.at[part]
        )
        for part in range(CHUNKS)
    ]
    others = [
        pltpu.make_async_copy(query_ref, queries, sems.at[CHUNKS]),
        pltpu.make_async_copy(gate_ref, gates, sems.at[CHUNKS + 1]),
        pltpu.make_async_copy(key_ref, keys, sems.at[CHUNKS + 2]),
    ]
    for copy in copies + others:
        copy.start()
    for part, copy in enumerate(copies):
        copy.wait()
        start = part * depth + (MIDDLE if part >= CHUNKS // 2 else 0)
        block_ref[start : start + depth, :] = latent[part * depth : (part + 1) * depth, :].astype(jnp.bfloat16)
    for copy in others:
        copy.wait()
    first = KV // 2
    block_ref[first + 64 : first + MIDDLE, :] = jnp.zeros((MIDDLE - 64, ROWS), jnp.bfloat16)
    lines = []
    for step in range(query_ref.shape[0]):
        for local in range(query_ref.shape[1]):
            pair = step * query_ref.shape[1] + local
            block_ref[first : first + 64, pair * IDX : (pair + 1) * IDX] = queries[step, local]
            lines.append(gates[step, local : local + 1, :].astype(jnp.float32))
    lines = jnp.concatenate(lines + [jnp.zeros((8, 64), jnp.float32)], axis=0)
    block_ref[first + 64 : first + 80, :64] = lines.astype(jnp.bfloat16)
    key_out_ref[...] = keys[...].astype(jnp.bfloat16)


def prepare(latent, index_queries, index_gates, index_keys):
    args = (latent, index_queries, index_gates, index_keys)
    return pl.pallas_call(
        prepare_kernel,
        out_shape=(
            jax.ShapeDtypeStruct((WIDE, ROWS), jnp.bfloat16),
            jax.ShapeDtypeStruct(index_keys.shape, jnp.bfloat16),
        ),
        in_specs=[pl.BlockSpec(memory_space=pl.ANY)] * 4,
        out_specs=(vmem(), vmem()),
        scratch_shapes=[pltpu.VMEM(arg.shape, arg.dtype) for arg in args] + [pltpu.SemaphoreType.DMA((CHUNKS + 3,))],
        compiler_params=pltpu.CompilerParams(vmem_limit_bytes=12 << 20),
        cost_estimate=CHEAP,
        name="prepare",
    )(*[pltpu.with_memory_space_constraint(arg, pltpu.HBM) for arg in args])


def x_shift(step):
    return [(x * 2 + c, ((x + step) % 4) * 2 + c) for x in range(4) for c in range(2)]


BOTH = ("pre", "tp")


def plane_shift(step, along_y):
    pairs = []
    for p in range(PRE):
        for z in range(4):
            for y in range(4):
                to_y = along_y == (p % 2 == 0)
                there = z * 4 + (y + step) % 4 if to_y else ((z + step) % 4) * 4 + y
                pairs.append((p * TP + z * 4 + y, p * TP + there))
    return pairs


def first_shift(step):
    return plane_shift(step, True)


def second_shift(step):
    return plane_shift(step, False)


CORE_SWAP = [(i, i ^ 1) for i in range(PRE)]


def on_device(
    latent_rows,
    index_keys,
    queries,
    index_queries,
    index_gates,
    value_proj,
    out_proj,
    block_rows,
    block_owner,
    block_count,
):
    block, keys = prepare(latent_rows.T, index_queries, index_gates, index_keys)
    forward = lax.ppermute(block, "pre", x_shift(1))
    backward = lax.ppermute(block, "pre", x_shift(3))

    own_queries = queries.reshape(PAIRS * HEADS, KV)
    row = jnp.concatenate(
        [own_queries] + [lax.ppermute(own_queries, BOTH, first_shift(4 - step)) for step in (1, 2, 3)], axis=0
    )
    plane = [row] + [lax.ppermute(row, BOTH, second_shift(4 - step)) for step in (1, 2, 3)]

    def swapped(part):
        return lax.ppermute(part, "pre", CORE_SWAP)

    def both(parts):
        return [list(parts), [swapped(part) for part in parts]]

    masks, positions, counts = make_tables(block_rows, block_owner, block_count)
    token = arrived(plane[1:] + [masks])
    forward, backward, block, keys, token = lax.optimization_barrier((forward, backward, block, keys, token))
    top, low = halves(forward, backward)
    far = [lax.ppermute(top, "pre", x_shift(1)), lax.ppermute(low, "pre", x_shift(3))]

    own, sides = both([block]), both([forward]) + both([backward])
    keys = [keys, swapped(keys)]
    packs = [
        pack(base, early, masks, positions, rows)
        for base, early, rows in ((0, keys[1], sides[:2]), (2, token, own), (4, token, sides[2:]))
    ]
    states, token = attend(0, counts, plane, masks, positions, packs, sides[:2] + own + sides[2:])
    partial = index_partial((0, 1, -1), keys, token, token, (own[0], sides[2], sides[0]))
    far, partial = lax.optimization_barrier((far, partial))
    far = both(far)
    packs = [pack(6, partial, masks, positions, far)]

    payloads = [None] * 4
    parts = [None] * 4
    for step in (2, 1, 3, 0):
        one = slice(step, step + 1)
        payloads[step] = attend(6, counts, plane[one], masks, positions, packs, far, states[one], last=True)[0]
        parts[step] = lax.ppermute(payloads[step], BOTH, second_shift(step)) if step else payloads[0]
    parts = combine(parts)
    received = [parts[0]] + [lax.ppermute(parts[step], BOTH, first_shift(step)) for step in (2, 1, 3)]
    partial = index_partial((2,), keys, payloads[3], partial, (far[0],))
    parts = [lax.ppermute(partial, "pre", x_shift(step)) for step in (2, 1, 3)]
    partial = log_add(log_add(partial, parts[0]), log_add(parts[1], parts[2]))
    part_out = project(received, value_proj, out_proj, partial)
    return summed_over(summed_over(part_out, first_shift, None), second_shift, queries.shape[:2])


def solution(mesh):
    placed = (
        P(("pre", "tp"), None),
        P(("pre", "tp"), None),
        P(None, "pre", "tp", None),
        P(None, "pre", None, None),
        P(None, "pre", None),
        P("tp", None, None),
        P("tp", None),
        P(None, "pre", None, None),
        P(None, "pre", None),
        P(None, "pre", None),
    )
    return jax.shard_map(
        on_device,
        mesh=mesh,
        in_specs=placed,
        out_specs=(P(None, "pre", None), P(None, "pre")),
        check_vma=False,
    )
```

```python
import jax
import jax.numpy as jnp
from jax import lax
from jax.experimental import pallas as pl
from jax.experimental.pallas import tpu as pltpu
from jax.sharding import PartitionSpec as P

IDX = 128
LAT = 512
KV = 576
BLOCK = 64
PRE = 8
TP = 16
PAIRS = 8
HEADS = 8
ROWS = 1024
PACK = 256
MIDDLE = 80
TOP = KV // 2 + 48
WIDE = KV + MIDDLE
CHUNKS = 6
QTILE = 256
STAT = 128
QROWS = TP * PAIRS * HEADS
LOWEST = -3.0e38
SOFT_SCALE = 192.0 ** (-0.5)
LOG2E = 1.4426950408889634
SCORE_SCALE = SOFT_SCALE * LOG2E

NT = (((1,), (1,)), ((), ()))


CHEAP = pl.CostEstimate(flops=1000, bytes_accessed=1000, transcendentals=0)


def vmem():
    return pl.BlockSpec(memory_space=pltpu.VMEM)


def smem():
    return pl.BlockSpec(memory_space=pltpu.SMEM)


def table_kernel(rows_ref, owner_ref, count_ref, mask_ref, pos_ref, total_ref):
    me_pre = lax.axis_index("pre")
    me_tp = lax.axis_index("tp")
    number = rows_ref.shape[2]
    before = (
        lax.broadcasted_iota(jnp.int32, (number, number), 0) < lax.broadcasted_iota(jnp.int32, (number, number), 1)
    ).astype(jnp.float32).astype(jnp.bfloat16)
    slot = lax.broadcasted_iota(jnp.int32, (8, number), 0).astype(jnp.float32)
    entry = lax.broadcasted_iota(jnp.int32, (8, BLOCK), 1).astype(jnp.float32)
    high_iota = lax.broadcasted_iota(jnp.int32, (PRE * 8, BLOCK), 0).astype(jnp.float32)
    low_iota = lax.broadcasted_iota(jnp.int32, (128, BLOCK), 0).astype(jnp.float32)
    for pair in range(PAIRS):
        step, local = pair // rows_ref.shape[1], pair % rows_ref.shape[1]
        rows = rows_ref[step, local]
        source = rows >> 10
        relative = ((((source >> 1) - (me_pre >> 1) + 1) & 3) << 1) | ((source ^ me_pre) & 1)
        high = ((relative << 3) | ((rows >> 7) & 7)).astype(jnp.float32).astype(jnp.bfloat16)
        low = (rows & 127).astype(jnp.float32).astype(jnp.bfloat16)
        owned = jnp.where(owner_ref[step, local : local + 1, :] == me_tp, 1.0, 0.0)
        rank = jnp.dot(owned.astype(jnp.bfloat16), before, preferred_element_type=jnp.float32)
        choose = jnp.where(slot == rank, owned, 0.0)
        limit = jnp.sum(choose * count_ref[step, local : local + 1, :].astype(jnp.float32), axis=1, keepdims=True)
        choose = choose.astype(jnp.bfloat16)
        valid = entry < limit
        high = jnp.where(valid, jnp.dot(choose, high, preferred_element_type=jnp.float32), -1.0)
        low = jnp.dot(choose, low, preferred_element_type=jnp.float32)
        chosen = jnp.zeros((PRE * 8, 128), jnp.float32)
        for block in range(number // TP):
            high_one = jnp.where(high_iota == high[block : block + 1, :], 1.0, 0.0).astype(jnp.bfloat16)
            low_one = jnp.where(low_iota == low[block : block + 1, :], 1.0, 0.0).astype(jnp.bfloat16)
            chosen = chosen + lax.dot_general(high_one, low_one, NT, preferred_element_type=jnp.float32)
        for block in range(PRE):
            for part in range(8):
                mask_ref[block, pair : pair + 1, part * 128 : (part + 1) * 128] = chosen[
                    block * 8 + part : block * 8 + part + 1, :
                ]
    union = jnp.concatenate([jnp.max(mask_ref[block], axis=0, keepdims=True) for block in range(PRE)], axis=0)
    before = (
        lax.broadcasted_iota(jnp.int32, (128, 128), 0) < lax.broadcasted_iota(jnp.int32, (128, 128), 1)
    ).astype(jnp.float32).astype(jnp.bfloat16)
    carry = jnp.zeros((PRE, 1), jnp.float32)
    for part in range(8):
        piece = union[:, part * 128 : (part + 1) * 128]
        ahead = jnp.dot(piece.astype(jnp.bfloat16), before, preferred_element_type=jnp.float32) + carry
        pos_ref[:, part * 128 : (part + 1) * 128] = jnp.where(piece > 0.0, ahead, -1.0)
        carry = carry + jnp.sum(piece, axis=1, keepdims=True)
    total_ref[...] = jnp.broadcast_to(carry, (PRE, 128)).astype(jnp.int32)


def make_tables(block_rows, block_owner, block_count):
    return pl.pallas_call(
        table_kernel,
        out_shape=(
            jax.ShapeDtypeStruct((PRE, PAIRS, ROWS), jnp.float32),
            jax.ShapeDtypeStruct((PRE, ROWS), jnp.float32),
            jax.ShapeDtypeStruct((PRE, 128), jnp.int32),
        ),
        in_specs=[vmem()] * 3,
        out_specs=(vmem(), vmem(), vmem()),
        compiler_params=pltpu.CompilerParams(vmem_limit_bytes=8 << 20),
        cost_estimate=CHEAP,
        name="row_tables",
    )(block_rows, block_owner, block_count)


TOKEN = jax.ShapeDtypeStruct((8, 128), jnp.float32)


def token_kernel(*refs):
    refs[-1][...] = jnp.zeros(refs[-1].shape, jnp.float32)


def arrived(values):
    return pl.pallas_call(
        token_kernel,
        out_shape=TOKEN,
        in_specs=[pl.BlockSpec(memory_space=pl.ANY)] * len(values),
        out_specs=vmem(),
        compiler_params=pltpu.CompilerParams(vmem_limit_bytes=2 << 20),
        cost_estimate=CHEAP,
        name="arrived",
    )(*values)


def halves_kernel(forward_ref, backward_ref, top_ref, low_ref):
    top_ref[...] = forward_ref[:TOP, :]
    low_ref[...] = backward_ref[TOP:, :]


def halves(forward, backward):
    return pl.pallas_call(
        halves_kernel,
        out_shape=(
            jax.ShapeDtypeStruct((TOP, ROWS), forward.dtype),
            jax.ShapeDtypeStruct((WIDE - TOP, ROWS), forward.dtype),
        ),
        in_specs=[vmem()] * 2,
        out_specs=(vmem(),) * 2,
        compiler_params=pltpu.CompilerParams(vmem_limit_bytes=8 << 20),
        cost_estimate=CHEAP,
        name="halves",
    )(forward, backward)


def pack_block(number, pieces, mask_row, pos_row, packed_ref, first_lane):
    slot = (lax.broadcasted_iota(jnp.int32, (PACK, ROWS), 0) + number * PACK).astype(jnp.float32)
    pick = jnp.where(slot == pos_row, 1.0, 0.0).astype(jnp.bfloat16)
    depth = KV // len(pieces)
    for order, piece in enumerate(pieces):
        packed = lax.dot_general(piece, pick, NT, preferred_element_type=jnp.float32)
        packed_ref[order * depth : (order + 1) * depth, first_lane : first_lane + PACK] = packed.astype(jnp.bfloat16)
    present = lax.dot_general(mask_row.astype(jnp.bfloat16), pick, NT, preferred_element_type=jnp.float32)
    return jnp.where(present > 0.5, 0.0, -jnp.inf)


def latent_parts(refs):
    half = KV // 2
    if len(refs) == 1:
        return [refs[0].at[pl.ds(0, half), :], refs[0].at[pl.ds(half + MIDDLE, half), :]]
    return [refs[0].at[pl.ds(0, half), :], refs[1].at[pl.ds(KV // 2 + MIDDLE - TOP, half), :]]


def pack_kernel(base, parts, unused_ref, mask_ref, pos_ref, *refs):
    packed_ref, absent_ref = refs[-2:]
    for block, number in enumerate(parts):
        pieces, refs = refs[:number], refs[number:]
        row = base + block
        absent_ref[:, block * PACK : (block + 1) * PACK] = pack_block(
            0, [part[...] for part in latent_parts(pieces)], mask_ref[row], pos_ref[row : row + 1, :], packed_ref,
            block * PACK,
        )


def pack(base, token, masks, positions, sources):
    parts = [len(pieces) for pieces in sources]
    rows = sum([list(pieces) for pieces in sources], [])

    def body(*refs):
        pack_kernel(base, parts, *refs)

    return pl.pallas_call(
        body,
        out_shape=(
            jax.ShapeDtypeStruct((KV, len(parts) * PACK), jnp.bfloat16),
            jax.ShapeDtypeStruct((PAIRS, len(parts) * PACK), jnp.float32),
        ),
        in_specs=[pl.BlockSpec(memory_space=pl.ANY)] + [vmem()] * (2 + len(rows)),
        out_specs=(vmem(), vmem()),
        compiler_params=pltpu.CompilerParams(vmem_limit_bytes=16 << 20),
        cost_estimate=CHEAP,
        name="pack_%d" % len(parts),
    )(token, masks, positions, *rows)


def attend_kernel(base, parts, shapes, first, last, count_ref, mask_ref, pos_ref, *refs):
    queries, refs = refs[: shapes[0]], refs[shapes[0] :]
    packs, refs = refs[: 2 * shapes[1]], refs[2 * shapes[1] :]
    sources = []
    for number in parts:
        sources.append(refs[:number])
        refs = refs[number:]
    groups = len(queries)
    if not first:
        former_state, refs = refs[: 2 * groups], refs[2 * groups :]
    if last:
        outs, refs = refs[:groups], refs[groups:]
    state, refs = refs[: 2 * groups], refs[2 * groups :]
    if not last:
        refs[0][...] = jnp.zeros(refs[0].shape, jnp.float32)
        refs = refs[1:]
    packed_ref, rows_ref, sem = refs
    column = lax.broadcasted_iota(jnp.int32, (QTILE, STAT), 1)

    def attention(packed, absent, fresh):
        span = absent.shape[1]
        for group in range(groups):
            stat_ref, acc_ref = state[2 * group], state[2 * group + 1]
            query = queries[group][...]
            scores = [jnp.dot(query, ref[...], preferred_element_type=jnp.float32) for ref in packed]
            scores = scores[0] if len(scores) == 1 else jnp.concatenate(scores, axis=1)
            scores = scores.reshape(QTILE // 64, PAIRS, HEADS, span) * SCORE_SCALE + absent[None, :, None, :]
            scores = scores.reshape(QTILE, span)
            newer = jnp.max(scores, axis=1, keepdims=True)
            if fresh and first:
                newer = jnp.maximum(newer, LOWEST)
            else:
                stats, acc = (former_state[2 * group], former_state[2 * group + 1]) if fresh else (stat_ref, acc_ref)
                former = stats[:, :1]
                newer = jnp.maximum(former, newer)
                decay = jnp.exp2(former - newer)
            weights = jnp.exp2(scores - newer)
            total = jnp.sum(weights, axis=1, keepdims=True)
            weights = weights.astype(jnp.bfloat16)
            added, start = None, 0
            for ref in packed:
                width = ref.shape[1]
                piece = lax.dot_general(
                    weights[:, start : start + width], ref[:LAT, :], NT, preferred_element_type=jnp.float32
                )
                added = piece if added is None else added + piece
                start += width
            if not (fresh and first):
                total = stats[:, STAT // 2 : STAT // 2 + 1] * decay + total
                added = acc[...] * decay + added
            acc_ref[...] = added
            stat_ref[...] = jnp.where(column < STAT // 2, newer, total)

    attention(packs[::2], jnp.concatenate([ref[...] for ref in packs[1::2]], axis=1), True)

    for block in range(len(parts)):
        row = base + block
        rounds = (count_ref[row, 0] + (PACK - 1)) // PACK

        @pl.when(rounds > 1)
        def _(block=block, row=row, rounds=rounds):
            for order, piece in enumerate(latent_parts(sources[block])):
                copy = pltpu.make_async_copy(piece, rows_ref.at[pl.ds(order * (KV // 2), KV // 2), :], sem)
                copy.start()
                copy.wait()

            @pl.loop(1, rounds)
            def _(number):
                absent = pack_block(
                    number, [rows_ref[...]], mask_ref[row], pos_ref[row : row + 1, :], packed_ref, 0
                )
                attention([packed_ref], absent, False)

    if last:
        for group in range(groups):
            stat_ref, acc_ref = state[2 * group], state[2 * group + 1]
            write_payload(outs[group], stat_ref[:, :1], stat_ref[:, STAT // 2 : STAT // 2 + 1], acc_ref[...])


def write_payload(out_ref, highest, total, acc):
    lane = lax.broadcasted_iota(jnp.int32, (acc.shape[0], STAT), 1)
    out_ref[:, :LAT] = acc.astype(jnp.bfloat16)
    out_ref[:, LAT:] = (split_three(highest, lane, 0) + split_three(total, lane, 3)).astype(jnp.bfloat16)


def attend(base, counts, queries, masks, positions, packs, sources, states=None, last=False):
    parts = [len(pieces) for pieces in sources]
    first = states is None
    groups = len(queries)
    shapes = (
        jax.ShapeDtypeStruct((QTILE, STAT), jnp.float32),
        jax.ShapeDtypeStruct((QTILE, LAT), jnp.float32),
    ) * groups
    if last:
        out_shape = (jax.ShapeDtypeStruct((QTILE, LAT + STAT), jnp.bfloat16),) * groups
        scratch = [pltpu.VMEM(s.shape, s.dtype) for s in shapes]
    else:
        out_shape = shapes + (TOKEN,)
        scratch = []
    scratch = scratch + [
        pltpu.VMEM((KV, PACK), jnp.bfloat16),
        pltpu.VMEM((KV, ROWS), jnp.bfloat16),
        pltpu.SemaphoreType.DMA(()),
    ]
    packed = sum([list(pair) for pair in packs], [])
    rows = [pltpu.with_memory_space_constraint(piece, pltpu.HBM) for pieces in sources for piece in pieces]
    former = [] if first else [part for state in states for part in state]

    def body(*refs):
        attend_kernel(base, parts, (groups, len(packs)), first, last, *refs)

    in_specs = [smem()] + [vmem()] * (2 + groups + len(packed))
    in_specs = in_specs + [pl.BlockSpec(memory_space=pl.ANY)] * len(rows) + [vmem()] * len(former)
    outs = pl.pallas_call(
        body,
        out_shape=out_shape,
        in_specs=in_specs,
        out_specs=(vmem(),) * len(out_shape),
        scratch_shapes=scratch,
        compiler_params=pltpu.CompilerParams(vmem_limit_bytes=16 << 20),
        cost_estimate=CHEAP,
        name="attend_%d_%d" % (len(parts), groups),
    )(counts, masks, positions, *queries, *packed, *rows, *former)
    if last:
        return list(outs)
    return [tuple(outs[2 * group : 2 * group + 2]) for group in range(groups)], outs[-1]


def combined(refs):
    row = lax.broadcasted_iota(jnp.int32, (STAT, 2 * STAT), 0)
    col = lax.broadcasted_iota(jnp.int32, (STAT, 2 * STAT), 1)
    spread = jnp.where((row // 3) == (col // STAT), 1.0, 0.0).astype(jnp.bfloat16)
    stats = [jnp.dot(ref[:, LAT:], spread, preferred_element_type=jnp.float32) for ref in refs]
    highest = stats[0][:, :STAT]
    for stat in stats[1:]:
        highest = jnp.maximum(highest, stat[:, :STAT])
    total, acc = None, None
    for ref, stat in zip(refs, stats):
        weight = jnp.exp2(stat[:, :STAT] - highest)
        wide = jnp.concatenate([weight] * (LAT // STAT), axis=1) * ref[:, :LAT].astype(jnp.float32)
        total = weight * stat[:, STAT:] if total is None else total + weight * stat[:, STAT:]
        acc = wide if acc is None else acc + wide
    return highest, total, acc


def combine_kernel(*refs):
    highest, total, acc = combined(refs[:4])
    for part, out_ref in enumerate(refs[4:]):
        here = slice(part * PAIRS * HEADS, (part + 1) * PAIRS * HEADS)
        write_payload(out_ref, highest[here, :1], total[here, :1], acc[here, :])


def combine(parts):
    return pl.pallas_call(
        combine_kernel,
        out_shape=(jax.ShapeDtypeStruct((PAIRS * HEADS, LAT + STAT), jnp.bfloat16),) * 4,
        in_specs=[vmem()] * 4,
        out_specs=(vmem(),) * 4,
        compiler_params=pltpu.CompilerParams(vmem_limit_bytes=8 << 20),
        cost_estimate=CHEAP,
        name="combine",
    )(*parts)


def project_kernel(value_ref, weights, partial_ref, *refs):
    out_ref = refs[4]
    highest, total, acc = combined(refs[:4])
    attn = (acc / jnp.concatenate([total] * (LAT // STAT), axis=1)).astype(jnp.bfloat16)
    head_of = lax.broadcasted_iota(jnp.int32, (PAIRS, HEADS, 128), 1)
    pieces = []
    for head in range(HEADS):
        product = jnp.dot(attn, value_ref[head], preferred_element_type=jnp.float32)
        product = jnp.where(head_of == head, product.reshape(PAIRS, HEADS, 128), 0.0)
        pieces.append(jnp.sum(product, axis=1))
    values = jnp.concatenate(pieces, axis=1).astype(jnp.bfloat16)
    width = weights.shape[1]
    result = jnp.dot(values, weights[...], preferred_element_type=jnp.float32)
    out_ref[:, :width] = result.astype(jnp.bfloat16)
    lane = lax.broadcasted_iota(jnp.int32, (PAIRS, STAT), 1)
    group = lax.axis_index("pre")
    mine = jnp.sum(jnp.where(lane == group, partial_ref[...], 0.0), axis=1, keepdims=True)
    out_ref[:, width:] = split_three(mine, lane, 0).astype(jnp.bfloat16)


def project(received, value_proj, out_proj, partial):
    return pl.pallas_call(
        project_kernel,
        out_shape=jax.ShapeDtypeStruct((PAIRS, out_proj.shape[1] + STAT), jnp.bfloat16),
        in_specs=[vmem()] * 7,
        out_specs=vmem(),
        compiler_params=pltpu.CompilerParams(vmem_limit_bytes=16 << 20),
        cost_estimate=CHEAP,
        name="project",
    )(value_proj, pltpu.with_memory_space_constraint(out_proj, pltpu.VMEM), partial, *received)


def index_kernel(chips, first_keys, second_keys, unused_ref, *refs):
    place = lax.axis_index("pre")
    former_ref, middles, out_ref, slab_ref = refs[0], refs[1:-2], refs[-2], refs[-1]
    lane = lax.broadcasted_iota(jnp.int32, (PAIRS, 128), 1)
    result = former_ref[...]
    for chip in chips:
        uses, middles = middles[: 1 if chip < 2 else 2], middles[1 if chip < 2 else 2 :]
        first, last = KV // 2, KV // 2 + MIDDLE
        if chip < 2:
            middle = uses[0][first:last, :]
        else:
            middle = jnp.concatenate([uses[0][first:TOP, :], uses[1][: last - TOP, :]], axis=0)
        for pair in range(PAIRS):
            slab_ref[pair * 64 : (pair + 1) * 64, :] = middle[:64, pair * IDX : (pair + 1) * IDX]
        gates = middle[64:80, :64].astype(jnp.float32)
        lines = [jnp.concatenate([gates[2 * line : 2 * line + 1], gates[2 * line + 1 : 2 * line + 2]], axis=1) for line in range(4)]
        columns = jnp.concatenate(lines + [jnp.zeros((124, 128), jnp.float32)], axis=0).T
        group = (((place >> 1) + chip) & 3) * 2 + (place & 1)
        sums = []
        for keys in (first_keys, second_keys):
            scores = []
            for part in range(4):
                logits = lax.dot_general(
                    slab_ref[part * 128 : (part + 1) * 128, :], keys[...], NT, preferred_element_type=jnp.float32
                )
                gated = jnp.maximum(logits, 0.0) * columns[:, part : part + 1]
                scores.append(jnp.sum(gated.reshape(2, 64, ROWS), axis=1))
            scores = jnp.concatenate(scores, axis=0) * IDX ** (-0.5)
            largest = jnp.max(scores, axis=1, keepdims=True)
            sums.append(largest + jnp.log(jnp.sum(jnp.exp(scores - largest), axis=1, keepdims=True)))
        result = jnp.where(lane == group, log_add(sums[0], sums[1]), result)
    out_ref[...] = result


def index_partial(chips, keys, token, former, blocks):
    args = [part for parts in blocks for part in parts]

    def body(*refs):
        index_kernel(chips, *refs)

    return pl.pallas_call(
        body,
        out_shape=jax.ShapeDtypeStruct((PAIRS, 128), jnp.float32),
        in_specs=[vmem()] * 2 + [pl.BlockSpec(memory_space=pl.ANY)] + [vmem()] * (1 + len(args)),
        out_specs=vmem(),
        scratch_shapes=[pltpu.VMEM((PAIRS * 64, IDX), jnp.bfloat16)],
        compiler_params=pltpu.CompilerParams(vmem_limit_bytes=16 << 20),
        cost_estimate=CHEAP,
        name="index_partial_%d" % len(chips),
    )(*keys, token, former, *args)


def log_add(one, two):
    top = jnp.maximum(one, two)
    return top + jnp.log(jnp.exp(one - top) + jnp.exp(two - top))


def split_three(value, lane, start):
    pieces = jnp.zeros(lane.shape, jnp.float32)
    for step in range(3):
        piece = value.astype(jnp.bfloat16).astype(jnp.float32)
        pieces = jnp.where(lane == start + step, piece, pieces)
        value = value - piece
    return pieces


def join_three(pieces, start):
    wide = pieces.astype(jnp.float32)
    return wide[:, start : start + 1] + wide[:, start + 1 : start + 2] + wide[:, start + 2 : start + 3]


def four_sum(refs):
    width = refs[0].shape[1] - STAT
    parts = [ref[:, :width].astype(jnp.float32) for ref in refs]
    logs = [join_three(ref[:, width:], 0) for ref in refs]
    return (parts[0] + parts[1]) + (parts[2] + parts[3]), log_add(log_add(logs[0], logs[1]), log_add(logs[2], logs[3]))


def middle_kernel(own_ref, far_ref, right_ref, left_ref, out_ref):
    summed, logs = four_sum((own_ref, far_ref, right_ref, left_ref))
    width = summed.shape[1]
    out_ref[:, :width] = summed.astype(jnp.bfloat16)
    lane = lax.broadcasted_iota(jnp.int32, (PAIRS, STAT), 1)
    out_ref[:, width:] = split_three(logs, lane, 0).astype(jnp.bfloat16)


def final_kernel(own_ref, far_ref, right_ref, left_ref, out_ref, log_ref):
    summed, logs = four_sum((own_ref, far_ref, right_ref, left_ref))
    steps, local = log_ref.shape
    flat = jnp.broadcast_to(logs, (PAIRS, STAT)).T[:1, :]
    for step in range(steps):
        out_ref[step] = summed[step * local : (step + 1) * local, :].astype(jnp.bfloat16)
        log_ref[step : step + 1, :] = flat[:, step * local : (step + 1) * local]


def summed_over(value, shift, final):
    parts = (value,) + tuple(lax.ppermute(value, BOTH, shift(step)) for step in (2, 1, 3))
    if final:
        out_shape = (
            jax.ShapeDtypeStruct(final + (value.shape[1] - STAT,), jnp.bfloat16),
            jax.ShapeDtypeStruct(final, jnp.float32),
        )
        out_specs = (vmem(), vmem())
    else:
        out_shape = jax.ShapeDtypeStruct(value.shape, jnp.bfloat16)
        out_specs = vmem()
    return pl.pallas_call(
        final_kernel if final else middle_kernel,
        out_shape=out_shape,
        in_specs=[vmem()] * 4,
        out_specs=out_specs,
        compiler_params=pltpu.CompilerParams(vmem_limit_bytes=4 << 20),
        cost_estimate=CHEAP,
        name="sum_last" if final else "sum_first",
    )(*parts)


def prepare_kernel(latent_ref, query_ref, gate_ref, key_ref, block_ref, key_out_ref, latent, queries, gates, keys, sems):
    depth = KV // CHUNKS
    copies = [
        pltpu.make_async_copy(
            latent_ref.at[pl.ds(part * depth, depth)], latent.at[pl.ds(part * depth, depth)], sems.at[part]
        )
        for part in range(CHUNKS)
    ]
    others = [
        pltpu.make_async_copy(query_ref, queries, sems.at[CHUNKS]),
        pltpu.make_async_copy(gate_ref, gates, sems.at[CHUNKS + 1]),
        pltpu.make_async_copy(key_ref, keys, sems.at[CHUNKS + 2]),
    ]
    for copy in copies + others:
        copy.start()
    for part, copy in enumerate(copies):
        copy.wait()
        start = part * depth + (MIDDLE if part >= CHUNKS // 2 else 0)
        block_ref[start : start + depth, :] = latent[part * depth : (part + 1) * depth, :].astype(jnp.bfloat16)
    for copy in others:
        copy.wait()
    first = KV // 2
    block_ref[first + 64 : first + MIDDLE, :] = jnp.zeros((MIDDLE - 64, ROWS), jnp.bfloat16)
    lines = []
    for step in range(query_ref.shape[0]):
        for local in range(query_ref.shape[1]):
            pair = step * query_ref.shape[1] + local
            block_ref[first : first + 64, pair * IDX : (pair + 1) * IDX] = queries[step, local]
            lines.append(gates[step, local : local + 1, :].astype(jnp.float32))
    lines = jnp.concatenate(lines + [jnp.zeros((8, 64), jnp.float32)], axis=0)
    block_ref[first + 64 : first + 80, :64] = lines.astype(jnp.bfloat16)
    key_out_ref[...] = keys[...].astype(jnp.bfloat16)


def prepare(latent, index_queries, index_gates, index_keys):
    args = (latent, index_queries, index_gates, index_keys)
    return pl.pallas_call(
        prepare_kernel,
        out_shape=(
            jax.ShapeDtypeStruct((WIDE, ROWS), jnp.bfloat16),
            jax.ShapeDtypeStruct(index_keys.shape, jnp.bfloat16),
        ),
        in_specs=[pl.BlockSpec(memory_space=pl.ANY)] * 4,
        out_specs=(vmem(), vmem()),
        scratch_shapes=[pltpu.VMEM(arg.shape, arg.dtype) for arg in args] + [pltpu.SemaphoreType.DMA((CHUNKS + 3,))],
        compiler_params=pltpu.CompilerParams(vmem_limit_bytes=12 << 20),
        cost_estimate=CHEAP,
        name="prepare",
    )(*[pltpu.with_memory_space_constraint(arg, pltpu.HBM) for arg in args])


def x_shift(step):
    return [(x * 2 + c, ((x + step) % 4) * 2 + c) for x in range(4) for c in range(2)]


BOTH = ("pre", "tp")


def plane_shift(step, along_y):
    pairs = []
    for p in range(PRE):
        for z in range(4):
            for y in range(4):
                to_y = along_y == (p % 2 == 0)
                there = z * 4 + (y + step) % 4 if to_y else ((z + step) % 4) * 4 + y
                pairs.append((p * TP + z * 4 + y, p * TP + there))
    return pairs


def first_shift(step):
    return plane_shift(step, True)


def second_shift(step):
    return plane_shift(step, False)


CORE_SWAP = [(i, i ^ 1) for i in range(PRE)]


def on_device(
    latent_rows,
    index_keys,
    queries,
    index_queries,
    index_gates,
    value_proj,
    out_proj,
    block_rows,
    block_owner,
    block_count,
):
    block, keys = prepare(latent_rows.T, index_queries, index_gates, index_keys)
    forward = lax.ppermute(block, "pre", x_shift(1))
    backward = lax.ppermute(block, "pre", x_shift(3))

    own_queries = queries.reshape(PAIRS * HEADS, KV)
    row = jnp.concatenate(
        [own_queries] + [lax.ppermute(own_queries, BOTH, first_shift(4 - step)) for step in (1, 2, 3)], axis=0
    )
    plane = [row] + [lax.ppermute(row, BOTH, second_shift(4 - step)) for step in (1, 2, 3)]

    def swapped(part):
        return lax.ppermute(part, "pre", CORE_SWAP)

    def both(parts):
        return [list(parts), [swapped(part) for part in parts]]

    masks, positions, counts = make_tables(block_rows, block_owner, block_count)
    token = arrived(plane[1:] + [masks])
    forward, backward, block, keys, token = lax.optimization_barrier((forward, backward, block, keys, token))
    top, low = halves(forward, backward)
    far = [lax.ppermute(top, "pre", x_shift(1)), lax.ppermute(low, "pre", x_shift(3))]

    own, sides = both([block]), both([forward]) + both([backward])
    keys = [keys, swapped(keys)]
    packs = [
        pack(base, early, masks, positions, rows)
        for base, early, rows in ((0, keys[1], sides[:2]), (2, token, own), (4, token, sides[2:]))
    ]
    states, token = attend(0, counts, plane, masks, positions, packs, sides[:2] + own + sides[2:])
    partial = index_partial((0, 1, -1), keys, token, token, (own[0], sides[2], sides[0]))
    far, partial = lax.optimization_barrier((far, partial))
    far = both(far)
    packs = [pack(6, partial, masks, positions, far)]

    payloads, parts = [None] * 4, [None] * 4
    for group in ((2,), (1, 3), (0,)):
        outs = attend(
            6, counts, [plane[step] for step in group], masks, positions, packs, far,
            [states[step] for step in group], last=True,
        )
        for step, out in zip(group, outs):
            payloads[step] = out
            parts[step] = lax.ppermute(out, BOTH, second_shift(step)) if step else out
    parts = combine(parts)
    received = [parts[0]] + [lax.ppermute(parts[step], BOTH, first_shift(step)) for step in (2, 1, 3)]
    partial = index_partial((2,), keys, payloads[3], partial, (far[0],))
    parts = [lax.ppermute(partial, "pre", x_shift(step)) for step in (2, 1, 3)]
    partial = log_add(log_add(partial, parts[0]), log_add(parts[1], parts[2]))
    part_out = project(received, value_proj, out_proj, partial)
    return summed_over(summed_over(part_out, first_shift, None), second_shift, queries.shape[:2])


def solution(mesh):
    placed = (
        P(("pre", "tp"), None),
        P(("pre", "tp"), None),
        P(None, "pre", "tp", None),
        P(None, "pre", None, None),
        P(None, "pre", None),
        P("tp", None, None),
        P("tp", None),
        P(None, "pre", None, None),
        P(None, "pre", None),
        P(None, "pre", None),
    )
    return jax.shard_map(
        on_device,
        mesh=mesh,
        in_specs=placed,
        out_specs=(P(None, "pre", None), P(None, "pre")),
        check_vma=False,
    )
```
